32 devices in a mesh: band: 4 (over x, core), slab: 8 (over z, y).
Axes of the slice: x: 2, y: 2, z: 4, core: 2. Of those that a mesh axis runs over, the one named last changes fastest.
Arguments:
- current_image: float32 [8, 4, 2, 32, 384], P('band', None, None, 'slab'), may hold values from -6 to 6
- langevin_noise: float32 [8, 4, 2, 32, 384], P('band', None, None, 'slab'), may hold values from -6 to 6
- step_size: float32 [1], replicated, may hold values from 0.2 to 0.5
- coil_maps: bfloat16 [8, 4, 32, 2, 32, 384], P(None, None, 'band', None, 'slab'), may hold values from -1 to 1
- measured_kspace: float32 [4, 32, 2, 32, 384], P(None, 'band', None, 'slab'), may hold values from -6 to 6
- sample_mask: int32 [4, 384], replicated, may hold values 0 or 1
- caipi_steps: int32 [8], replicated, may hold values from 0 to 7
- band_order: int32 [8], replicated, may hold values from 0 to 7, each once
- weight_in: bfloat16 [64, 2, 3, 3, 3], replicated, may hold values from -0.875 to 0.875
- weight_mid: bfloat16 [64, 64, 3, 3, 3], replicated, may hold values from -0.15625 to 0.15625
- weight_out: bfloat16 [2, 64, 3, 3, 3], replicated, may hold values from -0.359375 to 0.359375
Outputs:
- next_image: float32 [8, 4, 2, 32, 384], P('band', None, None, 'slab')
The draws below stay inside these ranges and needn't reach their ends.
Inputs may be any that keep to these rules, and one draw needn't show every extreme that they name: `sample_mask`: 1 where a phase-encode line of a slice group was sampled, else 0. `caipi_steps`: shift of a band in units of 48 columns. `band_order`: a permutation of 0 to 7.
All inputs are finite; a program needn't handle non-finite values.
Results may differ from the reference program's by a relative error of at most 0.0039.
Values may be sent and summed in bfloat16 or wider, within the bound.
No kernel may reach another device: no remote copies, remote signals or barrier semaphores. Data moves between devices by JAX's collectives and lax.ppermute only.
A program may use at most 128 MiB of HBM per device.

```python
import math
import jax
import jax.numpy as jnp
from jax import lax

NB = 8
NS = 4
Y = 384
C = 32
CH = 64
X = 32


def with_ends(drawn, stream_key, smallest, high):
    extent = drawn.shape
    index_at = [jax.random.randint(jax.random.fold_in(stream_key, axis), (), 0, extent[axis]) for axis in range(len(extent))]
    drawn = drawn.at[tuple(index_at)].set(smallest)
    longest = extent.index(max(extent))
    index_at[longest] = (index_at[longest] + 1) % extent[longest]
    return drawn.at[tuple(index_at)].set(high)


def steps_of(key, shape, cuts, low, largest):
    factor_of, own = 1.0, jax.random.fold_in(key, 6)
    for dim, blocks in cuts:
        steps = jnp.exp(jax.random.uniform(jax.random.fold_in(own, dim), (blocks,), jnp.float32, low / len(cuts), largest / len(cuts)))
        factor_of = factor_of * jnp.repeat(steps, shape[dim] // blocks).reshape([-1 if axis == dim else 1 for axis in range(len(shape))])
    return factor_of


def centred(key, shape, width, bound, cuts=(), dtype=jnp.bfloat16):
    array = jax.random.normal(key, shape, jnp.float32) * width
    if len(cuts) > 0:
        array = steps_of(key, shape, cuts, -0.22, 0.18) * array
    return jnp.clip(array, min=-bound, max=bound).astype(dtype)


def setup_inputs(seed: int = 0) -> dict:
    key_list = jax.random.split(jax.random.key(seed), 12)
    return {
        "current_image": centred(key_list[0], (NB, NS, 2, X, Y), 1.0, 6.0, ((0, 4), (3, 8)), jnp.float32),
        "langevin_noise": centred(key_list[1], (NB, NS, 2, X, Y), 1.0, 6.0, ((0, 4), (3, 8)), jnp.float32),
        "step_size": jnp.clip(jnp.exp(jax.random.uniform(key_list[2], (1,), jnp.float32, math.log(0.2), math.log(0.5))), 0.2, 0.5),
        "coil_maps": centred(key_list[3], (NB, NS, C, 2, X, Y), 0.18, 1.0, ((2, 4), (4, 8))),
        "measured_kspace": centred(key_list[4], (NS, C, 2, X, Y), 1.0, 6.0, ((1, 4), (3, 8)), jnp.float32),
        "sample_mask": with_ends((jax.random.randint(key_list[5], (NS, Y), 0, 3) < 1).astype(jnp.int32), jax.random.fold_in(key_list[5], 1), 0, 1),
        "caipi_steps": with_ends(jax.random.randint(key_list[6], (NB,), 0, 8), jax.random.fold_in(key_list[6], 1), 0, 7).astype(jnp.int32),
        "band_order": jax.random.permutation(key_list[7], NB).astype(jnp.int32),
        "weight_in": centred(key_list[8], (CH, 2, 3, 3, 3), 54 ** -0.5, 0.875),
        "weight_mid": centred(key_list[9], (CH, CH, 3, 3, 3), (CH * 27) ** -0.5, 0.15625),
        "weight_out": centred(key_list[10], (2, CH, 3, 3, 3), 0.06, 0.359375),
    }


def coil_product(coil_field, source):
    real_a = coil_field[..., 0, :, :]
    imag_a = coil_field[..., 1, :, :]
    real_b = source[..., 0, :, :]
    imag_b = source[..., 1, :, :]
    return jnp.stack([real_a * real_b - imag_a * imag_b, real_a * imag_b + imag_a * real_b], axis=-3)

def conjugate_product(coil_field, source):
    real_a = coil_field[..., 0, :, :]
    imag_a = coil_field[..., 1, :, :]
    real_b = source[..., 0, :, :]
    imag_b = source[..., 1, :, :]
    return jnp.stack([real_a * real_b + imag_a * imag_b, real_a * imag_b - imag_a * real_b], axis=-3)

def volume_conv(volume, weight):
    result = lax.conv_general_dilated(volume[None].astype(jnp.float32), weight.astype(jnp.float32), (1, 1, 1), ((1, 1), (1, 1), (1, 1)), dimension_numbers=('NCDHW', 'OIDHW', 'NCDHW'), precision=lax.Precision.HIGHEST)
    return result[0]

def reference(current_image, langevin_noise, step_size, coil_maps, measured_kspace, sample_mask, caipi_steps, band_order, weight_in, weight_mid, weight_out):
    columns = current_image.shape[-1]
    readout = current_image.shape[-2]
    group_slices = current_image.shape[1]
    all_positions = current_image.shape[0]
    caipi_shifts = caipi_steps[band_order] * (columns // 8)
    collapsed = jnp.zeros(measured_kspace.shape, jnp.float32)
    for position in range(all_positions):
        coil_field = coil_maps[position].astype(jnp.float32)
        coil_term = coil_product(coil_field, current_image[position][:, None])
        collapsed = collapsed + jnp.roll(coil_term, caipi_shifts[position], axis=-1)
    signal = lax.complex(collapsed[:, :, 0], collapsed[:, :, 1])
    spectrum = jnp.fft.fft(signal, axis=-1, norm='ortho')
    keep_mask = sample_mask[:, None, None, :].astype(jnp.float32)
    residual_real = keep_mask * (jnp.real(spectrum) - measured_kspace[:, :, 0])
    residual_imag = keep_mask * (jnp.imag(spectrum) - measured_kspace[:, :, 1])
    back_signal = jnp.fft.ifft(lax.complex(residual_real, residual_imag), axis=-1, norm='ortho')
    back_field = jnp.stack([jnp.real(back_signal), jnp.imag(back_signal)], axis=2)
    pieces = []
    for position in range(all_positions):
        coil_field = coil_maps[position].astype(jnp.float32)
        turned = jnp.roll(back_field, -caipi_shifts[position], axis=-1)
        pieces.append(lax.optimization_barrier(jnp.sum(conjugate_product(coil_field, turned), axis=1)))
    consistency = jnp.stack(pieces, axis=0)
    start_field = current_image.astype(jnp.bfloat16)
    volume = jnp.transpose(start_field, (2, 0, 1, 3, 4)).reshape(2, all_positions * group_slices, readout, columns)
    first_features = jax.nn.silu(volume_conv(volume, weight_in)).astype(jnp.bfloat16)
    second_features = jax.nn.silu(volume_conv(first_features, weight_mid)).astype(jnp.bfloat16)
    score_volume = volume_conv(second_features, weight_out)
    score_field = jnp.transpose(score_volume.reshape(2, all_positions, group_slices, readout, columns), (1, 2, 0, 3, 4))
    step_value = step_size[0]
    return current_image + step_value * (score_field - consistency) + jnp.sqrt(2.0 * step_value) * langevin_noise
```

```python
import functools
import math

import jax
import jax.numpy as jnp
import numpy as np
from jax import lax
from jax.experimental import pallas as pl
from jax.experimental.pallas import tpu as pltpu
from jax.sharding import PartitionSpec as P


def from_behind(block, axis, distance):
    devices = range(lax.axis_size(axis))
    route = [(i - distance, i) for i in devices if i - distance in devices]
    return lax.ppermute(block, axis, route)


def split_table(table):
    high = table.astype(jnp.bfloat16)
    low = (table - high.astype(np.float64)).astype(jnp.bfloat16)
    return high, low


def dft_table(columns):
    index = np.arange(columns)
    phase = (np.outer(index, index) % columns) * (2.0 * math.pi / columns)
    factor = 1.0 / math.sqrt(columns)
    return np.concatenate([np.cos(phase), np.sin(phase)], axis=1) * factor


def moved_right(value):
    lanes = value.shape[-1]
    lane = lax.broadcasted_iota(jnp.int32, (1, lanes), 1)
    return jnp.where(lane == 0, 0.0, pltpu.roll(value, 1, 1))


def moved_left(value):
    lanes = value.shape[-1]
    lane = lax.broadcasted_iota(jnp.int32, (1, lanes), 1)
    return jnp.where(lane == lanes - 1, 0.0, pltpu.roll(value, lanes - 1, 1))


def half_silu(half):
    return half + half * jnp.tanh(half)


def table_product(source, high_ref, low_ref):
    rows = source.shape[0]
    high = source.astype(jnp.bfloat16)
    low = (source - high.astype(jnp.float32)).astype(jnp.bfloat16)
    both = jnp.dot(
        jnp.concatenate([high, low], axis=0), high_ref[...], preferred_element_type=jnp.float32
    )
    rest = jnp.dot(high, low_ref[...], preferred_element_type=jnp.float32)
    return both[:rows] + both[rows:] + rest


def consistency_kernel(
    steps_ref, order_ref, image_ref, coil_ref, kspace_ref, mask_ref, high_ref, low_ref,
    out_ref, field_ref, kdata_ref,
):
    all_positions, slices, coils, _, rows, columns = coil_ref.shape
    total = slices * coils * rows
    unit = columns // 8
    shifts = [steps_ref[order_ref[g]] * unit for g in range(all_positions)]
    chunk = 4

    for s in range(slices):
        for begin in range(0, coils, chunk):
            real_sum = jnp.zeros((chunk, rows, columns), jnp.float32)
            imag_sum = jnp.zeros((chunk, rows, columns), jnp.float32)
            for g in range(all_positions):
                coil = coil_ref[g, s, begin : begin + chunk].astype(jnp.float32)
                real_x = image_ref[g, s, 0].astype(jnp.float32)
                imag_x = image_ref[g, s, 1].astype(jnp.float32)
                real_c, imag_c = coil[:, 0], coil[:, 1]
                real_y = real_c * real_x - imag_c * imag_x
                imag_y = real_c * imag_x + imag_c * real_x
                real_sum += pltpu.roll(real_y, shifts[g], 2)
                imag_sum += pltpu.roll(imag_y, shifts[g], 2)
            for c in range(chunk):
                row = (s * coils + begin + c) * rows
                field_ref[row : row + rows, :] = real_sum[c]
                field_ref[total + row : total + row + rows, :] = imag_sum[c]
                kdata_ref[row : row + rows, :] = kspace_ref[s, begin + c, 0]
                kdata_ref[total + row : total + row + rows, :] = kspace_ref[s, begin + c, 1]

    product = table_product(field_ref[...], high_ref, low_ref)
    with_cos, with_sin = product[:, :columns], product[:, columns:]
    keep = jnp.concatenate(
        [
            jnp.broadcast_to(mask_ref[s : s + 1, :].astype(jnp.float32), (coils * rows, columns))
            for s in range(slices)
        ],
        axis=0,
    )
    real_r = keep * (with_cos[:total] + with_sin[total:] - kdata_ref[:total])
    imag_r = keep * (with_cos[total:] - with_sin[:total] - kdata_ref[total:])
    product = table_product(jnp.concatenate([real_r, imag_r], axis=0), high_ref, low_ref)
    with_cos, with_sin = product[:, :columns], product[:, columns:]
    field_ref[:total] = with_cos[:total] - with_sin[total:]
    field_ref[total:] = with_cos[total:] + with_sin[:total]

    for s in range(slices):
        real_b = []
        imag_b = []
        for c in range(coils):
            row = (s * coils + c) * rows
            real_b.append(field_ref[row : row + rows, :])
            imag_b.append(field_ref[total + row : total + row + rows, :])
        real_b = jnp.stack(real_b, axis=0)
        imag_b = jnp.stack(imag_b, axis=0)
        for g in range(all_positions):
            back = lax.rem(columns - shifts[g], columns)
            real_sum = jnp.zeros((rows, columns), jnp.float32)
            imag_sum = jnp.zeros((rows, columns), jnp.float32)
            for begin in range(0, coils, chunk):
                coil = coil_ref[g, s, begin : begin + chunk].astype(jnp.float32)
                real_c, imag_c = coil[:, 0], coil[:, 1]
                real_t = pltpu.roll(real_b[begin : begin + chunk], back, 2)
                imag_t = pltpu.roll(imag_b[begin : begin + chunk], back, 2)
                real_sum += jnp.sum(real_c * real_t + imag_c * imag_t, axis=0)
                imag_sum += jnp.sum(real_c * imag_t - imag_c * real_t, axis=0)
            out_ref[g, s, 0] = real_sum.astype(jnp.bfloat16)
            out_ref[g, s, 1] = imag_sum.astype(jnp.bfloat16)


def partial_consistency(everyone, coil_maps, measured_kspace, sample_mask, caipi_steps, band_order):
    columns = coil_maps.shape[-1]
    slices, coils, _, rows, _ = measured_kspace.shape
    total = slices * coils * rows
    high, low = split_table(dft_table(columns))
    smem = pl.BlockSpec(memory_space=pltpu.SMEM)
    vmem = pl.BlockSpec(memory_space=pltpu.VMEM)
    return pl.pallas_call(
        consistency_kernel,
        out_shape=jax.ShapeDtypeStruct(everyone.shape, jnp.bfloat16),
        in_specs=[smem, smem] + [vmem] * 6,
        out_specs=vmem,
        scratch_shapes=[
            pltpu.VMEM((2 * total, columns), jnp.float32),
            pltpu.VMEM((2 * total, columns), jnp.float32),
        ],
        compiler_params=pltpu.CompilerParams(vmem_limit_bytes=40 * 2**20),
        cost_estimate=pl.CostEstimate(flops=10**9, bytes_accessed=4 * 10**6, transcendentals=0),
    )(
        caipi_steps, band_order, everyone, coil_maps, measured_kspace, sample_mask,
        jnp.asarray(high), jnp.asarray(low),
    )


def network_kernel(
    place_ref, window_ref, first_ref, mid_ref, last_ref,
    out_ref, taps_ref, wide_ref, f1_ref, f2_ref, part_ref, score_ref,
):
    channels = mid_ref.shape[-1]
    out_slices, _, columns = out_ref.shape
    slices1, slices2 = out_slices + 4, out_slices + 2
    lower_slice, upper_slice = place_ref[0] == 0, place_ref[0] == place_ref[1] - 1
    lower_row, upper_row = place_ref[2] == 0, place_ref[2] == place_ref[3] - 1
    four, two = 4 * channels, 2 * channels

    for t in range(3):
        for a in range(2):
            for r in range(2):
                row = ((t * 2 + a) * 2 + r) * channels
                for d in range(4):
                    for pair in range(2):
                        blocks = []
                        for q in (2 * pair, 2 * pair + 1):
                            if 0 <= d - a <= 2 and 0 <= q - r <= 2:
                                blocks.append(mid_ref[d - a, q - r, t] * jnp.bfloat16(0.5))
                            else:
                                blocks.append(jnp.zeros((channels, channels), jnp.bfloat16))
                        col = (d * 4 + 2 * pair) * channels
                        wide_ref[row : row + channels, col : col + two] = jnp.concatenate(
                            blocks, axis=1
                        )

    for g in range(2):
        base = window_ref[g].astype(jnp.float32)
        taps_ref[g, 0] = moved_right(base).astype(jnp.bfloat16)
        taps_ref[g, 1] = window_ref[g]
        taps_ref[g, 2] = moved_left(base).astype(jnp.bfloat16)

    def first_layer(z, carry):
        for g in range(2):
            begin = pl.multiple_of(16 * z, 16)
            source = jnp.concatenate(
                [taps_ref[g, t, pl.ds(begin, 48), :] for t in range(3)], axis=0
            )
            half = jnp.dot(first_ref[...], source, preferred_element_type=jnp.float32)
            f1_ref[z, four * g : four * (g + 1), :] = half_silu(half).astype(jnp.bfloat16)
        return carry

    lax.fori_loop(0, slices1, first_layer, 0)

    @pl.when(lower_slice)
    def _():
        f1_ref[0:2] = jnp.zeros_like(f1_ref[0:2])

    @pl.when(upper_slice)
    def _():
        f1_ref[slices1 - 2 :] = jnp.zeros_like(f1_ref[slices1 - 2 :])

    @pl.when(lower_row)
    def _():
        f1_ref[:, :two, :] = jnp.zeros_like(f1_ref[:, :two, :])

    @pl.when(upper_row)
    def _():
        f1_ref[:, 3 * two :, :] = jnp.zeros_like(f1_ref[:, 3 * two :, :])

    def second_layer(step, carry):
        z = 2 * step
        for pair in range(3):
            source = f1_ref[pl.ds(z, 4), two * pair : two * pair + four, :]
            part_ref[...] = jnp.dot(
                wide_ref[...],
                source.reshape(4 * four, columns),
                preferred_element_type=jnp.float32,
            )
            for a in range(2):
                for r in range(2):
                    row = (a * 2 + r) * channels
                    half = (
                        moved_right(part_ref[row : row + channels])
                        + part_ref[four + row : four + row + channels]
                        + moved_left(part_ref[2 * four + row : 2 * four + row + channels])
                    )
                    place = two * pair + r * channels
                    f2_ref[z + a, place : place + channels, :] = half_silu(half).astype(
                        jnp.bfloat16
                    )
        return carry

    lax.fori_loop(0, slices2 // 2, second_layer, 0)

    @pl.when(lower_slice)
    def _():
        f2_ref[0] = jnp.zeros_like(f2_ref[0])

    @pl.when(upper_slice)
    def _():
        f2_ref[slices2 - 1] = jnp.zeros_like(f2_ref[slices2 - 1])

    @pl.when(lower_row)
    def _():
        f2_ref[:, :channels, :] = jnp.zeros_like(f2_ref[:, :channels, :])

    @pl.when(upper_row)
    def _():
        f2_ref[:, 5 * channels :, :] = jnp.zeros_like(f2_ref[:, 5 * channels :, :])

    for z in range(slices2):
        score_ref[z] = jnp.dot(last_ref[...], f2_ref[z], preferred_element_type=jnp.float32)

    for z in range(out_slices):
        taps = []
        for t in range(3):
            taps.append(
                sum(score_ref[z + d, (3 * d + t) * 8 : (3 * d + t + 1) * 8, :] for d in range(3))
            )
        out_ref[z] = moved_right(taps[0]) + taps[1] + moved_left(taps[2])


def score_network(place, windows, weight_in, weight_mid, weight_out):
    channels = weight_mid.shape[0]
    slices0, columns = windows.shape[1] // 16, windows.shape[-1]
    out_slices = slices0 - 6
    first = jnp.stack(
        [jnp.pad(weight_in, ((0, 0), (0, 0), (0, 0), (r, 5 - r), (0, 0))) for r in range(4)]
    )
    first = jnp.transpose(first, (0, 1, 5, 3, 2, 4)).reshape(4 * channels, 144)
    first = first * jnp.bfloat16(0.5)
    mid = jnp.transpose(weight_mid, (2, 3, 4, 0, 1))
    last = jnp.stack(
        [jnp.pad(weight_out, ((0, 0), (0, 0), (0, 0), (r, 3 - r), (0, 0))) for r in range(4)]
    )
    last = jnp.transpose(last, (3, 5, 1, 0, 4, 2)).reshape(72, 6 * channels)
    smem = pl.BlockSpec(memory_space=pltpu.SMEM)
    vmem = pl.BlockSpec(memory_space=pltpu.VMEM)
    return pl.pallas_call(
        network_kernel,
        out_shape=jax.ShapeDtypeStruct((out_slices, 8, columns), jnp.float32),
        in_specs=[smem] + [vmem] * 4,
        out_specs=vmem,
        scratch_shapes=[
            pltpu.VMEM((2, 3, slices0 * 16, columns), jnp.bfloat16),
            pltpu.VMEM((12 * channels, 16 * channels), jnp.bfloat16),
            pltpu.VMEM((out_slices + 4, 8 * channels, columns), jnp.bfloat16),
            pltpu.VMEM((out_slices + 2, 6 * channels, columns), jnp.bfloat16),
            pltpu.VMEM((12 * channels, columns), jnp.float32),
            pltpu.VMEM((out_slices + 2, 72, columns), jnp.float32),
        ],
        compiler_params=pltpu.CompilerParams(vmem_limit_bytes=40 * 2**20),
        cost_estimate=pl.CostEstimate(
            flops=10**10, bytes_accessed=2 * 10**6, transcendentals=4 * 10**6
        ),
    )(place, windows, first, mid, last)


def per_device(
    current_image, langevin_noise, step_size, coil_maps, measured_kspace, sample_mask,
    caipi_steps, band_order, weight_in, weight_mid, weight_out,
):
    positions, group_slices, _, row_count, columns = current_image.shape
    local_slices = positions * group_slices
    everyone = lax.all_gather(current_image.astype(jnp.bfloat16), "band", axis=0, tiled=True)

    volume = everyone.reshape(-1, 2, row_count, columns)
    volume = jnp.pad(volume, ((3, 3), (0, 0), (0, 0), (0, 0)))
    tall = lax.dynamic_slice_in_dim(
        volume, lax.axis_index("band") * local_slices, local_slices + 6, axis=0
    )
    below = from_behind(tall[:, :, row_count - 3 :, :], "slab", 1)
    above = from_behind(tall[:, :, :3, :], "slab", -1)
    field = jnp.concatenate([below, tall, above, jnp.zeros_like(above[:, :, :2])], axis=2)
    windows = jnp.stack(
        [field[:, :, 4 * g : 4 * g + 8].reshape(-1, columns) for g in range(2)], axis=0
    )
    place = jnp.stack(
        [
            lax.axis_index("band"),
            jnp.int32(lax.axis_size("band")),
            lax.axis_index("slab"),
            jnp.int32(lax.axis_size("slab")),
        ]
    ).astype(jnp.int32)

    partial_sums = partial_consistency(
        everyone, coil_maps, measured_kspace, sample_mask, caipi_steps, band_order
    )
    swapped = lax.all_to_all(partial_sums, "band", split_axis=0, concat_axis=0, tiled=True)
    score = score_network(place, windows, weight_in, weight_mid, weight_out)
    score_field = score.reshape(positions, group_slices, 2, row_count, columns)
    pieces = swapped.reshape((-1, positions) + swapped.shape[1:]).astype(jnp.float32)
    consistency = jnp.sum(pieces, axis=0)
    step_value = step_size[0]
    return (
        current_image
        + step_value * (score_field - consistency)
        + jnp.sqrt(2.0 * step_value) * langevin_noise
    )


def solution(mesh):
    band5 = P("band", None, None, "slab", None)
    in_specs = (
        band5,
        band5,
        P(),
        P(None, None, "band", None, "slab", None),
        P(None, "band", None, "slab", None),
        P(), P(), P(), P(), P(), P(),
    )
    return jax.shard_map(
        per_device, mesh=mesh, in_specs=in_specs, out_specs=band5, check_vma=False
    )
```

```python
import functools
import math

import jax
import jax.numpy as jnp
import numpy as np
from jax import lax
from jax.experimental import pallas as pl
from jax.experimental.pallas import tpu as pltpu
from jax.sharding import PartitionSpec as P


def from_behind(block, axis, distance):
    devices = range(lax.axis_size(axis))
    route = [(i - distance, i) for i in devices if i - distance in devices]
    return lax.ppermute(block, axis, route)


def split_table(table):
    high = table.astype(jnp.bfloat16)
    low = (table - high.astype(np.float64)).astype(jnp.bfloat16)
    return high, low


def dft_table(columns):
    index = np.arange(columns)
    phase = (np.outer(index, index) % columns) * (2.0 * math.pi / columns)
    factor = 1.0 / math.sqrt(columns)
    return np.concatenate([np.cos(phase), np.sin(phase)], axis=1) * factor


def moved_right(value):
    lanes = value.shape[-1]
    lane = lax.broadcasted_iota(jnp.int32, (1, lanes), 1)
    return jnp.where(lane == 0, 0.0, pltpu.roll(value, 1, 1))


def moved_left(value):
    lanes = value.shape[-1]
    lane = lax.broadcasted_iota(jnp.int32, (1, lanes), 1)
    return jnp.where(lane == lanes - 1, 0.0, pltpu.roll(value, lanes - 1, 1))


def half_silu(half):
    return half + half * jnp.tanh(half)


def table_product(source, high_ref, low_ref):
    rows = source.shape[0]
    high = source.astype(jnp.bfloat16)
    low = (source - high.astype(jnp.float32)).astype(jnp.bfloat16)
    both = jnp.dot(
        jnp.concatenate([high, low], axis=0), high_ref[...], preferred_element_type=jnp.float32
    )
    rest = jnp.dot(high, low_ref[...], preferred_element_type=jnp.float32)
    return both[:rows] + both[rows:] + rest


def halves_swapped(value):
    return pltpu.roll(value, 4, value.ndim - 2)


def upper_half(value):
    return lax.broadcasted_iota(jnp.int32, value.shape, value.ndim - 2) < 4


def signed_swap(value, top, bottom):
    sign = jnp.where(upper_half(value), top, bottom)
    return sign * halves_swapped(value)


def stacked_parts(value):
    return jnp.concatenate([value[..., 0, :, :], value[..., 1, :, :]], axis=-2)


def turned_tiles(value, shift, store):
    tiles = value.shape[-1] // 128
    whole, part = shift // 128, lax.rem(shift, 128)
    moved = [
        pltpu.roll(value[..., 128 * j : 128 * (j + 1)], part, value.ndim - 1) for j in range(tiles)
    ]
    lane = lax.broadcasted_iota(jnp.int32, moved[0].shape, value.ndim - 1)
    for j in range(tiles):
        store(lax.rem(j + whole, tiles), jnp.where(lane < part, moved[j - 1], moved[j]))


def consistency_kernel(
    image_ref, steps_hbm, order_hbm, size_hbm, coil_hbm, kspace_hbm, mask_hbm, high_hbm, low_hbm,
    out_ref,
    steps_ref, order_ref, size_ref, coil_ref, kspace_ref, mask_ref, high_ref, low_ref,
    turned_ref, real_ref, imag_ref, field_ref, swap_ref, sum_ref, sems, coil_sems,
):
    all_positions, slices, coils, _, rows, columns = coil_ref.shape
    tiles = columns // 128
    unit = columns // 8
    pairs = (
        (steps_hbm, steps_ref), (order_hbm, order_ref), (size_hbm, size_ref),
        (kspace_hbm, kspace_ref), (mask_hbm, mask_ref), (high_hbm, high_ref), (low_hbm, low_ref),
    )
    copies = [pltpu.make_async_copy(src, dst, sems.at[i]) for i, (src, dst) in enumerate(pairs)]
    for copy in copies[:3]:
        copy.start()
    for g in range(all_positions):
        pltpu.make_async_copy(coil_hbm.at[g], coil_ref.at[g], coil_sems.at[g]).start()
    for copy in copies[3:]:
        copy.start()
    for copy in copies[:3]:
        copy.wait()

    def shift_of(g):
        return steps_ref[order_ref[g]] * unit

    def turn_coils(g, carry):
        shift = shift_of(g)
        image = image_ref[g].astype(jnp.float32)

        def store_image(j, value):
            other = halves_swapped(value)
            top = upper_half(value)
            real_ref[j, g] = jnp.where(top, value, other)
            imag_ref[j, g] = jnp.where(top, other, value)

        turned_tiles(image, shift, store_image)
        pltpu.make_async_copy(coil_hbm.at[g], coil_ref.at[g], coil_sems.at[g]).wait()
        for s in range(slices):
            coil = stacked_parts(coil_ref[g, s].astype(jnp.float32))

            def store_coil(j, value, s=s):
                turned_ref[j, g, s] = value

            turned_tiles(coil, shift, store_coil)
        return carry

    lax.fori_loop(0, all_positions, turn_coils, 0)

    block = coils * 2 * rows
    for j in range(tiles):
        for s in range(slices):
            with_real = jnp.zeros((coils, 2 * rows, 128), jnp.float32)
            with_imag = jnp.zeros((coils, 2 * rows, 128), jnp.float32)
            for g in range(all_positions):
                coil = turned_ref[j, g, s]
                with_real += coil * real_ref[j, g, s]
                with_imag += coil * imag_ref[j, g, s]
            total = with_real + signed_swap(with_imag, -1.0, 1.0)
            field_ref[s * block : (s + 1) * block, 128 * j : 128 * (j + 1)] = total.reshape(
                block, 128
            )

    for copy in copies[3:]:
        copy.wait()
    product = table_product(field_ref[...], high_ref, low_ref)
    grouped = (slices, coils, 2 * rows, columns)
    with_cos = product[:, :columns].reshape(grouped)
    with_sin = product[:, columns:].reshape(grouped)
    spectrum = with_cos + signed_swap(with_sin, 1.0, -1.0)
    keep = mask_ref[...].astype(jnp.float32).reshape(slices, 1, 1, columns)
    residual = keep * (spectrum - stacked_parts(kspace_ref[...]))
    product = table_product(residual.reshape(slices * block, columns), high_ref, low_ref)
    with_cos = product[:, :columns].reshape(grouped)
    with_sin = product[:, columns:].reshape(grouped)
    back = with_cos + signed_swap(with_sin, -1.0, 1.0)
    field_ref[...] = back.reshape(slices * block, columns)
    swap_ref[...] = halves_swapped(back).reshape(slices * block, columns)

    size = size_ref[0]
    for j in range(tiles):
        for s in range(slices):
            place = (slice(s * block, (s + 1) * block), slice(128 * j, 128 * (j + 1)))
            field = field_ref[place].reshape(coils, 2 * rows, 128)
            swapped = swap_ref[place].reshape(coils, 2 * rows, 128)
            for g in range(all_positions):
                coil = turned_ref[j, g, s]
                straight = jnp.sum(coil * field, axis=0)
                crossed = jnp.sum(coil * swapped, axis=0)
                straight = straight + halves_swapped(straight)
                crossed = halves_swapped(crossed) - crossed
                sum_ref[g, s, :, 128 * j : 128 * (j + 1)] = size * jnp.where(
                    upper_half(straight), straight, crossed
                )

    def turn_sums(g, carry):
        back_shift = lax.rem(columns - shift_of(g), columns)
        turned = pltpu.roll(sum_ref[g], back_shift, 2).astype(jnp.bfloat16)
        out_ref[g, :, 0] = turned[:, :rows]
        out_ref[g, :, 1] = turned[:, rows:]
        return carry

    lax.fori_loop(0, all_positions, turn_sums, 0)


def partial_consistency(
    everyone, step_size, coil_maps, measured_kspace, sample_mask, caipi_steps, band_order
):
    all_positions, slices, coils, _, rows, columns = coil_maps.shape
    total = slices * coils * 2 * rows
    high, low = split_table(dft_table(columns))
    hbm = pl.BlockSpec(memory_space=pltpu.HBM)
    vmem = pl.BlockSpec(memory_space=pltpu.VMEM)
    tile_shape = (columns // 128, all_positions, slices)
    return pl.pallas_call(
        consistency_kernel,
        out_shape=jax.ShapeDtypeStruct((all_positions, slices, 2, rows, columns), jnp.bfloat16),
        in_specs=[vmem] + [hbm] * 8,
        out_specs=vmem,
        scratch_shapes=[
            pltpu.SMEM(caipi_steps.shape, jnp.int32),
            pltpu.SMEM(band_order.shape, jnp.int32),
            pltpu.SMEM(step_size.shape, jnp.float32),
            pltpu.VMEM(coil_maps.shape, jnp.bfloat16),
            pltpu.VMEM(measured_kspace.shape, jnp.float32),
            pltpu.VMEM(sample_mask.shape, jnp.int32),
            pltpu.VMEM(high.shape, jnp.bfloat16),
            pltpu.VMEM(low.shape, jnp.bfloat16),
            pltpu.VMEM(tile_shape + (coils, 2 * rows, 128), jnp.float32),
            pltpu.VMEM(tile_shape + (2 * rows, 128), jnp.float32),
            pltpu.VMEM(tile_shape + (2 * rows, 128), jnp.float32),
            pltpu.VMEM((total, columns), jnp.float32),
            pltpu.VMEM((total, columns), jnp.float32),
            pltpu.VMEM((all_positions, slices, 2 * rows, columns), jnp.float32),
            pltpu.SemaphoreType.DMA((7,)),
            pltpu.SemaphoreType.DMA((all_positions,)),
        ],
        compiler_params=pltpu.CompilerParams(vmem_limit_bytes=48 * 2**20),
        cost_estimate=pl.CostEstimate(flops=10**9, bytes_accessed=4 * 10**6, transcendentals=0),
    )(
        everyone, caipi_steps, band_order, step_size, coil_maps, measured_kspace, sample_mask,
        jnp.asarray(high), jnp.asarray(low),
    )


def network_kernel(
    window_ref, size_hbm, first_hbm, mid_hbm, last_hbm, image_hbm, noise_hbm,
    out_ref,
    size_ref, first_raw, mid_raw, last_raw, image_ref, noise_ref,
    first_sum, last_sum, first_ref, wide_ref, last_ref,
    taps_ref, f1_ref, f2_ref, part_a, part_b, score_ref, sems,
):
    channels = mid_raw.shape[-1]
    out_slices, _, rows, columns = out_ref.shape
    slices1, slices2 = out_slices + 4, out_slices + 2
    pairs = (
        (first_hbm, first_raw), (mid_hbm, mid_raw), (last_hbm, last_raw),
        (size_hbm, size_ref), (image_hbm, image_ref), (noise_hbm, noise_ref),
    )
    copies = [pltpu.make_async_copy(src, dst, sems.at[i]) for i, (src, dst) in enumerate(pairs)]
    for copy in copies:
        copy.start()

    def inside(axis, end):
        edge = lax.axis_size(axis) - 1 if end else 0
        return jnp.where(lax.axis_index(axis) == edge, 0.0, 1.0).astype(jnp.float32)

    low_slice, high_slice = inside("band", False), inside("band", True)
    low_row, high_row = inside("slab", False), inside("slab", True)
    four, two = 4 * channels, 2 * channels

    for g in range(2):
        base = window_ref[g].astype(jnp.float32)
        taps_ref[g, 0] = moved_right(base).astype(jnp.bfloat16)
        taps_ref[g, 1] = window_ref[g]
        taps_ref[g, 2] = moved_left(base).astype(jnp.bfloat16)

    first_sum[...] = jnp.zeros_like(first_sum)
    copies[0].wait()
    for d in range(3):
        for u in range(3):
            for t in range(3):
                block = first_raw[d, u, t].astype(jnp.float32) * 0.5
                for i in range(2):
                    for r in range(4):
                        row = (t * 3 + d) * 16 + i * 8 + u + r
                        first_sum[row : row + 1, r * channels : (r + 1) * channels] = block[
                            i : i + 1
                        ]
    first_ref[...] = first_sum[...].T[:, : first_ref.shape[1]].astype(jnp.bfloat16)

    copies[1].wait()
    half_weight = jnp.bfloat16(0.5)
    for t in range(3):
        for r in range(2):
            row = (t * 2 + r) * channels
            for d in range(3):
                for pair in range(2):
                    blocks = []
                    for q in (2 * pair, 2 * pair + 1):
                        if 0 <= q - r <= 2:
                            blocks.append(mid_raw[d, q - r, t] * half_weight)
                        else:
                            blocks.append(jnp.zeros((channels, channels), jnp.bfloat16))
                    col = (d * 4 + 2 * pair) * channels
                    wide_ref[row : row + channels, col : col + two] = jnp.concatenate(
                        blocks, axis=1
                    )

    last_sum[...] = jnp.zeros_like(last_sum)
    copies[2].wait()
    for d in range(3):
        for u in range(3):
            for t in range(3):
                block = last_raw[d, u, t].astype(jnp.float32)
                for o in range(2):
                    for r in range(4):
                        row = (d * 3 + t) * 8 + o * 4 + r
                        col = (r + u) * channels
                        last_sum[row : row + 1, col : col + channels] = block[o : o + 1]
    last_ref[...] = last_sum[...].astype(jnp.bfloat16)

    def first_layer(z):
        source = jnp.concatenate(
            [
                jnp.concatenate([taps_ref[g, t, 16 * z : 16 * z + 48, :] for t in range(3)], axis=0)
                for g in range(2)
            ],
            axis=1,
        )
        half = jnp.dot(first_ref[...], source, preferred_element_type=jnp.float32)
        for r in range(8):
            begin = (r % 4) * channels
            first = columns * (r // 4)
            value = half_silu(half[begin : begin + channels, first : first + columns])
            factors = []
            if z < 2:
                factors.append(low_slice)
            if z >= slices1 - 2:
                factors.append(high_slice)
            if r < 2:
                factors.append(low_row)
            if r >= 6:
                factors.append(high_row)
            for factor in factors:
                value = value * factor
            f1_ref[z, r * channels : (r + 1) * channels, :] = value.astype(jnp.bfloat16)

    def second_product(z, pair, part_ref):
        source = jnp.concatenate(
            [
                f1_ref[z + a : z + a + 3, two * pair : two * pair + four, :].reshape(
                    3 * four, columns
                )
                for a in range(2)
            ],
            axis=1,
        )
        part_ref[...] = jnp.dot(wide_ref[...], source, preferred_element_type=jnp.float32)

    def second_layer(z, pair, part_ref):
        for a in range(2):
            first = columns * a
            for r in range(2):
                row = r * channels
                half = (
                    moved_right(part_ref[row : row + channels, first : first + columns])
                    + part_ref[two + row : two + row + channels, first : first + columns]
                    + moved_left(
                        part_ref[four + row : four + row + channels, first : first + columns]
                    )
                )
                value = half_silu(half)
                factors = []
                if z + a == 0:
                    factors.append(low_slice)
                if z + a == slices2 - 1:
                    factors.append(high_slice)
                if pair == 0 and r == 0:
                    factors.append(low_row)
                if pair == 2 and r == 1:
                    factors.append(high_row)
                for factor in factors:
                    value = value * factor
                place = two * pair + r * channels
                f2_ref[z + a, place : place + channels, :] = value.astype(jnp.bfloat16)

    def third_product(z):
        source = jnp.concatenate([f2_ref[z], f2_ref[z + 1]], axis=1)
        score_ref[z // 2] = jnp.dot(last_ref[...], source, preferred_element_type=jnp.float32)

    for z in range(4):
        first_layer(z)
    waiting = None
    parts = (part_a, part_b)
    count = 0
    for z in range(0, slices2, 2):
        for pair in range(3):
            second_product(z, pair, parts[count % 2])
            if pair < 2 and z + 4 + pair < slices1:
                first_layer(z + 4 + pair)
            if waiting is not None:
                second_layer(*waiting)
                if waiting[1] == 2:
                    third_product(waiting[0])
            waiting = (z, pair, parts[count % 2])
            count += 1
    second_layer(*waiting)
    third_product(waiting[0])

    for copy in copies[3:]:
        copy.wait()
    size = size_ref[0]
    noise_scale = jnp.sqrt(jnp.full((1, columns), 2.0 * size, jnp.float32))
    for z in range(out_slices):
        taps = []
        for t in range(3):
            total = None
            for d in range(3):
                row, first = (3 * d + t) * 8, columns * ((z + d) % 2)
                piece = score_ref[(z + d) // 2, row : row + 8, first : first + columns]
                total = piece if total is None else total + piece
            taps.append(total)
        score = size * (moved_right(taps[0]) + taps[1] + moved_left(taps[2]))
        for part in range(2):
            out_ref[z, part] = (
                image_ref[z, part]
                + score[part * rows : (part + 1) * rows]
                + noise_scale * noise_ref[z, part]
            )


def stepped_without_data(
    windows, current_image, langevin_noise, step_size, weight_in, weight_mid, weight_out
):
    channels = weight_mid.shape[0]
    slices0, columns = windows.shape[1] // 16, windows.shape[-1]
    out_slices = slices0 - 6
    local = (out_slices,) + current_image.shape[2:]
    first = jnp.transpose(weight_in, (2, 3, 4, 1, 0))
    mid = jnp.transpose(weight_mid, (2, 3, 4, 0, 1))
    last = jnp.transpose(weight_out, (2, 3, 4, 0, 1))
    hbm = pl.BlockSpec(memory_space=pltpu.HBM)
    vmem = pl.BlockSpec(memory_space=pltpu.VMEM)
    return pl.pallas_call(
        network_kernel,
        out_shape=jax.ShapeDtypeStruct(local, jnp.float32),
        in_specs=[vmem] + [hbm] * 6,
        out_specs=vmem,
        scratch_shapes=[
            pltpu.SMEM(step_size.shape, jnp.float32),
            pltpu.VMEM(first.shape, jnp.bfloat16),
            pltpu.VMEM(mid.shape, jnp.bfloat16),
            pltpu.VMEM(last.shape, jnp.bfloat16),
            pltpu.VMEM(local, jnp.float32),
            pltpu.VMEM(local, jnp.float32),
            pltpu.VMEM((256, 4 * channels), jnp.float32),
            pltpu.VMEM((72, 6 * channels), jnp.float32),
            pltpu.VMEM((4 * channels, 144), jnp.bfloat16),
            pltpu.VMEM((6 * channels, 12 * channels), jnp.bfloat16),
            pltpu.VMEM((72, 6 * channels), jnp.bfloat16),
            pltpu.VMEM((2, 3, slices0 * 16, columns), jnp.bfloat16),
            pltpu.VMEM((out_slices + 4, 8 * channels, columns), jnp.bfloat16),
            pltpu.VMEM((out_slices + 2, 6 * channels, columns), jnp.bfloat16),
            pltpu.VMEM((6 * channels, 2 * columns), jnp.float32),
            pltpu.VMEM((6 * channels, 2 * columns), jnp.float32),
            pltpu.VMEM((out_slices // 2 + 1, 72, 2 * columns), jnp.float32),
            pltpu.SemaphoreType.DMA((6,)),
        ],
        compiler_params=pltpu.CompilerParams(vmem_limit_bytes=48 * 2**20),
        cost_estimate=pl.CostEstimate(
            flops=10**10, bytes_accessed=2 * 10**6, transcendentals=4 * 10**6
        ),
    )(
        windows, step_size, first, mid, last,
        current_image.reshape(local), langevin_noise.reshape(local),
    ).reshape(current_image.shape)


def per_device(
    current_image, langevin_noise, step_size, coil_maps, measured_kspace, sample_mask,
    caipi_steps, band_order, weight_in, weight_mid, weight_out,
):
    positions, group_slices, _, row_count, columns = current_image.shape
    local_slices = positions * group_slices
    own = current_image.astype(jnp.bfloat16).reshape(
        positions, group_slices, 2 * row_count, columns
    )
    everyone = lax.all_gather(own, "band", axis=0, tiled=True)

    volume = everyone.reshape(-1, 2, row_count, columns)
    volume = jnp.pad(volume, ((3, 3), (0, 0), (0, 0), (0, 0)))
    tall = lax.dynamic_slice_in_dim(
        volume, lax.axis_index("band") * local_slices, local_slices + 6, axis=0
    )
    below = from_behind(tall[:, :, row_count - 3 :, :], "slab", 1)
    above = from_behind(tall[:, :, :3, :], "slab", -1)
    field = jnp.concatenate([below, tall, above, jnp.zeros_like(above[:, :, :2])], axis=2)
    windows = jnp.stack(
        [field[:, :, 4 * g : 4 * g + 8].reshape(-1, columns) for g in range(2)], axis=0
    )
    partial_sums = partial_consistency(
        everyone, step_size, coil_maps, measured_kspace, sample_mask, caipi_steps, band_order
    )
    swapped = lax.all_to_all(partial_sums, "band", split_axis=0, concat_axis=0, tiled=True)
    base = stepped_without_data(
        windows, current_image, langevin_noise, step_size, weight_in, weight_mid, weight_out
    )
    pieces = swapped.reshape((-1, positions) + swapped.shape[1:]).astype(jnp.float32)
    return base - jnp.sum(pieces, axis=0)


def solution(mesh):
    band5 = P("band", None, None, "slab", None)
    in_specs = (
        band5,
        band5,
        P(),
        P(None, None, "band", None, "slab", None),
        P(None, "band", None, "slab", None),
        P(), P(), P(), P(), P(), P(),
    )
    return jax.shard_map(
        per_device, mesh=mesh, in_specs=in_specs, out_specs=band5, check_vma=False
    )
```

```python
import functools
import math

import jax
import jax.numpy as jnp
import numpy as np
from jax import lax
from jax.experimental import pallas as pl
from jax.experimental.pallas import tpu as pltpu
from jax.sharding import PartitionSpec as P


def exchanged_rows(tall, width):
    count = lax.axis_size("slab")
    odd = lax.axis_index("slab") % 2 == 1
    head, tail = tall[:, :, :width, :], tall[:, :, tall.shape[2] - width :, :]
    arrived = []
    for first in range(2):
        route = []
        for i in range(first, count - 1, 2):
            route += [(i, i + 1), (i + 1, i)]
        sent = jnp.where(odd, head, tail) if first == 0 else jnp.where(odd, tail, head)
        arrived.append(lax.ppermute(sent, "slab", route))
    below = jnp.where(odd, arrived[0], arrived[1])
    above = jnp.where(odd, arrived[1], arrived[0])
    return below, above


def in_hbm(*arrays):
    return [pltpu.with_memory_space_constraint(array, pltpu.HBM) for array in arrays]


def dft_factors(columns):
    near = 16
    index = np.arange(columns)
    pieces = []
    for rows in (near * np.arange(columns // near), np.arange(near)):
        phase = (np.outer(rows, index) % columns) * (2.0 * math.pi / columns)
        pieces += [np.cos(phase), np.sin(phase)]
    far = np.concatenate(pieces[:2], axis=0) / math.sqrt(columns)
    return np.concatenate([far] + pieces[2:], axis=0).astype(np.float32)


def build_tables(factors_ref, high_ref, low_ref):
    columns = factors_ref.shape[1]
    near = 16
    count = columns // near
    near_cos = factors_ref[2 * count : 2 * count + near, :]
    near_sin = factors_ref[2 * count + near :, :]
    for a in range(count):
        far_cos = factors_ref[a : a + 1, :]
        far_sin = factors_ref[count + a : count + a + 1, :]
        tables = (far_cos * near_cos - far_sin * near_sin, far_sin * near_cos + far_cos * near_sin)
        rows = slice(near * a, near * (a + 1))
        for part, table in enumerate(tables):
            high = table.astype(jnp.bfloat16)
            lanes = slice(columns * part, columns * (part + 1))
            high_ref[rows, lanes] = high
            low_ref[rows, lanes] = (table - high.astype(jnp.float32)).astype(jnp.bfloat16)


def moved_right(value):
    lanes = value.shape[-1]
    lane = lax.broadcasted_iota(jnp.int32, (1, lanes), 1)
    return jnp.where(lane == 0, 0.0, pltpu.roll(value, 1, 1))


def moved_left(value):
    lanes = value.shape[-1]
    lane = lax.broadcasted_iota(jnp.int32, (1, lanes), 1)
    return jnp.where(lane == lanes - 1, 0.0, pltpu.roll(value, lanes - 1, 1))


def half_silu(half):
    return half + half * jnp.tanh(half)


def table_product(source, high_ref, low_ref):
    rows = source.shape[0]
    high = source.astype(jnp.bfloat16)
    low = (source - high.astype(jnp.float32)).astype(jnp.bfloat16)
    both = jnp.dot(
        jnp.concatenate([high, low], axis=0), high_ref[...], preferred_element_type=jnp.float32
    )
    rest = jnp.dot(high, low_ref[...], preferred_element_type=jnp.float32)
    return both[:rows] + both[rows:] + rest


def halves_swapped(value):
    return pltpu.roll(value, 4, value.ndim - 2)


def upper_half(value):
    return lax.broadcasted_iota(jnp.int32, value.shape, value.ndim - 2) < 4


def signed_swap(value, top, bottom):
    sign = jnp.where(upper_half(value), top, bottom)
    return sign * halves_swapped(value)


def stacked_parts(value):
    return jnp.concatenate([value[..., 0, :, :], value[..., 1, :, :]], axis=-2)


def turned_tiles(value, shift, store):
    tiles = value.shape[-1] // 128
    whole, part = shift // 128, lax.rem(shift, 128)
    moved = [
        pltpu.roll(value[..., 128 * j : 128 * (j + 1)], part, value.ndim - 1) for j in range(tiles)
    ]
    lane = lax.broadcasted_iota(jnp.int32, moved[0].shape, value.ndim - 1)
    for j in range(tiles):
        store(lax.rem(j + whole, tiles), jnp.where(lane < part, moved[j - 1], moved[j]))


def consistency_kernel(
    image_ref, steps_hbm, order_hbm, size_ref, coil_hbm, kspace_hbm, mask_hbm, factors_hbm,
    out_ref,
    steps_ref, order_ref, coil_ref, kspace_ref, mask_ref, factors_ref, high_ref, low_ref,
    turned_ref, real_ref, imag_ref, field_ref, swap_ref, sum_ref, sems, coil_sems,
):
    all_positions, slices, coils, _, rows, columns = coil_ref.shape
    tiles = columns // 128
    unit = columns // 8
    pairs = (
        (steps_hbm, steps_ref), (order_hbm, order_ref),
        (kspace_hbm, kspace_ref), (mask_hbm, mask_ref), (factors_hbm, factors_ref),
    )
    copies = [pltpu.make_async_copy(src, dst, sems.at[i]) for i, (src, dst) in enumerate(pairs)]
    for copy in copies[:2]:
        copy.start()
    for g in range(all_positions):
        pltpu.make_async_copy(coil_hbm.at[g], coil_ref.at[g], coil_sems.at[g]).start()
    for copy in copies[2:]:
        copy.start()
    for copy in copies[:2]:
        copy.wait()

    def shift_of(g):
        return steps_ref[order_ref[g]] * unit

    def turn_coils(g):
        shift = shift_of(g)
        image = image_ref[g].astype(jnp.float32)

        def store_image(j, value):
            other = halves_swapped(value)
            top = upper_half(value)
            real_ref[j, g] = jnp.where(top, value, other)
            imag_ref[j, g] = jnp.where(top, other, value)

        turned_tiles(image, shift, store_image)
        pltpu.make_async_copy(coil_hbm.at[g], coil_ref.at[g], coil_sems.at[g]).wait()
        for s in range(slices):
            coil = stacked_parts(coil_ref[g, s].astype(jnp.float32))

            def store_coil(j, value, s=s):
                turned_ref[j, g, s] = value

            turned_tiles(coil, shift, store_coil)

    for g in range(all_positions):
        turn_coils(g)

    block = coils * 2 * rows
    for j in range(tiles):
        for s in range(slices):
            with_real = jnp.zeros((coils, 2 * rows, 128), jnp.float32)
            with_imag = jnp.zeros((coils, 2 * rows, 128), jnp.float32)
            for g in range(all_positions):
                coil = turned_ref[j, g, s]
                with_real += coil * real_ref[j, g, s]
                with_imag += coil * imag_ref[j, g, s]
            total = with_real + signed_swap(with_imag, -1.0, 1.0)
            field_ref[s * block : (s + 1) * block, 128 * j : 128 * (j + 1)] = total.reshape(
                block, 128
            )

    for copy in copies[2:]:
        copy.wait()
    build_tables(factors_ref, high_ref, low_ref)
    product = table_product(field_ref[...], high_ref, low_ref)
    grouped = (slices, coils, 2 * rows, columns)
    with_cos = product[:, :columns].reshape(grouped)
    with_sin = product[:, columns:].reshape(grouped)
    spectrum = with_cos + signed_swap(with_sin, 1.0, -1.0)
    keep = mask_ref[...].astype(jnp.float32).reshape(slices, 1, 1, columns)
    residual = keep * (spectrum - stacked_parts(kspace_ref[...]))
    product = table_product(residual.reshape(slices * block, columns), high_ref, low_ref)
    with_cos = product[:, :columns].reshape(grouped)
    with_sin = product[:, columns:].reshape(grouped)
    back = with_cos + signed_swap(with_sin, -1.0, 1.0)
    field_ref[...] = back.reshape(slices * block, columns)
    swap_ref[...] = halves_swapped(back).reshape(slices * block, columns)

    size = size_ref[0]
    for j in range(tiles):
        for s in range(slices):
            place = (slice(s * block, (s + 1) * block), slice(128 * j, 128 * (j + 1)))
            field = field_ref[place].reshape(coils, 2 * rows, 128)
            swapped = swap_ref[place].reshape(coils, 2 * rows, 128)
            for g in range(all_positions):
                coil = turned_ref[j, g, s]
                straight = jnp.sum(coil * field, axis=0)
                crossed = jnp.sum(coil * swapped, axis=0)
                straight = straight + halves_swapped(straight)
                crossed = halves_swapped(crossed) - crossed
                sum_ref[g, s, :, 128 * j : 128 * (j + 1)] = size * jnp.where(
                    upper_half(straight), straight, crossed
                )

    for g in range(all_positions):
        back_shift = lax.rem(columns - shift_of(g), columns)
        turned = pltpu.roll(sum_ref[g], back_shift, 2).astype(jnp.bfloat16)
        out_ref[g, :, 0] = turned[:, :rows]
        out_ref[g, :, 1] = turned[:, rows:]


def partial_consistency(
    everyone, step_size, coil_maps, measured_kspace, sample_mask, caipi_steps, band_order
):
    all_positions, slices, coils, _, rows, columns = coil_maps.shape
    total = slices * coils * 2 * rows
    factors = jnp.asarray(dft_factors(columns))
    table = (columns, 2 * columns)
    hbm = pl.BlockSpec(memory_space=pltpu.HBM)
    vmem = pl.BlockSpec(memory_space=pltpu.VMEM)
    tile_shape = (columns // 128, all_positions, slices)
    return pl.pallas_call(
        consistency_kernel,
        out_shape=jax.ShapeDtypeStruct((all_positions, slices, 2, rows, columns), jnp.bfloat16),
        in_specs=[vmem, hbm, hbm, pl.BlockSpec(memory_space=pltpu.SMEM)] + [hbm] * 4,
        out_specs=vmem,
        scratch_shapes=[
            pltpu.SMEM(caipi_steps.shape, jnp.int32),
            pltpu.SMEM(band_order.shape, jnp.int32),
            pltpu.VMEM(coil_maps.shape, jnp.bfloat16),
            pltpu.VMEM(measured_kspace.shape, jnp.float32),
            pltpu.VMEM(sample_mask.shape, jnp.int32),
            pltpu.VMEM(factors.shape, jnp.float32),
            pltpu.VMEM(table, jnp.bfloat16),
            pltpu.VMEM(table, jnp.bfloat16),
            pltpu.VMEM(tile_shape + (coils, 2 * rows, 128), jnp.float32),
            pltpu.VMEM(tile_shape + (2 * rows, 128), jnp.float32),
            pltpu.VMEM(tile_shape + (2 * rows, 128), jnp.float32),
            pltpu.VMEM((total, columns), jnp.float32),
            pltpu.VMEM((total, columns), jnp.float32),
            pltpu.VMEM((all_positions, slices, 2 * rows, columns), jnp.float32),
            pltpu.SemaphoreType.DMA((5,)),
            pltpu.SemaphoreType.DMA((all_positions,)),
        ],
        compiler_params=pltpu.CompilerParams(vmem_limit_bytes=48 * 2**20),
        cost_estimate=pl.CostEstimate(
            flops=8 * 10**9, bytes_accessed=4 * 10**6, transcendentals=0
        ),
    )(
        everyone,
        *in_hbm(caipi_steps, band_order),
        step_size,
        *in_hbm(coil_maps, measured_kspace, sample_mask),
        factors,
    )


def network_kernel(
    window_ref, size_ref, first_hbm, mid_hbm, last_hbm, image_hbm, noise_hbm,
    out_ref,
    first_raw, mid_raw, last_raw, image_ref, noise_ref,
    first_sum, last_sum, first_ref, wide_ref, last_ref,
    taps_ref, f1_ref, f2_ref, part_a, part_b, score_ref, sems,
):
    channels = mid_raw.shape[-1]
    out_slices, _, rows, columns = out_ref.shape
    slices1, slices2 = out_slices + 4, out_slices + 2
    pairs = (
        (first_hbm, first_raw), (mid_hbm, mid_raw), (last_hbm, last_raw),
        (image_hbm, image_ref), (noise_hbm, noise_ref),
    )
    copies = [pltpu.make_async_copy(src, dst, sems.at[i]) for i, (src, dst) in enumerate(pairs)]
    for copy in copies:
        copy.start()

    def inside(axis, end):
        edge = lax.axis_size(axis) - 1 if end else 0
        return jnp.where(lax.axis_index(axis) == edge, 0.0, 1.0).astype(jnp.float32)

    low_slice, high_slice = inside("band", False), inside("band", True)
    low_row, high_row = inside("slab", False), inside("slab", True)
    four, two = 4 * channels, 2 * channels

    for g in range(2):
        base = window_ref[g].astype(jnp.float32)
        taps_ref[g, 0] = moved_right(base).astype(jnp.bfloat16)
        taps_ref[g, 1] = window_ref[g]
        taps_ref[g, 2] = moved_left(base).astype(jnp.bfloat16)

    first_sum[...] = jnp.zeros_like(first_sum)
    copies[0].wait()
    for d in range(3):
        for u in range(3):
            for t in range(3):
                block = first_raw[d, u, t].astype(jnp.float32) * 0.5
                for i in range(2):
                    for r in range(4):
                        row = (t * 3 + d) * 16 + i * 8 + u + r
                        first_sum[row : row + 1, r * channels : (r + 1) * channels] = block[
                            i : i + 1
                        ]
    first_ref[...] = first_sum[...].T[:, : first_ref.shape[1]].astype(jnp.bfloat16)

    copies[1].wait()
    half_weight = jnp.bfloat16(0.5)
    for t in range(3):
        for r in range(2):
            row = (t * 2 + r) * channels
            for d in range(3):
                for pair in range(2):
                    blocks = []
                    for q in (2 * pair, 2 * pair + 1):
                        if 0 <= q - r <= 2:
                            blocks.append(mid_raw[d, q - r, t] * half_weight)
                        else:
                            blocks.append(jnp.zeros((channels, channels), jnp.bfloat16))
                    col = (d * 4 + 2 * pair) * channels
                    wide_ref[row : row + channels, col : col + two] = jnp.concatenate(
                        blocks, axis=1
                    )

    last_sum[...] = jnp.zeros_like(last_sum)
    copies[2].wait()
    for d in range(3):
        for u in range(3):
            for t in range(3):
                block = last_raw[d, u, t].astype(jnp.float32)
                for o in range(2):
                    for r in range(4):
                        row = (d * 3 + t) * 8 + o * 4 + r
                        col = (r + u) * channels
                        last_sum[row : row + 1, col : col + channels] = block[o : o + 1]
    last_ref[...] = last_sum[...].astype(jnp.bfloat16)

    def first_layer(z):
        source = jnp.concatenate(
            [
                jnp.concatenate([taps_ref[g, t, 16 * z : 16 * z + 48, :] for t in range(3)], axis=0)
                for g in range(2)
            ],
            axis=1,
        )
        half = jnp.dot(first_ref[...], source, preferred_element_type=jnp.float32)
        for r in range(8):
            begin = (r % 4) * channels
            first = columns * (r // 4)
            value = half_silu(half[begin : begin + channels, first : first + columns])
            factors = []
            if z < 2:
                factors.append(low_slice)
            if z >= slices1 - 2:
                factors.append(high_slice)
            if r < 2:
                factors.append(low_row)
            if r >= 6:
                factors.append(high_row)
            for factor in factors:
                value = value * factor
            f1_ref[z, r * channels : (r + 1) * channels, :] = value.astype(jnp.bfloat16)

    def second_product(z, pair, part_ref):
        source = jnp.concatenate(
            [
                f1_ref[z + a : z + a + 3, two * pair : two * pair + four, :].reshape(
                    3 * four, columns
                )
                for a in range(2)
            ],
            axis=1,
        )
        part_ref[...] = jnp.dot(wide_ref[...], source, preferred_element_type=jnp.float32)

    def second_layer(z, pair, part_ref):
        for a in range(2):
            first = columns * a
            for r in range(2):
                row = r * channels
                half = (
                    moved_right(part_ref[row : row + channels, first : first + columns])
                    + part_ref[two + row : two + row + channels, first : first + columns]
                    + moved_left(
                        part_ref[four + row : four + row + channels, first : first + columns]
                    )
                )
                value = half_silu(half)
                factors = []
                if z + a == 0:
                    factors.append(low_slice)
                if z + a == slices2 - 1:
                    factors.append(high_slice)
                if pair == 0 and r == 0:
                    factors.append(low_row)
                if pair == 2 and r == 1:
                    factors.append(high_row)
                for factor in factors:
                    value = value * factor
                place = two * pair + r * channels
                f2_ref[z + a, place : place + channels, :] = value.astype(jnp.bfloat16)

    def third_product(z):
        source = jnp.concatenate([f2_ref[z], f2_ref[z + 1]], axis=1)
        score_ref[z // 2] = jnp.dot(last_ref[...], source, preferred_element_type=jnp.float32)

    for z in range(4):
        first_layer(z)
    waiting = None
    parts = (part_a, part_b)
    count = 0
    for z in range(0, slices2, 2):
        for pair in range(3):
            second_product(z, pair, parts[count % 2])
            if pair < 2 and z + 4 + pair < slices1:
                first_layer(z + 4 + pair)
            if waiting is not None:
                second_layer(*waiting)
                if waiting[1] == 2:
                    third_product(waiting[0])
            waiting = (z, pair, parts[count % 2])
            count += 1
    second_layer(*waiting)
    third_product(waiting[0])

    for copy in copies[3:]:
        copy.wait()
    size = size_ref[0]
    noise_scale = jnp.sqrt(jnp.full((1, columns), 2.0 * size, jnp.float32))
    for z in range(out_slices):
        taps = []
        for t in range(3):
            total = None
            for d in range(3):
                row, first = (3 * d + t) * 8, columns * ((z + d) % 2)
                piece = score_ref[(z + d) // 2, row : row + 8, first : first + columns]
                total = piece if total is None else total + piece
            taps.append(total)
        score = size * (moved_right(taps[0]) + taps[1] + moved_left(taps[2]))
        for part in range(2):
            out_ref[z, part] = (
                image_ref[z, part]
                + score[part * rows : (part + 1) * rows]
                + noise_scale * noise_ref[z, part]
            )


def stepped_without_data(
    windows, current_image, langevin_noise, step_size, weight_in, weight_mid, weight_out
):
    channels = weight_mid.shape[0]
    slices0, columns = windows.shape[1] // 16, windows.shape[-1]
    out_slices = slices0 - 6
    local = (out_slices,) + current_image.shape[2:]
    first = jnp.transpose(weight_in, (2, 3, 4, 1, 0))
    mid = jnp.transpose(weight_mid, (2, 3, 4, 0, 1))
    last = jnp.transpose(weight_out, (2, 3, 4, 0, 1))
    hbm = pl.BlockSpec(memory_space=pltpu.HBM)
    vmem = pl.BlockSpec(memory_space=pltpu.VMEM)
    return pl.pallas_call(
        network_kernel,
        out_shape=jax.ShapeDtypeStruct(local, jnp.float32),
        in_specs=[vmem, pl.BlockSpec(memory_space=pltpu.SMEM)] + [hbm] * 5,
        out_specs=vmem,
        scratch_shapes=[
            pltpu.VMEM(first.shape, jnp.bfloat16),
            pltpu.VMEM(mid.shape, jnp.bfloat16),
            pltpu.VMEM(last.shape, jnp.bfloat16),
            pltpu.VMEM(local, jnp.float32),
            pltpu.VMEM(local, jnp.float32),
            pltpu.VMEM((256, 4 * channels), jnp.float32),
            pltpu.VMEM((72, 6 * channels), jnp.float32),
            pltpu.VMEM((4 * channels, 144), jnp.bfloat16),
            pltpu.VMEM((6 * channels, 12 * channels), jnp.bfloat16),
            pltpu.VMEM((72, 6 * channels), jnp.bfloat16),
            pltpu.VMEM((2, 3, slices0 * 16, columns), jnp.bfloat16),
            pltpu.VMEM((out_slices + 4, 8 * channels, columns), jnp.bfloat16),
            pltpu.VMEM((out_slices + 2, 6 * channels, columns), jnp.bfloat16),
            pltpu.VMEM((6 * channels, 2 * columns), jnp.float32),
            pltpu.VMEM((6 * channels, 2 * columns), jnp.float32),
            pltpu.VMEM((out_slices // 2 + 1, 72, 2 * columns), jnp.float32),
            pltpu.SemaphoreType.DMA((5,)),
        ],
        compiler_params=pltpu.CompilerParams(vmem_limit_bytes=48 * 2**20),
        cost_estimate=pl.CostEstimate(
            flops=10**10, bytes_accessed=2 * 10**6, transcendentals=4 * 10**6
        ),
    )(
        windows,
        step_size,
        *in_hbm(first, mid, last),
        *in_hbm(current_image.reshape(local), langevin_noise.reshape(local)),
    ).reshape(current_image.shape)


def per_device(
    current_image, langevin_noise, step_size, coil_maps, measured_kspace, sample_mask,
    caipi_steps, band_order, weight_in, weight_mid, weight_out,
):
    positions, group_slices, _, row_count, columns = current_image.shape
    local_slices = positions * group_slices
    own = current_image.astype(jnp.bfloat16).reshape(
        positions, group_slices, 2 * row_count, columns
    )
    everyone = lax.all_gather(own, "band", axis=0, tiled=True)

    volume = everyone.reshape(-1, 2, row_count, columns)
    volume = jnp.pad(volume, ((3, 3), (0, 0), (0, 0), (0, 0)))
    tall = lax.dynamic_slice_in_dim(
        volume, lax.axis_index("band") * local_slices, local_slices + 6, axis=0
    )
    below, above = exchanged_rows(tall, 3)
    field = jnp.concatenate([below, tall, above, jnp.zeros_like(above[:, :, :2])], axis=2)
    windows = jnp.stack(
        [field[:, :, 4 * g : 4 * g + 8].reshape(-1, columns) for g in range(2)], axis=0
    )
    partial_sums = partial_consistency(
        everyone, step_size, coil_maps, measured_kspace, sample_mask, caipi_steps, band_order
    )
    swapped = lax.all_to_all(partial_sums, "band", split_axis=0, concat_axis=0, tiled=True)
    base = stepped_without_data(
        windows, current_image, langevin_noise, step_size, weight_in, weight_mid, weight_out
    )
    pieces = swapped.reshape((-1, positions) + swapped.shape[1:]).astype(jnp.float32)
    return base - jnp.sum(pieces, axis=0)


def solution(mesh):
    band5 = P("band", None, None, "slab", None)
    in_specs = (
        band5,
        band5,
        P(),
        P(None, None, "band", None, "slab", None),
        P(None, "band", None, "slab", None),
        P(), P(), P(), P(), P(), P(),
    )
    return jax.shard_map(
        per_device, mesh=mesh, in_specs=in_specs, out_specs=band5, check_vma=False
    )
```

```python
import functools
import math

import jax
import jax.numpy as jnp
import numpy as np
from jax import lax
from jax.experimental import pallas as pl
from jax.experimental.pallas import tpu as pltpu
from jax.sharding import PartitionSpec as P


def exchanged_rows(tall, width):
    count = lax.axis_size("slab")
    odd = lax.axis_index("slab") % 2 == 1
    head, tail = tall[:, :, :width, :], tall[:, :, tall.shape[2] - width :, :]
    arrived = []
    for first in range(2):
        route = []
        for i in range(first, count - 1, 2):
            route += [(i, i + 1), (i + 1, i)]
        sent = jnp.where(odd, head, tail) if first == 0 else jnp.where(odd, tail, head)
        arrived.append(lax.ppermute(sent, "slab", route))
    below = jnp.where(odd, arrived[0], arrived[1])
    above = jnp.where(odd, arrived[1], arrived[0])
    return below, above


def in_hbm(*arrays):
    return [pltpu.with_memory_space_constraint(array, pltpu.HBM) for array in arrays]


def dft_factors(columns):
    near = 16
    index = np.arange(columns)
    pieces = []
    for rows in (near * np.arange(columns // near), np.arange(near)):
        phase = (np.outer(rows, index) % columns) * (2.0 * math.pi / columns)
        pieces += [np.cos(phase), np.sin(phase)]
    far = np.concatenate(pieces[:2], axis=0) / math.sqrt(columns)
    return np.concatenate([far] + pieces[2:], axis=0).astype(np.float32)


def build_tables(factors_ref, high_ref, low_ref):
    columns = factors_ref.shape[1]
    near = 16
    count = columns // near
    near_cos = factors_ref[2 * count : 2 * count + near, :]
    near_sin = factors_ref[2 * count + near :, :]
    for a in range(count):
        far_cos = factors_ref[a : a + 1, :]
        far_sin = factors_ref[count + a : count + a + 1, :]
        tables = (far_cos * near_cos - far_sin * near_sin, far_sin * near_cos + far_cos * near_sin)
        rows = slice(near * a, near * (a + 1))
        for part, table in enumerate(tables):
            high = table.astype(jnp.bfloat16)
            lanes = slice(columns * part, columns * (part + 1))
            high_ref[rows, lanes] = high
            low_ref[rows, lanes] = (table - high.astype(jnp.float32)).astype(jnp.bfloat16)


def moved_right(value):
    tiles = value.shape[-1] // 128
    moved = [pltpu.roll(value[:, 128 * j : 128 * (j + 1)], 1, 1) for j in range(tiles)]
    edge = lax.broadcasted_iota(jnp.int32, moved[0].shape, 1) == 0
    return jnp.concatenate(
        [jnp.where(edge, moved[j - 1] if j > 0 else 0.0, moved[j]) for j in range(tiles)], axis=1
    )


def moved_left(value):
    tiles = value.shape[-1] // 128
    moved = [pltpu.roll(value[:, 128 * j : 128 * (j + 1)], 127, 1) for j in range(tiles)]
    edge = lax.broadcasted_iota(jnp.int32, moved[0].shape, 1) == 127
    return jnp.concatenate(
        [
            jnp.where(edge, moved[j + 1] if j < tiles - 1 else 0.0, moved[j])
            for j in range(tiles)
        ],
        axis=1,
    )


def half_silu(half):
    return half + half * jnp.tanh(half)


def table_product(source, high_ref, low_ref):
    rows = source.shape[0]
    high = source.astype(jnp.bfloat16)
    low = (source - high.astype(jnp.float32)).astype(jnp.bfloat16)
    both = jnp.dot(
        jnp.concatenate([high, low], axis=0), high_ref[...], preferred_element_type=jnp.float32
    )
    rest = jnp.dot(high, low_ref[...], preferred_element_type=jnp.float32)
    return both[:rows] + both[rows:] + rest


def halves_swapped(value):
    return pltpu.roll(value, 4, value.ndim - 2)


def upper_half(value):
    return lax.broadcasted_iota(jnp.int32, value.shape, value.ndim - 2) < 4


def signed_swap(value, top, bottom):
    sign = jnp.where(upper_half(value), top, bottom)
    return sign * halves_swapped(value)


def stacked_parts(value):
    return jnp.concatenate([value[..., 0, :, :], value[..., 1, :, :]], axis=-2)


def turned_tiles(value, shift, store):
    tiles = value.shape[-1] // 128
    whole, part = shift // 128, lax.rem(shift, 128)
    moved = [
        pltpu.roll(value[..., 128 * j : 128 * (j + 1)], part, value.ndim - 1) for j in range(tiles)
    ]
    lane = lax.broadcasted_iota(jnp.int32, moved[0].shape, value.ndim - 1)
    for j in range(tiles):
        store(lax.rem(j + whole, tiles), jnp.where(lane < part, moved[j - 1], moved[j]))


def consistency_kernel(
    image_hbm, steps_hbm, order_hbm, size_ref, coil_hbm, kspace_hbm, mask_hbm, factors_hbm,
    out_ref,
    image_ref, steps_ref, order_ref, coil_ref, kspace_ref, mask_ref, factors_ref,
    high_ref, low_ref, turned_ref, real_ref, imag_ref, field_ref, swap_ref, sum_ref,
    sems, coil_sems,
):
    all_positions, slices, coils, _, rows, columns = coil_ref.shape
    tiles = columns // 128
    unit = columns // 8
    pairs = (
        (factors_hbm, factors_ref), (steps_hbm, steps_ref), (order_hbm, order_ref),
        (image_hbm, image_ref), (kspace_hbm, kspace_ref), (mask_hbm, mask_ref),
    )
    copies = [pltpu.make_async_copy(src, dst, sems.at[i]) for i, (src, dst) in enumerate(pairs)]
    for copy in copies[:3]:
        copy.start()
    for g in range(all_positions):
        pltpu.make_async_copy(coil_hbm.at[g], coil_ref.at[g], coil_sems.at[g]).start()
    for copy in copies[3:]:
        copy.start()
    copies[0].wait()
    build_tables(factors_ref, high_ref, low_ref)
    for copy in copies[1:3]:
        copy.wait()

    def shift_of(g):
        return steps_ref[order_ref[g]] * unit

    def turn_coils(g):
        shift = shift_of(g)
        pltpu.make_async_copy(coil_hbm.at[g], coil_ref.at[g], coil_sems.at[g]).wait()
        for s in range(slices):
            coil = stacked_parts(coil_ref[g, s].astype(jnp.float32))

            def store_coil(j, value, s=s):
                turned_ref[j, g, s] = value

            turned_tiles(coil, shift, store_coil)

    for g in range(all_positions):
        turn_coils(g)
    for copy in copies[3:]:
        copy.wait()
    for g in range(all_positions):

        def store_image(j, value, g=g):
            other = halves_swapped(value)
            top = upper_half(value)
            real_ref[j, g] = jnp.where(top, value, other)
            imag_ref[j, g] = jnp.where(top, other, value)

        turned_tiles(image_ref[g].astype(jnp.float32), shift_of(g), store_image)

    block = coils * 2 * rows
    for j in range(tiles):
        for s in range(slices):
            with_real = jnp.zeros((coils, 2 * rows, 128), jnp.float32)
            with_imag = jnp.zeros((coils, 2 * rows, 128), jnp.float32)
            for g in range(all_positions):
                coil = turned_ref[j, g, s]
                with_real += coil * real_ref[j, g, s]
                with_imag += coil * imag_ref[j, g, s]
            total = with_real + signed_swap(with_imag, -1.0, 1.0)
            field_ref[s * block : (s + 1) * block, 128 * j : 128 * (j + 1)] = total.reshape(
                block, 128
            )

    product = table_product(field_ref[...], high_ref, low_ref)
    grouped = (slices, coils, 2 * rows, columns)
    with_cos = product[:, :columns].reshape(grouped)
    with_sin = product[:, columns:].reshape(grouped)
    spectrum = with_cos + signed_swap(with_sin, 1.0, -1.0)
    keep = mask_ref[...].astype(jnp.float32).reshape(slices, 1, 1, columns)
    residual = keep * (spectrum - stacked_parts(kspace_ref[...]))
    product = table_product(residual.reshape(slices * block, columns), high_ref, low_ref)
    with_cos = product[:, :columns].reshape(grouped)
    with_sin = product[:, columns:].reshape(grouped)
    back = with_cos + signed_swap(with_sin, -1.0, 1.0)
    field_ref[...] = back.reshape(slices * block, columns)
    swap_ref[...] = halves_swapped(back).reshape(slices * block, columns)

    size = size_ref[0]
    for j in range(tiles):
        for s in range(slices):
            place = (slice(s * block, (s + 1) * block), slice(128 * j, 128 * (j + 1)))
            field = field_ref[place].reshape(coils, 2 * rows, 128)
            swapped = swap_ref[place].reshape(coils, 2 * rows, 128)
            for g in range(all_positions):
                coil = turned_ref[j, g, s]
                straight = jnp.sum(coil * field, axis=0)
                crossed = jnp.sum(coil * swapped, axis=0)
                straight = straight + halves_swapped(straight)
                crossed = halves_swapped(crossed) - crossed
                sum_ref[g, s, :, 128 * j : 128 * (j + 1)] = size * jnp.where(
                    upper_half(straight), straight, crossed
                )

    for g in range(all_positions):
        back_shift = lax.rem(columns - shift_of(g), columns)
        turned = pltpu.roll(sum_ref[g], back_shift, 2).astype(jnp.bfloat16)
        out_ref[g, :, 0] = turned[:, :rows]
        out_ref[g, :, 1] = turned[:, rows:]


def partial_consistency(
    everyone, step_size, coil_maps, measured_kspace, sample_mask, caipi_steps, band_order
):
    all_positions, slices, coils, _, rows, columns = coil_maps.shape
    total = slices * coils * 2 * rows
    factors = jnp.asarray(dft_factors(columns))
    table = (columns, 2 * columns)
    hbm = pl.BlockSpec(memory_space=pltpu.HBM)
    vmem = pl.BlockSpec(memory_space=pltpu.VMEM)
    tile_shape = (columns // 128, all_positions, slices)
    return pl.pallas_call(
        consistency_kernel,
        out_shape=jax.ShapeDtypeStruct((all_positions, slices, 2, rows, columns), jnp.bfloat16),
        in_specs=[hbm] * 3 + [pl.BlockSpec(memory_space=pltpu.SMEM)] + [hbm] * 4,
        out_specs=vmem,
        scratch_shapes=[
            pltpu.VMEM(everyone.shape, jnp.bfloat16),
            pltpu.SMEM(caipi_steps.shape, jnp.int32),
            pltpu.SMEM(band_order.shape, jnp.int32),
            pltpu.VMEM(coil_maps.shape, jnp.bfloat16),
            pltpu.VMEM(measured_kspace.shape, jnp.float32),
            pltpu.VMEM(sample_mask.shape, jnp.int32),
            pltpu.VMEM(factors.shape, jnp.float32),
            pltpu.VMEM(table, jnp.bfloat16),
            pltpu.VMEM(table, jnp.bfloat16),
            pltpu.VMEM(tile_shape + (coils, 2 * rows, 128), jnp.float32),
            pltpu.VMEM(tile_shape + (2 * rows, 128), jnp.float32),
            pltpu.VMEM(tile_shape + (2 * rows, 128), jnp.float32),
            pltpu.VMEM((total, columns), jnp.float32),
            pltpu.VMEM((total, columns), jnp.float32),
            pltpu.VMEM((all_positions, slices, 2 * rows, columns), jnp.float32),
            pltpu.SemaphoreType.DMA((6,)),
            pltpu.SemaphoreType.DMA((all_positions,)),
        ],
        compiler_params=pltpu.CompilerParams(vmem_limit_bytes=48 * 2**20),
        cost_estimate=pl.CostEstimate(
            flops=8 * 10**9, bytes_accessed=4 * 10**6, transcendentals=0
        ),
    )(
        *in_hbm(everyone, caipi_steps, band_order),
        step_size,
        *in_hbm(coil_maps, measured_kspace, sample_mask),
        factors,
    )


def network_kernel(
    window_ref, size_ref, first_hbm, mid_hbm, last_hbm, image_hbm, noise_hbm,
    out_ref,
    first_raw, mid_raw, last_raw, image_ref, noise_ref,
    first_sum, last_sum, first_ref, wide_ref, last_ref,
    taps_ref, f1_ref, f2_ref, part_a, part_b, score_ref, sems,
):
    channels = mid_raw.shape[-1]
    out_slices, _, rows, columns = out_ref.shape
    slices1, slices2 = out_slices + 4, out_slices + 2
    pairs = (
        (first_hbm, first_raw), (mid_hbm, mid_raw), (last_hbm, last_raw),
        (image_hbm, image_ref), (noise_hbm, noise_ref),
    )
    copies = [pltpu.make_async_copy(src, dst, sems.at[i]) for i, (src, dst) in enumerate(pairs)]
    for copy in copies:
        copy.start()

    def inside(axis, end):
        edge = lax.axis_size(axis) - 1 if end else 0
        return jnp.where(lax.axis_index(axis) == edge, 0.0, 1.0).astype(jnp.float32)

    low_slice, high_slice = inside("band", False), inside("band", True)
    low_row, high_row = inside("slab", False), inside("slab", True)
    four, two = 4 * channels, 2 * channels

    for g in range(2):
        base = window_ref[g].astype(jnp.float32)
        taps_ref[g, 0] = moved_right(base).astype(jnp.bfloat16)
        taps_ref[g, 1] = window_ref[g]
        taps_ref[g, 2] = moved_left(base).astype(jnp.bfloat16)

    first_sum[...] = jnp.zeros_like(first_sum)
    copies[0].wait()
    for d in range(3):
        for u in range(3):
            for t in range(3):
                block = first_raw[d, u, t].astype(jnp.float32) * 0.5
                for i in range(2):
                    for r in range(4):
                        row = (t * 3 + d) * 16 + i * 8 + u + r
                        first_sum[row : row + 1, r * channels : (r + 1) * channels] = block[
                            i : i + 1
                        ]
    first_ref[...] = first_sum[...].T[:, : first_ref.shape[1]].astype(jnp.bfloat16)

    copies[1].wait()
    half_weight = jnp.bfloat16(0.5)
    for t in range(3):
        for r in range(2):
            row = (t * 2 + r) * channels
            for d in range(3):
                for pair in range(2):
                    blocks = []
                    for q in (2 * pair, 2 * pair + 1):
                        if 0 <= q - r <= 2:
                            blocks.append(mid_raw[d, q - r, t] * half_weight)
                        else:
                            blocks.append(jnp.zeros((channels, channels), jnp.bfloat16))
                    col = (d * 4 + 2 * pair) * channels
                    wide_ref[row : row + channels, col : col + two] = jnp.concatenate(
                        blocks, axis=1
                    )

    last_sum[...] = jnp.zeros_like(last_sum)
    copies[2].wait()
    for d in range(3):
        for u in range(3):
            for t in range(3):
                block = last_raw[d, u, t].astype(jnp.float32)
                for o in range(2):
                    for r in range(4):
                        row = (d * 3 + t) * 8 + o * 4 + r
                        col = (r + u) * channels
                        last_sum[row : row + 1, col : col + channels] = block[o : o + 1]
    last_ref[...] = last_sum[...].astype(jnp.bfloat16)

    def first_layer(z):
        source = jnp.concatenate(
            [
                jnp.concatenate([taps_ref[g, t, 16 * z : 16 * z + 48, :] for t in range(3)], axis=0)
                for g in range(2)
            ],
            axis=1,
        )
        half = jnp.dot(first_ref[...], source, preferred_element_type=jnp.float32)
        for r in range(8):
            begin = (r % 4) * channels
            first = columns * (r // 4)
            value = half_silu(half[begin : begin + channels, first : first + columns])
            factors = []
            if z < 2:
                factors.append(low_slice)
            if z >= slices1 - 2:
                factors.append(high_slice)
            if r < 2:
                factors.append(low_row)
            if r >= 6:
                factors.append(high_row)
            for factor in factors:
                value = value * factor
            f1_ref[z, r * channels : (r + 1) * channels, :] = value.astype(jnp.bfloat16)

    def second_product(z, pair, part_ref):
        source = jnp.concatenate(
            [
                f1_ref[z + a : z + a + 3, two * pair : two * pair + four, :].reshape(
                    3 * four, columns
                )
                for a in range(2)
            ],
            axis=1,
        )
        part_ref[...] = jnp.dot(wide_ref[...], source, preferred_element_type=jnp.float32)

    def second_layer(z, pair, part_ref):
        for a in range(2):
            first = columns * a
            for r in range(2):
                row = r * channels
                half = (
                    moved_right(part_ref[row : row + channels, first : first + columns])
                    + part_ref[two + row : two + row + channels, first : first + columns]
                    + moved_left(
                        part_ref[four + row : four + row + channels, first : first + columns]
                    )
                )
                value = half_silu(half)
                factors = []
                if z + a == 0:
                    factors.append(low_slice)
                if z + a == slices2 - 1:
                    factors.append(high_slice)
                if pair == 0 and r == 0:
                    factors.append(low_row)
                if pair == 2 and r == 1:
                    factors.append(high_row)
                for factor in factors:
                    value = value * factor
                place = two * pair + r * channels
                f2_ref[z + a, place : place + channels, :] = value.astype(jnp.bfloat16)

    def third_product(z):
        source = jnp.concatenate([f2_ref[z], f2_ref[z + 1]], axis=1)
        score_ref[z // 2] = jnp.dot(last_ref[...], source, preferred_element_type=jnp.float32)

    for z in range(4):
        first_layer(z)
    waiting = None
    parts = (part_a, part_b)
    count = 0
    for z in range(0, slices2, 2):
        for pair in range(3):
            second_product(z, pair, parts[count % 2])
            if pair < 2 and z + 4 + pair < slices1:
                first_layer(z + 4 + pair)
            if waiting is not None:
                second_layer(*waiting)
                if waiting[1] == 2:
                    third_product(waiting[0])
            waiting = (z, pair, parts[count % 2])
            count += 1
    second_layer(*waiting)
    third_product(waiting[0])

    for copy in copies[3:]:
        copy.wait()
    size = size_ref[0]
    noise_scale = jnp.sqrt(jnp.full((1, columns), 2.0 * size, jnp.float32))
    for z in range(out_slices):
        taps = []
        for t in range(3):
            total = None
            for d in range(3):
                row, first = (3 * d + t) * 8, columns * ((z + d) % 2)
                piece = score_ref[(z + d) // 2, row : row + 8, first : first + columns]
                total = piece if total is None else total + piece
            taps.append(total)
        score = size * (moved_right(taps[0]) + taps[1] + moved_left(taps[2]))
        for part in range(2):
            out_ref[z, part] = (
                image_ref[z, part]
                + score[part * rows : (part + 1) * rows]
                + noise_scale * noise_ref[z, part]
            )


def stepped_without_data(
    windows, current_image, langevin_noise, step_size, weight_in, weight_mid, weight_out
):
    channels = weight_mid.shape[0]
    slices0, columns = windows.shape[1] // 16, windows.shape[-1]
    out_slices = slices0 - 6
    local = (out_slices,) + current_image.shape[2:]
    first = jnp.transpose(weight_in, (2, 3, 4, 1, 0))
    mid = jnp.transpose(weight_mid, (2, 3, 4, 0, 1))
    last = jnp.transpose(weight_out, (2, 3, 4, 0, 1))
    hbm = pl.BlockSpec(memory_space=pltpu.HBM)
    vmem = pl.BlockSpec(memory_space=pltpu.VMEM)
    return pl.pallas_call(
        network_kernel,
        out_shape=jax.ShapeDtypeStruct(local, jnp.float32),
        in_specs=[vmem, pl.BlockSpec(memory_space=pltpu.SMEM)] + [hbm] * 5,
        out_specs=vmem,
        scratch_shapes=[
            pltpu.VMEM(first.shape, jnp.bfloat16),
            pltpu.VMEM(mid.shape, jnp.bfloat16),
            pltpu.VMEM(last.shape, jnp.bfloat16),
            pltpu.VMEM(local, jnp.float32),
            pltpu.VMEM(local, jnp.float32),
            pltpu.VMEM((256, 4 * channels), jnp.float32),
            pltpu.VMEM((72, 6 * channels), jnp.float32),
            pltpu.VMEM((4 * channels, 144), jnp.bfloat16),
            pltpu.VMEM((6 * channels, 12 * channels), jnp.bfloat16),
            pltpu.VMEM((72, 6 * channels), jnp.bfloat16),
            pltpu.VMEM((2, 3, slices0 * 16, columns), jnp.bfloat16),
            pltpu.VMEM((out_slices + 4, 8 * channels, columns), jnp.bfloat16),
            pltpu.VMEM((out_slices + 2, 6 * channels, columns), jnp.bfloat16),
            pltpu.VMEM((6 * channels, 2 * columns), jnp.float32),
            pltpu.VMEM((6 * channels, 2 * columns), jnp.float32),
            pltpu.VMEM((out_slices // 2 + 1, 72, 2 * columns), jnp.float32),
            pltpu.SemaphoreType.DMA((5,)),
        ],
        compiler_params=pltpu.CompilerParams(vmem_limit_bytes=48 * 2**20),
        cost_estimate=pl.CostEstimate(
            flops=10**10, bytes_accessed=2 * 10**6, transcendentals=4 * 10**6
        ),
    )(
        windows,
        step_size,
        *in_hbm(first, mid, last),
        *in_hbm(current_image.reshape(local), langevin_noise.reshape(local)),
    ).reshape(current_image.shape)


def per_device(
    current_image, langevin_noise, step_size, coil_maps, measured_kspace, sample_mask,
    caipi_steps, band_order, weight_in, weight_mid, weight_out,
):
    positions, group_slices, _, row_count, columns = current_image.shape
    local_slices = positions * group_slices
    own = current_image.astype(jnp.bfloat16).reshape(
        positions, group_slices, 2 * row_count, columns
    )
    everyone = lax.all_gather(own, "band", axis=0, tiled=True)

    volume = everyone.reshape(-1, 2, row_count, columns)
    volume = jnp.pad(volume, ((3, 3), (0, 0), (0, 0), (0, 0)))
    tall = lax.dynamic_slice_in_dim(
        volume, lax.axis_index("band") * local_slices, local_slices + 6, axis=0
    )
    below, above = exchanged_rows(tall, 3)
    partial_sums = partial_consistency(
        everyone, step_size, coil_maps, measured_kspace, sample_mask, caipi_steps, band_order
    )
    partial_sums, below, above = lax.optimization_barrier((partial_sums, below, above))
    swapped = lax.all_to_all(partial_sums, "band", split_axis=0, concat_axis=0, tiled=True)
    field = jnp.concatenate([below, tall, above, jnp.zeros_like(above[:, :, :2])], axis=2)
    windows = jnp.stack(
        [field[:, :, 4 * g : 4 * g + 8].reshape(-1, columns) for g in range(2)], axis=0
    )
    base = stepped_without_data(
        windows, current_image, langevin_noise, step_size, weight_in, weight_mid, weight_out
    )
    pieces = swapped.reshape((-1, positions) + swapped.shape[1:]).astype(jnp.float32)
    return base - jnp.sum(pieces, axis=0)


def solution(mesh):
    band5 = P("band", None, None, "slab", None)
    in_specs = (
        band5,
        band5,
        P(),
        P(None, None, "band", None, "slab", None),
        P(None, "band", None, "slab", None),
        P(), P(), P(), P(), P(), P(),
    )
    return jax.shard_map(
        per_device, mesh=mesh, in_specs=in_specs, out_specs=band5, check_vma=False
    )
```

```python
import functools
import math

import jax
import jax.numpy as jnp
import numpy as np
from jax import lax
from jax.experimental import pallas as pl
from jax.experimental.pallas import tpu as pltpu
from jax.sharding import PartitionSpec as P


def exchanged_rows(tall, width):
    count = lax.axis_size("slab")
    odd = lax.axis_index("slab") % 2 == 1
    head, tail = tall[:, :, :width, :], tall[:, :, tall.shape[2] - width :, :]
    arrived = []
    for first in range(2):
        route = []
        for i in range(first, count - 1, 2):
            route += [(i, i + 1), (i + 1, i)]
        sent = jnp.where(odd, head, tail) if first == 0 else jnp.where(odd, tail, head)
        arrived.append(lax.ppermute(sent, "slab", route))
    below = jnp.where(odd, arrived[0], arrived[1])
    above = jnp.where(odd, arrived[1], arrived[0])
    return below, above


def in_hbm(*arrays):
    return [pltpu.with_memory_space_constraint(array, pltpu.HBM) for array in arrays]


def dft_factors(columns):
    near = 16
    index = np.arange(columns)
    pieces = []
    for rows in (near * np.arange(columns // near), np.arange(near)):
        phase = (np.outer(rows, index) % columns) * (2.0 * math.pi / columns)
        pieces += [np.cos(phase), np.sin(phase)]
    far = np.concatenate(pieces[:2], axis=0) / math.sqrt(columns)
    return np.concatenate([far] + pieces[2:], axis=0).astype(np.float32)


def build_tables(factors_ref, high_ref, low_ref):
    columns = factors_ref.shape[1]
    near = 16
    count = columns // near
    near_cos = factors_ref[2 * count : 2 * count + near, :]
    near_sin = factors_ref[2 * count + near :, :]
    for a in range(count):
        far_cos = factors_ref[a : a + 1, :]
        far_sin = factors_ref[count + a : count + a + 1, :]
        tables = (far_cos * near_cos - far_sin * near_sin, far_sin * near_cos + far_cos * near_sin)
        rows = slice(near * a, near * (a + 1))
        for part, table in enumerate(tables):
            high = table.astype(jnp.bfloat16)
            lanes = slice(columns * part, columns * (part + 1))
            high_ref[rows, lanes] = high
            low_ref[rows, lanes] = (table - high.astype(jnp.float32)).astype(jnp.bfloat16)


def moved_right(value):
    tiles = value.shape[-1] // 128
    moved = [pltpu.roll(value[:, 128 * j : 128 * (j + 1)], 1, 1) for j in range(tiles)]
    edge = lax.broadcasted_iota(jnp.int32, moved[0].shape, 1) == 0
    return jnp.concatenate(
        [jnp.where(edge, moved[j - 1] if j > 0 else 0.0, moved[j]) for j in range(tiles)], axis=1
    )


def moved_left(value):
    tiles = value.shape[-1] // 128
    moved = [pltpu.roll(value[:, 128 * j : 128 * (j + 1)], 127, 1) for j in range(tiles)]
    edge = lax.broadcasted_iota(jnp.int32, moved[0].shape, 1) == 127
    return jnp.concatenate(
        [
            jnp.where(edge, moved[j + 1] if j < tiles - 1 else 0.0, moved[j])
            for j in range(tiles)
        ],
        axis=1,
    )


def half_silu(half):
    return half + half * jnp.tanh(half)


def table_product(source, high_ref, low_ref):
    rows = source.shape[0]
    high = source.astype(jnp.bfloat16)
    low = (source - high.astype(jnp.float32)).astype(jnp.bfloat16)
    both = jnp.dot(
        jnp.concatenate([high, low], axis=0), high_ref[...], preferred_element_type=jnp.float32
    )
    rest = jnp.dot(high, low_ref[...], preferred_element_type=jnp.float32)
    return both[:rows] + both[rows:] + rest


def halves_swapped(value):
    return pltpu.roll(value, 4, value.ndim - 2)


def upper_half(value):
    return lax.broadcasted_iota(jnp.int32, value.shape, value.ndim - 2) < 4


def signed_swap(value, top, bottom):
    sign = jnp.where(upper_half(value), top, bottom)
    return sign * halves_swapped(value)


def stacked_parts(value):
    return jnp.concatenate([value[..., 0, :, :], value[..., 1, :, :]], axis=-2)


def turned_tiles(value, shift, store):
    tiles = value.shape[-1] // 128
    whole, part = shift // 128, lax.rem(shift, 128)
    moved = [
        pltpu.roll(value[..., 128 * j : 128 * (j + 1)], part, value.ndim - 1) for j in range(tiles)
    ]
    lane = lax.broadcasted_iota(jnp.int32, moved[0].shape, value.ndim - 1)
    for j in range(tiles):
        store(lax.rem(j + whole, tiles), jnp.where(lane < part, moved[j - 1], moved[j]))


def fill_weights(first_raw, mid_raw, last_raw, first_sum, last_sum, first_ref, wide_ref, last_ref):
    channels = mid_raw.shape[-1]
    two = 2 * channels
    first_sum[...] = jnp.zeros_like(first_sum)
    last_sum[...] = jnp.zeros_like(last_sum)
    for d in range(3):
        for u in range(3):
            for t in range(3):
                block = first_raw[d, u, t].astype(jnp.float32) * 0.5
                for i in range(2):
                    for r in range(4):
                        row = (t * 3 + d) * 16 + i * 8 + u + r
                        first_sum[row : row + 1, r * channels : (r + 1) * channels] = block[
                            i : i + 1
                        ]
                block = last_raw[d, u, t].astype(jnp.float32)
                for o in range(2):
                    for r in range(4):
                        row = (d * 3 + t) * 8 + o * 4 + r
                        col = (r + u) * channels
                        last_sum[row : row + 1, col : col + channels] = block[o : o + 1]
    first_ref[...] = first_sum[...].T[:, : first_ref.shape[1]].astype(jnp.bfloat16)
    last_ref[...] = last_sum[...].astype(jnp.bfloat16)
    half_weight = jnp.bfloat16(0.5)
    for t in range(3):
        for r in range(2):
            row = (t * 2 + r) * channels
            for d in range(3):
                for pair in range(2):
                    blocks = []
                    for q in (2 * pair, 2 * pair + 1):
                        if 0 <= q - r <= 2:
                            blocks.append(mid_raw[d, q - r, t] * half_weight)
                        else:
                            blocks.append(jnp.zeros((channels, channels), jnp.bfloat16))
                    col = (d * 4 + 2 * pair) * channels
                    wide_ref[row : row + channels, col : col + two] = jnp.concatenate(
                        blocks, axis=1
                    )


def preparation_kernel(
    steps_hbm, order_hbm, coil_hbm, kspace_hbm, factors_hbm, first_hbm, mid_hbm, last_hbm,
    turned_ref, stacked_ref, high_ref, low_ref, first_ref, wide_ref, last_ref,
    steps_ref, order_ref, coil_ref, kspace_ref, factors_ref, first_raw, mid_raw, last_raw,
    first_sum, last_sum, sems, coil_sems,
):
    all_positions, slices, coils, _, rows, columns = coil_ref.shape
    unit = columns // 8
    pairs = (
        (first_hbm, first_raw), (mid_hbm, mid_raw), (last_hbm, last_raw),
        (factors_hbm, factors_ref), (steps_hbm, steps_ref), (order_hbm, order_ref),
        (kspace_hbm, kspace_ref),
    )
    copies = [pltpu.make_async_copy(src, dst, sems.at[i]) for i, (src, dst) in enumerate(pairs)]
    coil_copies = [
        pltpu.make_async_copy(coil_hbm.at[g], coil_ref.at[g], coil_sems.at[g])
        for g in range(all_positions)
    ]
    for copy in copies[:6] + coil_copies + copies[6:]:
        copy.start()
    for copy in copies[:3]:
        copy.wait()
    fill_weights(
        first_raw, mid_raw, last_raw, first_sum, last_sum, first_ref, wide_ref, last_ref
    )
    copies[3].wait()
    build_tables(factors_ref, high_ref, low_ref)
    for copy in copies[4:6]:
        copy.wait()
    for g in range(all_positions):
        shift = steps_ref[order_ref[g]] * unit
        coil_copies[g].wait()
        for s in range(slices):

            def store_coil(j, value, s=s, g=g):
                turned_ref[j, g, s] = value

            turned_tiles(stacked_parts(coil_ref[g, s].astype(jnp.float32)), shift, store_coil)
    copies[6].wait()
    for s in range(slices):
        stacked_ref[s] = stacked_parts(kspace_ref[s])


def preparation(
    coil_maps, measured_kspace, caipi_steps, band_order, weight_in, weight_mid, weight_out
):
    all_positions, slices, coils, _, rows, columns = coil_maps.shape
    channels = weight_mid.shape[0]
    factors = jnp.asarray(dft_factors(columns))
    first = jnp.transpose(weight_in, (2, 3, 4, 1, 0))
    mid = jnp.transpose(weight_mid, (2, 3, 4, 0, 1))
    last = jnp.transpose(weight_out, (2, 3, 4, 0, 1))
    f32, bf16 = jnp.float32, jnp.bfloat16
    hbm = pl.BlockSpec(memory_space=pltpu.HBM)
    vmem = pl.BlockSpec(memory_space=pltpu.VMEM)
    return pl.pallas_call(
        preparation_kernel,
        out_shape=(
            jax.ShapeDtypeStruct((columns // 128, all_positions, slices, coils, 2 * rows, 128), f32),
            jax.ShapeDtypeStruct((slices, coils, 2 * rows, columns), f32),
            jax.ShapeDtypeStruct((columns, 2 * columns), bf16),
            jax.ShapeDtypeStruct((columns, 2 * columns), bf16),
            jax.ShapeDtypeStruct((4 * channels, 144), bf16),
            jax.ShapeDtypeStruct((6 * channels, 12 * channels), bf16),
            jax.ShapeDtypeStruct((72, 6 * channels), bf16),
        ),
        in_specs=[hbm] * 8,
        out_specs=(vmem,) * 7,
        scratch_shapes=[
            pltpu.SMEM(caipi_steps.shape, jnp.int32),
            pltpu.SMEM(band_order.shape, jnp.int32),
            pltpu.VMEM(coil_maps.shape, bf16),
            pltpu.VMEM(measured_kspace.shape, f32),
            pltpu.VMEM(factors.shape, f32),
            pltpu.VMEM(first.shape, bf16),
            pltpu.VMEM(mid.shape, bf16),
            pltpu.VMEM(last.shape, bf16),
            pltpu.VMEM((256, 4 * channels), f32),
            pltpu.VMEM((72, 6 * channels), f32),
            pltpu.SemaphoreType.DMA((7,)),
            pltpu.SemaphoreType.DMA((all_positions,)),
        ],
        compiler_params=pltpu.CompilerParams(vmem_limit_bytes=40 * 2**20),
        cost_estimate=pl.CostEstimate(
            flops=4 * 10**9, bytes_accessed=4 * 10**6, transcendentals=0
        ),
    )(
        *in_hbm(caipi_steps, band_order, coil_maps, measured_kspace),
        factors,
        *in_hbm(first, mid, last),
    )


def consistency_kernel(
    own_ref, one_ref, two_ref, three_ref, turned_ref, stacked_ref, high_ref, low_ref,
    size_ref, steps_hbm, order_hbm, mask_hbm,
    out_ref,
    steps_ref, order_ref, mask_ref, real_ref, imag_ref, field_ref, swap_ref, sum_ref,
    sems,
):
    tiles, all_positions, slices, coils, doubled, _ = turned_ref.shape
    rows, columns = doubled // 2, stacked_ref.shape[-1]
    positions = all_positions // 4
    unit = columns // 8
    pairs = (
        (steps_hbm, steps_ref), (order_hbm, order_ref), (mask_hbm, mask_ref),
    )
    copies = [pltpu.make_async_copy(src, dst, sems.at[i]) for i, (src, dst) in enumerate(pairs)]
    for copy in copies:
        copy.start()
    for copy in copies:
        copy.wait()

    def shift_of(g):
        return steps_ref[order_ref[g]] * unit

    for x, ref in enumerate((own_ref, one_ref, two_ref, three_ref)):
        for p in range(positions):
            g = lax.bitwise_xor(lax.axis_index("band"), jnp.int32(x)) * positions + p

            def store_image(j, value, g=g):
                other = halves_swapped(value)
                top = upper_half(value)
                real_ref[j, g] = jnp.where(top, value, other)
                imag_ref[j, g] = jnp.where(top, other, value)

            image = ref[p * slices : (p + 1) * slices].astype(jnp.float32)
            turned_tiles(image, shift_of(g), store_image)

    block = coils * 2 * rows
    for j in range(tiles):
        for s in range(slices):
            with_real = jnp.zeros((coils, 2 * rows, 128), jnp.float32)
            with_imag = jnp.zeros((coils, 2 * rows, 128), jnp.float32)
            for g in range(all_positions):
                coil = turned_ref[j, g, s]
                with_real += coil * real_ref[j, g, s]
                with_imag += coil * imag_ref[j, g, s]
            total = with_real + signed_swap(with_imag, -1.0, 1.0)
            field_ref[s * block : (s + 1) * block, 128 * j : 128 * (j + 1)] = total.reshape(
                block, 128
            )

    product = table_product(field_ref[...], high_ref, low_ref)
    grouped = (slices, coils, 2 * rows, columns)
    with_cos = product[:, :columns].reshape(grouped)
    with_sin = product[:, columns:].reshape(grouped)
    spectrum = with_cos + signed_swap(with_sin, 1.0, -1.0)
    keep = mask_ref[...].astype(jnp.float32).reshape(slices, 1, 1, columns)
    residual = keep * (spectrum - stacked_ref[...])
    product = table_product(residual.reshape(slices * block, columns), high_ref, low_ref)
    with_cos = product[:, :columns].reshape(grouped)
    with_sin = product[:, columns:].reshape(grouped)
    back = with_cos + signed_swap(with_sin, -1.0, 1.0)
    field_ref[...] = back.reshape(slices * block, columns)
    swap_ref[...] = halves_swapped(back).reshape(slices * block, columns)

    size = size_ref[0]
    for j in range(tiles):
        for s in range(slices):
            place = (slice(s * block, (s + 1) * block), slice(128 * j, 128 * (j + 1)))
            field = field_ref[place].reshape(coils, 2 * rows, 128)
            swapped = swap_ref[place].reshape(coils, 2 * rows, 128)
            for g in range(all_positions):
                coil = turned_ref[j, g, s]
                straight = jnp.sum(coil * field, axis=0)
                crossed = jnp.sum(coil * swapped, axis=0)
                straight = straight + halves_swapped(straight)
                crossed = halves_swapped(crossed) - crossed
                sum_ref[g, s, :, 128 * j : 128 * (j + 1)] = size * jnp.where(
                    upper_half(straight), straight, crossed
                )

    for g in range(all_positions):
        back_shift = lax.rem(columns - shift_of(g), columns)
        turned = pltpu.roll(sum_ref[g], back_shift, 2).astype(jnp.bfloat16)
        out_ref[g, :, 0] = turned[:, :rows]
        out_ref[g, :, 1] = turned[:, rows:]


def partial_consistency(images, prepared, size, sample_mask, caipi_steps, band_order):
    tiles, all_positions, slices, coils, doubled, _ = prepared[0].shape
    columns = sample_mask.shape[-1]
    total = slices * coils * doubled
    hbm = pl.BlockSpec(memory_space=pltpu.HBM)
    vmem = pl.BlockSpec(memory_space=pltpu.VMEM)
    image_shape = (tiles, all_positions, slices, doubled, 128)
    return pl.pallas_call(
        consistency_kernel,
        out_shape=jax.ShapeDtypeStruct(
            (all_positions, slices, 2, doubled // 2, columns), jnp.bfloat16
        ),
        in_specs=[vmem] * 8 + [pl.BlockSpec(memory_space=pltpu.SMEM)] + [hbm] * 3,
        out_specs=vmem,
        scratch_shapes=[
            pltpu.SMEM(caipi_steps.shape, jnp.int32),
            pltpu.SMEM(band_order.shape, jnp.int32),
            pltpu.VMEM(sample_mask.shape, jnp.int32),
            pltpu.VMEM(image_shape, jnp.float32),
            pltpu.VMEM(image_shape, jnp.float32),
            pltpu.VMEM((total, columns), jnp.float32),
            pltpu.VMEM((total, columns), jnp.float32),
            pltpu.VMEM((all_positions, slices, doubled, columns), jnp.float32),
            pltpu.SemaphoreType.DMA((3,)),
        ],
        compiler_params=pltpu.CompilerParams(vmem_limit_bytes=40 * 2**20),
        cost_estimate=pl.CostEstimate(
            flops=4 * 10**9, bytes_accessed=4 * 10**6, transcendentals=0
        ),
    )(*images, *prepared, size, *in_hbm(caipi_steps, band_order, sample_mask))


def network_kernel(
    window_ref, first_ref, wide_ref, last_ref, size_ref, image_hbm, noise_hbm,
    out_ref,
    image_ref, noise_ref, taps_ref, f1_ref, f2_ref, part_a, part_b, score_ref, sems,
):
    channels = first_ref.shape[0] // 4
    out_slices, _, rows, columns = out_ref.shape
    slices1, slices2 = out_slices + 4, out_slices + 2
    pairs = (
        (image_hbm, image_ref), (noise_hbm, noise_ref),
    )
    copies = [pltpu.make_async_copy(src, dst, sems.at[i]) for i, (src, dst) in enumerate(pairs)]
    for copy in copies:
        copy.start()

    def inside(axis, end):
        edge = lax.axis_size(axis) - 1 if end else 0
        return jnp.where(lax.axis_index(axis) == edge, 0.0, 1.0).astype(jnp.float32)

    low_slice, high_slice = inside("band", False), inside("band", True)
    low_row, high_row = inside("slab", False), inside("slab", True)
    four, two = 4 * channels, 2 * channels

    for g in range(2):
        base = window_ref[g].astype(jnp.float32)
        taps_ref[g, 0] = moved_right(base).astype(jnp.bfloat16)
        taps_ref[g, 1] = window_ref[g]
        taps_ref[g, 2] = moved_left(base).astype(jnp.bfloat16)

    def first_layer(z):
        source = jnp.concatenate(
            [
                jnp.concatenate([taps_ref[g, t, 16 * z : 16 * z + 48, :] for t in range(3)], axis=0)
                for g in range(2)
            ],
            axis=1,
        )
        half = jnp.dot(first_ref[...], source, preferred_element_type=jnp.float32)
        for r in range(8):
            begin = (r % 4) * channels
            first = columns * (r // 4)
            value = half_silu(half[begin : begin + channels, first : first + columns])
            factors = []
            if z < 2:
                factors.append(low_slice)
            if z >= slices1 - 2:
                factors.append(high_slice)
            if r < 2:
                factors.append(low_row)
            if r >= 6:
                factors.append(high_row)
            for factor in factors:
                value = value * factor
            f1_ref[z, r * channels : (r + 1) * channels, :] = value.astype(jnp.bfloat16)

    def second_product(z, pair, part_ref):
        source = jnp.concatenate(
            [
                f1_ref[z + a : z + a + 3, two * pair : two * pair + four, :].reshape(
                    3 * four, columns
                )
                for a in range(2)
            ],
            axis=1,
        )
        part_ref[...] = jnp.dot(wide_ref[...], source, preferred_element_type=jnp.float32)

    def second_layer(z, pair, part_ref):
        for a in range(2):
            first = columns * a
            for r in range(2):
                row = r * channels
                half = (
                    moved_right(part_ref[row : row + channels, first : first + columns])
                    + part_ref[two + row : two + row + channels, first : first + columns]
                    + moved_left(
                        part_ref[four + row : four + row + channels, first : first + columns]
                    )
                )
                value = half_silu(half)
                factors = []
                if z + a == 0:
                    factors.append(low_slice)
                if z + a == slices2 - 1:
                    factors.append(high_slice)
                if pair == 0 and r == 0:
                    factors.append(low_row)
                if pair == 2 and r == 1:
                    factors.append(high_row)
                for factor in factors:
                    value = value * factor
                place = two * pair + r * channels
                f2_ref[z + a, place : place + channels, :] = value.astype(jnp.bfloat16)

    def third_product(z):
        source = jnp.concatenate([f2_ref[z], f2_ref[z + 1]], axis=1)
        score_ref[z // 2] = jnp.dot(last_ref[...], source, preferred_element_type=jnp.float32)

    for z in range(4):
        first_layer(z)
    waiting = None
    parts = (part_a, part_b)
    count = 0
    for z in range(0, slices2, 2):
        for pair in range(3):
            second_product(z, pair, parts[count % 2])
            if pair < 2 and z + 4 + pair < slices1:
                first_layer(z + 4 + pair)
            if waiting is not None:
                second_layer(*waiting)
                if waiting[1] == 2:
                    third_product(waiting[0])
            waiting = (z, pair, parts[count % 2])
            count += 1
    second_layer(*waiting)
    third_product(waiting[0])

    for copy in copies:
        copy.wait()
    size = size_ref[0]
    noise_scale = jnp.sqrt(jnp.full((1, columns), 2.0 * size, jnp.float32))
    for z in range(out_slices):
        taps = []
        for t in range(3):
            total = None
            for d in range(3):
                row, first = (3 * d + t) * 8, columns * ((z + d) % 2)
                piece = score_ref[(z + d) // 2, row : row + 8, first : first + columns]
                total = piece if total is None else total + piece
            taps.append(total)
        score = size * (moved_right(taps[0]) + taps[1] + moved_left(taps[2]))
        for part in range(2):
            out_ref[z, part] = (
                image_ref[z, part]
                + score[part * rows : (part + 1) * rows]
                + noise_scale * noise_ref[z, part]
            )


def stepped_without_data(windows, weights, size, current_image, langevin_noise):
    channels = weights[0].shape[0] // 4
    slices0, columns = windows.shape[1] // 16, windows.shape[-1]
    out_slices = slices0 - 6
    local = (out_slices,) + current_image.shape[2:]
    hbm = pl.BlockSpec(memory_space=pltpu.HBM)
    vmem = pl.BlockSpec(memory_space=pltpu.VMEM)
    return pl.pallas_call(
        network_kernel,
        out_shape=jax.ShapeDtypeStruct(local, jnp.float32),
        in_specs=[vmem] * 4 + [pl.BlockSpec(memory_space=pltpu.SMEM)] + [hbm] * 2,
        out_specs=vmem,
        scratch_shapes=[
            pltpu.VMEM(local, jnp.float32),
            pltpu.VMEM(local, jnp.float32),
            pltpu.VMEM((2, 3, slices0 * 16, columns), jnp.bfloat16),
            pltpu.VMEM((out_slices + 4, 8 * channels, columns), jnp.bfloat16),
            pltpu.VMEM((out_slices + 2, 6 * channels, columns), jnp.bfloat16),
            pltpu.VMEM((6 * channels, 2 * columns), jnp.float32),
            pltpu.VMEM((6 * channels, 2 * columns), jnp.float32),
            pltpu.VMEM((out_slices // 2 + 1, 72, 2 * columns), jnp.float32),
            pltpu.SemaphoreType.DMA((2,)),
        ],
        compiler_params=pltpu.CompilerParams(vmem_limit_bytes=40 * 2**20),
        cost_estimate=pl.CostEstimate(
            flops=10**10, bytes_accessed=2 * 10**6, transcendentals=4 * 10**6
        ),
    )(
        windows,
        *weights,
        size,
        *in_hbm(current_image.reshape(local), langevin_noise.reshape(local)),
    ).reshape(current_image.shape)


def per_device(
    current_image, langevin_noise, step_size, coil_maps, measured_kspace, sample_mask,
    caipi_steps, band_order, weight_in, weight_mid, weight_out,
):
    positions, group_slices, _, row_count, columns = current_image.shape
    local_slices = positions * group_slices
    band, bands = lax.axis_index("band"), lax.axis_size("band")
    own = current_image.astype(jnp.bfloat16).reshape(local_slices, 2 * row_count, columns)
    images = [own] + [
        lax.ppermute(own, "band", [(i, i ^ x) for i in range(bands)]) for x in range(1, 4)
    ]
    turned, stacked, high, low, *weights = preparation(
        coil_maps, measured_kspace, caipi_steps, band_order, weight_in, weight_mid, weight_out
    )

    odd = band % 2 == 1
    under = jnp.where(odd, images[1], images[3])[local_slices - 3 :]
    over = jnp.where(odd, images[3], images[1])[:3]
    under = jnp.where(band == 0, jnp.zeros_like(under), under)
    over = jnp.where(band == bands - 1, jnp.zeros_like(over), over)
    tall = jnp.concatenate([under, own, over], axis=0)
    tall = tall.reshape(-1, 2, row_count, columns)
    below, above = exchanged_rows(tall, 3)
    partial_sums = partial_consistency(
        images, (turned, stacked, high, low), step_size, sample_mask, caipi_steps, band_order
    )
    partial_sums, below, above = lax.optimization_barrier((partial_sums, below, above))
    swapped = lax.all_to_all(partial_sums, "band", split_axis=0, concat_axis=0, tiled=True)
    field = jnp.concatenate([below, tall, above, jnp.zeros_like(above[:, :, :2])], axis=2)
    windows = jnp.stack(
        [field[:, :, 4 * g : 4 * g + 8].reshape(-1, columns) for g in range(2)], axis=0
    )
    base = stepped_without_data(windows, weights, step_size, current_image, langevin_noise)
    pieces = swapped.reshape((-1, positions) + swapped.shape[1:]).astype(jnp.float32)
    return base - jnp.sum(pieces, axis=0)


def solution(mesh):
    band5 = P("band", None, None, "slab", None)
    in_specs = (
        band5,
        band5,
        P(),
        P(None, None, "band", None, "slab", None),
        P(None, "band", None, "slab", None),
        P(), P(), P(), P(), P(), P(),
    )
    return jax.shard_map(
        per_device, mesh=mesh, in_specs=in_specs, out_specs=band5, check_vma=False
    )
```

```python
import functools
import math

import jax
import jax.numpy as jnp
from jax import lax
from jax.experimental import pallas as pl
from jax.experimental.pallas import tpu as pltpu
from jax.sharding import PartitionSpec as P


def exchanged_rows(tall, width):
    count = lax.axis_size("slab")
    odd = lax.axis_index("slab") % 2 == 1
    head, tail = tall[:, :, :width, :], tall[:, :, tall.shape[2] - width :, :]
    arrived = []
    for first in range(2):
        route = []
        for i in range(first, count - 1, 2):
            route += [(i, i + 1), (i + 1, i)]
        sent = jnp.where(odd, head, tail) if first == 0 else jnp.where(odd, tail, head)
        arrived.append(lax.ppermute(sent, "slab", route))
    below = jnp.where(odd, arrived[0], arrived[1])
    above = jnp.where(odd, arrived[1], arrived[0])
    return below, above


def in_hbm(*arrays):
    return [pltpu.with_memory_space_constraint(array, pltpu.HBM) for array in arrays]


def fill_factors(factors_ref):
    rows, columns = factors_ref.shape
    near = 16
    count = columns // near
    half = count + near
    row = lax.broadcasted_iota(jnp.int32, (half, columns), 0)
    row = jnp.where(row < count, near * row, row - count).astype(jnp.float32)
    phase = row * lax.broadcasted_iota(jnp.int32, (half, columns), 1).astype(jnp.float32)
    phase = phase - columns * jnp.floor(phase * (1.0 / columns))
    phase = phase * (2.0 * math.pi / columns)
    scale = 1.0 / math.sqrt(columns)
    for begin, wave in ((0, jnp.cos(phase)), (count, jnp.sin(phase))):
        factors_ref[begin : begin + count, :] = scale * wave[:count]
        begin = 2 * count + (0 if begin == 0 else near)
        factors_ref[begin : begin + near, :] = wave[count:]


def build_tables(factors_ref, high_ref, low_ref):
    columns = factors_ref.shape[1]
    near = 16
    count = columns // near
    near_cos = factors_ref[2 * count : 2 * count + near, :]
    near_sin = factors_ref[2 * count + near :, :]
    for a in range(count):
        far_cos = factors_ref[a : a + 1, :]
        far_sin = factors_ref[count + a : count + a + 1, :]
        tables = (far_cos * near_cos - far_sin * near_sin, far_sin * near_cos + far_cos * near_sin)
        rows = slice(near * a, near * (a + 1))
        for part, table in enumerate(tables):
            high = table.astype(jnp.bfloat16)
            lanes = slice(columns * part, columns * (part + 1))
            high_ref[rows, lanes] = high
            low_ref[rows, lanes] = (table - high.astype(jnp.float32)).astype(jnp.bfloat16)


def moved_right(value):
    tiles = value.shape[-1] // 128
    moved = [pltpu.roll(value[:, 128 * j : 128 * (j + 1)], 1, 1) for j in range(tiles)]
    edge = lax.broadcasted_iota(jnp.int32, moved[0].shape, 1) == 0
    return jnp.concatenate(
        [jnp.where(edge, moved[j - 1] if j > 0 else 0.0, moved[j]) for j in range(tiles)], axis=1
    )


def moved_left(value):
    tiles = value.shape[-1] // 128
    moved = [pltpu.roll(value[:, 128 * j : 128 * (j + 1)], 127, 1) for j in range(tiles)]
    edge = lax.broadcasted_iota(jnp.int32, moved[0].shape, 1) == 127
    return jnp.concatenate(
        [
            jnp.where(edge, moved[j + 1] if j < tiles - 1 else 0.0, moved[j])
            for j in range(tiles)
        ],
        axis=1,
    )


def half_silu(half):
    return half + half * jnp.tanh(half)


def table_product(source, high_ref, low_ref):
    rows = source.shape[0]
    high = source.astype(jnp.bfloat16)
    low = (source - high.astype(jnp.float32)).astype(jnp.bfloat16)
    both = jnp.dot(
        jnp.concatenate([high, low], axis=0), high_ref[...], preferred_element_type=jnp.float32
    )
    rest = jnp.dot(high, low_ref[...], preferred_element_type=jnp.float32)
    return both[:rows] + both[rows:] + rest


def halves_swapped(value):
    return pltpu.roll(value, 4, value.ndim - 2)


def upper_half(value):
    return lax.broadcasted_iota(jnp.int32, value.shape, value.ndim - 2) < 4


def signed_swap(value, top, bottom):
    sign = jnp.where(upper_half(value), top, bottom)
    return sign * halves_swapped(value)


def stacked_parts(value):
    return jnp.concatenate([value[..., 0, :, :], value[..., 1, :, :]], axis=-2)


def turned_tiles(value, shift, store):
    tiles = value.shape[-1] // 128
    whole, part = shift // 128, lax.rem(shift, 128)
    moved = [
        pltpu.roll(value[..., 128 * j : 128 * (j + 1)], part, value.ndim - 1) for j in range(tiles)
    ]
    lane = lax.broadcasted_iota(jnp.int32, moved[0].shape, value.ndim - 1)
    for j in range(tiles):
        store(lax.rem(j + whole, tiles), jnp.where(lane < part, moved[j - 1], moved[j]))


def fill_weights(first_raw, mid_raw, last_raw, first_sum, last_sum, first_ref, wide_ref, last_ref):
    channels = mid_raw.shape[-1]
    two = 2 * channels
    first_sum[...] = jnp.zeros_like(first_sum)
    last_sum[...] = jnp.zeros_like(last_sum)
    for d in range(3):
        for u in range(3):
            for t in range(3):
                block = first_raw[d, u, t].astype(jnp.float32) * 0.5
                for i in range(2):
                    for r in range(4):
                        row = (t * 3 + d) * 16 + i * 8 + u + r
                        first_sum[row : row + 1, r * channels : (r + 1) * channels] = block[
                            i : i + 1
                        ]
                block = last_raw[d, u, t].astype(jnp.float32)
                for o in range(2):
                    for r in range(4):
                        row = (d * 3 + t) * 8 + o * 4 + r
                        col = (r + u) * channels
                        last_sum[row : row + 1, col : col + channels] = block[o : o + 1]
    first_ref[...] = first_sum[...].T[:, : first_ref.shape[1]].astype(jnp.bfloat16)
    last_ref[...] = last_sum[...].astype(jnp.bfloat16)
    half_weight = jnp.bfloat16(0.5)
    for t in range(3):
        for r in range(2):
            row = (t * 2 + r) * channels
            for d in range(3):
                for pair in range(2):
                    blocks = []
                    for q in (2 * pair, 2 * pair + 1):
                        if 0 <= q - r <= 2:
                            blocks.append(mid_raw[d, q - r, t] * half_weight)
                        else:
                            blocks.append(jnp.zeros((channels, channels), jnp.bfloat16))
                    col = (d * 4 + 2 * pair) * channels
                    wide_ref[row : row + channels, col : col + two] = jnp.concatenate(
                        blocks, axis=1
                    )


def preparation_kernel(
    size_ref, steps_hbm, order_hbm, coil_hbm, kspace_hbm, first_hbm, mid_hbm, last_hbm,
    turned_ref, scalars_ref,
    stacked_out, high_out, low_out, first_out, wide_out, last_out,
    steps_ref, order_ref, coil_ref, kspace_ref, factors_ref, first_raw, mid_raw, last_raw,
    first_sum, last_sum, stacked_ref, high_ref, low_ref, first_ref, wide_ref, last_ref,
    sems, coil_sems, out_sems,
):
    all_positions, slices, coils, _, rows, columns = coil_ref.shape
    unit = columns // 8
    block = coils * 2 * rows
    pairs = (
        (first_hbm, first_raw), (mid_hbm, mid_raw), (last_hbm, last_raw),
        (steps_hbm, steps_ref), (order_hbm, order_ref), (kspace_hbm, kspace_ref),
    )
    copies = [pltpu.make_async_copy(src, dst, sems.at[i]) for i, (src, dst) in enumerate(pairs)]
    coil_copies = [
        pltpu.make_async_copy(coil_hbm.at[g], coil_ref.at[g], coil_sems.at[g])
        for g in range(all_positions)
    ]
    results = (
        (first_ref, first_out), (wide_ref, wide_out), (last_ref, last_out),
        (high_ref, high_out), (low_ref, low_out), (stacked_ref, stacked_out),
    )
    returns = [
        pltpu.make_async_copy(src, dst, out_sems.at[i]) for i, (src, dst) in enumerate(results)
    ]
    for copy in copies[:5] + coil_copies + copies[5:]:
        copy.start()
    fill_factors(factors_ref)
    build_tables(factors_ref, high_ref, low_ref)
    for copy in copies[:3]:
        copy.wait()
    fill_weights(
        first_raw, mid_raw, last_raw, first_sum, last_sum, first_ref, wide_ref, last_ref
    )
    for copy in returns[:5]:
        copy.start()
    for copy in copies[3:5]:
        copy.wait()
    for g in range(all_positions):
        shift = steps_ref[order_ref[g]] * unit
        scalars_ref[g : g + 1, :] = jnp.full((1, 128), shift, jnp.int32).astype(jnp.float32)
        coil_copies[g].wait()
        for s in range(slices):

            def store_coil(j, value, s=s, g=g):
                turned_ref[j, g, s] = value.reshape(block, 128).astype(jnp.bfloat16)

            turned_tiles(stacked_parts(coil_ref[g, s].astype(jnp.float32)), shift, store_coil)
    scalars_ref[all_positions:, :] = jnp.full(
        (scalars_ref.shape[0] - all_positions, 128), size_ref[0], jnp.float32
    )
    copies[5].wait()
    for s in range(slices):
        stacked_ref[s] = stacked_parts(kspace_ref[s])
    returns[5].start()
    for copy in returns:
        copy.wait()


def preparation(
    step_size, coil_maps, measured_kspace, caipi_steps, band_order, weight_in, weight_mid, weight_out
):
    all_positions, slices, coils, _, rows, columns = coil_maps.shape
    channels = weight_mid.shape[0]
    first = jnp.transpose(weight_in, (2, 3, 4, 1, 0))
    mid = jnp.transpose(weight_mid, (2, 3, 4, 0, 1))
    last = jnp.transpose(weight_out, (2, 3, 4, 0, 1))
    f32, bf16 = jnp.float32, jnp.bfloat16
    hbm = pl.BlockSpec(memory_space=pltpu.HBM)
    vmem = pl.BlockSpec(memory_space=pltpu.VMEM)
    results = (
        ((slices, coils, 2 * rows, columns), f32),
        ((columns, 2 * columns), bf16),
        ((columns, 2 * columns), bf16),
        ((4 * channels, 144), bf16),
        ((6 * channels, 12 * channels), bf16),
        ((72, 6 * channels), bf16),
    )
    turned_shape = (columns // 128, all_positions, slices, coils * 2 * rows, 128)
    return pl.pallas_call(
        preparation_kernel,
        out_shape=(
            jax.ShapeDtypeStruct(turned_shape, bf16),
            jax.ShapeDtypeStruct((2 * all_positions, 128), f32),
        )
        + tuple(pltpu.HBM(shape, dtype) for shape, dtype in results),
        in_specs=[pl.BlockSpec(memory_space=pltpu.SMEM)] + [hbm] * 7,
        out_specs=(vmem,) * 2 + (hbm,) * 6,
        scratch_shapes=[
            pltpu.SMEM(caipi_steps.shape, jnp.int32),
            pltpu.SMEM(band_order.shape, jnp.int32),
            pltpu.VMEM(coil_maps.shape, bf16),
            pltpu.VMEM(measured_kspace.shape, f32),
            pltpu.VMEM((2 * (columns // 16 + 16), columns), f32),
            pltpu.VMEM(first.shape, bf16),
            pltpu.VMEM(mid.shape, bf16),
            pltpu.VMEM(last.shape, bf16),
            pltpu.VMEM((256, 4 * channels), f32),
            pltpu.VMEM((72, 6 * channels), f32),
        ]
        + [pltpu.VMEM(shape, dtype) for shape, dtype in results]
        + [
            pltpu.SemaphoreType.DMA((6,)),
            pltpu.SemaphoreType.DMA((all_positions,)),
            pltpu.SemaphoreType.DMA((6,)),
        ],
        compiler_params=pltpu.CompilerParams(vmem_limit_bytes=40 * 2**20),
        cost_estimate=pl.CostEstimate(
            flops=4 * 10**9, bytes_accessed=4 * 10**6, transcendentals=0
        ),
    )(
        step_size,
        *in_hbm(caipi_steps, band_order, coil_maps, measured_kspace),
        *in_hbm(first, mid, last),
    )


def consistency_kernel(
    own_ref, one_ref, two_ref, three_ref, turned_ref, scalars_ref,
    stacked_hbm, high_hbm, low_hbm, mask_hbm,
    out_ref,
    stacked_ref, high_ref, low_ref, mask_ref, real_ref, imag_ref, field_ref, swap_ref, sum_ref,
    sems,
):
    tiles, all_positions, slices, _, _ = turned_ref.shape
    _, coils, doubled, columns = stacked_ref.shape
    rows, positions = doubled // 2, all_positions // 4
    pairs = (
        (high_hbm, high_ref), (low_hbm, low_ref), (stacked_hbm, stacked_ref), (mask_hbm, mask_ref),
    )
    copies = [pltpu.make_async_copy(src, dst, sems.at[i]) for i, (src, dst) in enumerate(pairs)]
    for copy in copies:
        copy.start()
    size = scalars_ref[all_positions : all_positions + 1, :]

    def shift_of(g):
        return jnp.max(scalars_ref[pl.ds(g, 1), :]).astype(jnp.int32)

    def coil_of(j, g, s):
        return turned_ref[j, g, s].astype(jnp.float32).reshape(coils, doubled, 128)

    for x, ref in enumerate((own_ref, one_ref, two_ref, three_ref)):
        for p in range(positions):
            g = lax.bitwise_xor(lax.axis_index("band"), jnp.int32(x)) * positions + p

            def store_image(j, value, g=g):
                other = halves_swapped(value)
                top = upper_half(value)
                real_ref[j, g] = jnp.where(top, value, other)
                imag_ref[j, g] = jnp.where(top, other, value)

            image = ref[p * slices : (p + 1) * slices].astype(jnp.float32)
            turned_tiles(image, shift_of(g), store_image)

    block = coils * 2 * rows
    for j in range(tiles):
        for s in range(slices):
            with_real = jnp.zeros((coils, 2 * rows, 128), jnp.float32)
            with_imag = jnp.zeros((coils, 2 * rows, 128), jnp.float32)
            for g in range(all_positions):
                coil = coil_of(j, g, s)
                with_real += coil * real_ref[j, g, s]
                with_imag += coil * imag_ref[j, g, s]
            total = with_real + signed_swap(with_imag, -1.0, 1.0)
            field_ref[s * block : (s + 1) * block, 128 * j : 128 * (j + 1)] = total.reshape(
                block, 128
            )

    for copy in copies:
        copy.wait()
    product = table_product(field_ref[...], high_ref, low_ref)
    grouped = (slices, coils, 2 * rows, columns)
    with_cos = product[:, :columns].reshape(grouped)
    with_sin = product[:, columns:].reshape(grouped)
    spectrum = with_cos + signed_swap(with_sin, 1.0, -1.0)
    keep = mask_ref[...].astype(jnp.float32).reshape(slices, 1, 1, columns)
    residual = keep * (spectrum - stacked_ref[...])
    product = table_product(residual.reshape(slices * block, columns), high_ref, low_ref)
    with_cos = product[:, :columns].reshape(grouped)
    with_sin = product[:, columns:].reshape(grouped)
    back = with_cos + signed_swap(with_sin, -1.0, 1.0)
    field_ref[...] = back.reshape(slices * block, columns)
    swap_ref[...] = halves_swapped(back).reshape(slices * block, columns)

    for j in range(tiles):
        for s in range(slices):
            place = (slice(s * block, (s + 1) * block), slice(128 * j, 128 * (j + 1)))
            field = field_ref[place].reshape(coils, 2 * rows, 128)
            swapped = swap_ref[place].reshape(coils, 2 * rows, 128)
            for g in range(all_positions):
                coil = coil_of(j, g, s)
                straight = jnp.sum(coil * field, axis=0)
                crossed = jnp.sum(coil * swapped, axis=0)
                straight = straight + halves_swapped(straight)
                crossed = halves_swapped(crossed) - crossed
                sum_ref[g, s, :, 128 * j : 128 * (j + 1)] = size * jnp.where(
                    upper_half(straight), straight, crossed
                )

    for g in range(all_positions):
        back_shift = lax.rem(columns - shift_of(g), columns)
        out_ref[g] = pltpu.roll(sum_ref[g], back_shift, 2).astype(jnp.bfloat16)


def partial_consistency(images, prepared, sample_mask):
    tiles, all_positions, slices, _, _ = prepared[0].shape
    _, coils, doubled, columns = prepared[2].shape
    total = slices * coils * doubled
    hbm = pl.BlockSpec(memory_space=pltpu.HBM)
    vmem = pl.BlockSpec(memory_space=pltpu.VMEM)
    image_shape = (tiles, all_positions, slices, doubled, 128)
    return pl.pallas_call(
        consistency_kernel,
        out_shape=jax.ShapeDtypeStruct((all_positions, slices, doubled, columns), jnp.bfloat16),
        in_specs=[vmem] * 6 + [hbm] * 4,
        out_specs=vmem,
        scratch_shapes=[
            pltpu.VMEM((slices, coils, doubled, columns), jnp.float32),
            pltpu.VMEM((columns, 2 * columns), jnp.bfloat16),
            pltpu.VMEM((columns, 2 * columns), jnp.bfloat16),
            pltpu.VMEM(sample_mask.shape, jnp.int32),
            pltpu.VMEM(image_shape, jnp.float32),
            pltpu.VMEM(image_shape, jnp.float32),
            pltpu.VMEM((total, columns), jnp.float32),
            pltpu.VMEM((total, columns), jnp.float32),
            pltpu.VMEM((all_positions, slices, doubled, columns), jnp.float32),
            pltpu.SemaphoreType.DMA((4,)),
        ],
        compiler_params=pltpu.CompilerParams(vmem_limit_bytes=40 * 2**20),
        cost_estimate=pl.CostEstimate(
            flops=4 * 10**9, bytes_accessed=4 * 10**6, transcendentals=0
        ),
    )(*images, *prepared[:2], *in_hbm(*prepared[2:], sample_mask))


def network_kernel(
    window_ref, scalars_ref, first_hbm, wide_hbm, last_hbm, image_hbm, noise_hbm,
    out_ref,
    first_ref, wide_ref, last_ref, image_ref, noise_ref, taps_ref, f1_ref, f2_ref, part_a, part_b, score_ref, sems,
):
    channels = first_ref.shape[0] // 4
    out_slices, _, rows, columns = out_ref.shape
    slices1, slices2 = out_slices + 4, out_slices + 2
    pairs = (
        (first_hbm, first_ref), (wide_hbm, wide_ref), (last_hbm, last_ref),
        (image_hbm, image_ref), (noise_hbm, noise_ref),
    )
    copies = [pltpu.make_async_copy(src, dst, sems.at[i]) for i, (src, dst) in enumerate(pairs)]
    for copy in copies:
        copy.start()

    def inside(axis, end):
        edge = lax.axis_size(axis) - 1 if end else 0
        return jnp.where(lax.axis_index(axis) == edge, 0.0, 1.0).astype(jnp.float32)

    low_slice, high_slice = inside("band", False), inside("band", True)
    low_row, high_row = inside("slab", False), inside("slab", True)
    four, two = 4 * channels, 2 * channels

    for g in range(2):
        base = window_ref[g].astype(jnp.float32)
        taps_ref[g, 0] = moved_right(base).astype(jnp.bfloat16)
        taps_ref[g, 1] = window_ref[g]
        taps_ref[g, 2] = moved_left(base).astype(jnp.bfloat16)

    for copy in copies[:3]:
        copy.wait()

    def first_layer(z):
        source = jnp.concatenate(
            [
                jnp.concatenate([taps_ref[g, t, 16 * z : 16 * z + 48, :] for t in range(3)], axis=0)
                for g in range(2)
            ],
            axis=1,
        )
        half = jnp.dot(first_ref[...], source, preferred_element_type=jnp.float32)
        for r in range(8):
            begin = (r % 4) * channels
            first = columns * (r // 4)
            value = half_silu(half[begin : begin + channels, first : first + columns])
            factors = []
            if z < 2:
                factors.append(low_slice)
            if z >= slices1 - 2:
                factors.append(high_slice)
            if r < 2:
                factors.append(low_row)
            if r >= 6:
                factors.append(high_row)
            for factor in factors:
                value = value * factor
            f1_ref[z, r * channels : (r + 1) * channels, :] = value.astype(jnp.bfloat16)

    def second_product(z, pair, part_ref):
        source = jnp.concatenate(
            [
                f1_ref[z + a : z + a + 3, two * pair : two * pair + four, :].reshape(
                    3 * four, columns
                )
                for a in range(2)
            ],
            axis=1,
        )
        part_ref[...] = jnp.dot(wide_ref[...], source, preferred_element_type=jnp.float32)

    def second_layer(z, pair, part_ref):
        for a in range(2):
            first = columns * a
            for r in range(2):
                row = r * channels
                half = (
                    moved_right(part_ref[row : row + channels, first : first + columns])
                    + part_ref[two + row : two + row + channels, first : first + columns]
                    + moved_left(
                        part_ref[four + row : four + row + channels, first : first + columns]
                    )
                )
                value = half_silu(half)
                factors = []
                if z + a == 0:
                    factors.append(low_slice)
                if z + a == slices2 - 1:
                    factors.append(high_slice)
                if pair == 0 and r == 0:
                    factors.append(low_row)
                if pair == 2 and r == 1:
                    factors.append(high_row)
                for factor in factors:
                    value = value * factor
                place = two * pair + r * channels
                f2_ref[z + a, place : place + channels, :] = value.astype(jnp.bfloat16)

    def third_product(z):
        source = jnp.concatenate([f2_ref[z], f2_ref[z + 1]], axis=1)
        score_ref[z // 2] = jnp.dot(last_ref[...], source, preferred_element_type=jnp.float32)

    for z in range(4):
        first_layer(z)
    waiting = None
    parts = (part_a, part_b)
    count = 0
    for z in range(0, slices2, 2):
        for pair in range(3):
            second_product(z, pair, parts[count % 2])
            if pair < 2 and z + 4 + pair < slices1:
                first_layer(z + 4 + pair)
            if waiting is not None:
                second_layer(*waiting)
                if waiting[1] == 2:
                    third_product(waiting[0])
            waiting = (z, pair, parts[count % 2])
            count += 1
    second_layer(*waiting)
    third_product(waiting[0])

    for copy in copies[3:]:
        copy.wait()
    size = scalars_ref[scalars_ref.shape[0] - 1 :, :]
    size = jnp.concatenate([size] * (columns // 128), axis=1)
    noise_scale = jnp.sqrt(2.0 * size)
    for z in range(out_slices):
        taps = []
        for t in range(3):
            total = None
            for d in range(3):
                row, first = (3 * d + t) * 8, columns * ((z + d) % 2)
                piece = score_ref[(z + d) // 2, row : row + 8, first : first + columns]
                total = piece if total is None else total + piece
            taps.append(total)
        score = size * (moved_right(taps[0]) + taps[1] + moved_left(taps[2]))
        for part in range(2):
            out_ref[z, part] = (
                image_ref[z, part]
                + score[part * rows : (part + 1) * rows]
                + noise_scale * noise_ref[z, part]
            )


def stepped_without_data(windows, scalars, weights, current_image, langevin_noise):
    channels = weights[0].shape[0] // 4
    slices0, columns = windows.shape[1] // 16, windows.shape[-1]
    out_slices = slices0 - 6
    local = (out_slices,) + current_image.shape[2:]
    hbm = pl.BlockSpec(memory_space=pltpu.HBM)
    vmem = pl.BlockSpec(memory_space=pltpu.VMEM)
    return pl.pallas_call(
        network_kernel,
        out_shape=jax.ShapeDtypeStruct(local, jnp.float32),
        in_specs=[vmem] * 2 + [hbm] * 5,
        out_specs=vmem,
        scratch_shapes=[pltpu.VMEM(weight.shape, weight.dtype) for weight in weights]
        + [
            pltpu.VMEM(local, jnp.float32),
            pltpu.VMEM(local, jnp.float32),
            pltpu.VMEM((2, 3, slices0 * 16, columns), jnp.bfloat16),
            pltpu.VMEM((out_slices + 4, 8 * channels, columns), jnp.bfloat16),
            pltpu.VMEM((out_slices + 2, 6 * channels, columns), jnp.bfloat16),
            pltpu.VMEM((6 * channels, 2 * columns), jnp.float32),
            pltpu.VMEM((6 * channels, 2 * columns), jnp.float32),
            pltpu.VMEM((out_slices // 2 + 1, 72, 2 * columns), jnp.float32),
            pltpu.SemaphoreType.DMA((5,)),
        ],
        compiler_params=pltpu.CompilerParams(vmem_limit_bytes=40 * 2**20),
        cost_estimate=pl.CostEstimate(
            flops=10**10, bytes_accessed=2 * 10**6, transcendentals=4 * 10**6
        ),
    )(
        windows, scalars,
        *in_hbm(*weights, current_image.reshape(local), langevin_noise.reshape(local)),
    ).reshape(current_image.shape)


def per_device(
    current_image, langevin_noise, step_size, coil_maps, measured_kspace, sample_mask,
    caipi_steps, band_order, weight_in, weight_mid, weight_out,
):
    positions, group_slices, _, row_count, columns = current_image.shape
    local_slices = positions * group_slices
    band, bands = lax.axis_index("band"), lax.axis_size("band")
    own = current_image.astype(jnp.bfloat16).reshape(local_slices, 2 * row_count, columns)
    images = [own] + [
        lax.ppermute(own, "band", [(i, i ^ x) for i in range(bands)]) for x in range(1, 4)
    ]
    turned, scalars, stacked, high, low, *weights = preparation(
        step_size, coil_maps, measured_kspace, caipi_steps, band_order,
        weight_in, weight_mid, weight_out,
    )

    odd = band % 2 == 1
    under = jnp.where(odd, images[1], images[3])[local_slices - 3 :]
    over = jnp.where(odd, images[3], images[1])[:3]
    under = jnp.where(band == 0, jnp.zeros_like(under), under)
    over = jnp.where(band == bands - 1, jnp.zeros_like(over), over)
    tall = jnp.concatenate([under, own, over], axis=0)
    tall = tall.reshape(-1, 2, row_count, columns)
    below, above = exchanged_rows(tall, 3)
    partial_sums = partial_consistency(
        images, (turned, scalars, stacked, high, low), sample_mask
    )
    partial_sums, below, above = lax.optimization_barrier((partial_sums, below, above))
    swapped = lax.all_to_all(partial_sums, "band", split_axis=0, concat_axis=0, tiled=True)
    field = jnp.concatenate([below, tall, above, jnp.zeros_like(above[:, :, :2])], axis=2)
    windows = jnp.stack(
        [field[:, :, 4 * g : 4 * g + 8].reshape(-1, columns) for g in range(2)], axis=0
    )
    base = stepped_without_data(windows, scalars, weights, current_image, langevin_noise)
    pieces = swapped.reshape((-1, positions) + swapped.shape[1:]).astype(jnp.float32)
    return base - jnp.sum(pieces, axis=0).reshape(base.shape)


def solution(mesh):
    band5 = P("band", None, None, "slab", None)
    in_specs = (
        band5,
        band5,
        P(),
        P(None, None, "band", None, "slab", None),
        P(None, "band", None, "slab", None),
        P(), P(), P(), P(), P(), P(),
    )
    return jax.shard_map(
        per_device, mesh=mesh, in_specs=in_specs, out_specs=band5, check_vma=False
    )
```

```python
import functools
import math

import jax
import jax.numpy as jnp
from jax import lax
from jax.experimental import pallas as pl
from jax.experimental.pallas import tpu as pltpu
from jax.sharding import PartitionSpec as P


def exchanged_rows(tall, width):
    count = lax.axis_size("slab")
    odd = lax.axis_index("slab") % 2 == 1
    head, tail = tall[:, :, :width, :], tall[:, :, tall.shape[2] - width :, :]
    arrived = []
    for first in range(2):
        route = []
        for i in range(first, count - 1, 2):
            route += [(i, i + 1), (i + 1, i)]
        sent = jnp.where(odd, head, tail) if first == 0 else jnp.where(odd, tail, head)
        arrived.append(lax.ppermute(sent, "slab", route))
    below = jnp.where(odd, arrived[0], arrived[1])
    above = jnp.where(odd, arrived[1], arrived[0])
    return below, above


def in_hbm(*arrays):
    return [pltpu.with_memory_space_constraint(array, pltpu.HBM) for array in arrays]


def series(square, coefficients):
    total = jnp.full_like(square, coefficients[-1])
    for coefficient in coefficients[-2::-1]:
        total = total * square + coefficient
    return total


def fill_factors(factors_ref):
    rows, columns = factors_ref.shape
    near = 16
    count = columns // near
    half = count + near
    row = lax.broadcasted_iota(jnp.int32, (half, columns), 0)
    row = jnp.where(row < count, near * row, row - count).astype(jnp.float32)
    phase = row * lax.broadcasted_iota(jnp.int32, (half, columns), 1).astype(jnp.float32)
    phase = phase - columns * jnp.floor(phase * (1.0 / columns) + 0.5)
    angle = phase * (math.pi / columns)
    square = angle * angle
    sine = angle * series(square, [(-1.0) ** k / math.factorial(2 * k + 1) for k in range(7)])
    cosine = series(square, [(-1.0) ** k / math.factorial(2 * k) for k in range(8)])
    scale = 1.0 / math.sqrt(columns)
    waves = (1.0 - 2.0 * sine * sine, 2.0 * sine * cosine)
    for part, wave in enumerate(waves):
        begin = count * part
        factors_ref[begin : begin + count, :] = scale * wave[:count]
        begin = 2 * count + near * part
        factors_ref[begin : begin + near, :] = wave[count:]


def build_tables(factors_ref, high_ref, low_ref):
    columns = factors_ref.shape[1]
    near = 16
    count = columns // near
    near_cos = factors_ref[2 * count : 2 * count + near, :]
    near_sin = factors_ref[2 * count + near :, :]
    for a in range(count):
        far_cos = factors_ref[a : a + 1, :]
        far_sin = factors_ref[count + a : count + a + 1, :]
        tables = (far_cos * near_cos - far_sin * near_sin, far_sin * near_cos + far_cos * near_sin)
        rows = slice(near * a, near * (a + 1))
        for part, table in enumerate(tables):
            high = table.astype(jnp.bfloat16)
            lanes = slice(columns * part, columns * (part + 1))
            high_ref[rows, lanes] = high
            low_ref[rows, lanes] = (table - high.astype(jnp.float32)).astype(jnp.bfloat16)


def moved_right(value):
    tiles = value.shape[-1] // 128
    moved = [pltpu.roll(value[:, 128 * j : 128 * (j + 1)], 1, 1) for j in range(tiles)]
    edge = lax.broadcasted_iota(jnp.int32, moved[0].shape, 1) == 0
    return jnp.concatenate(
        [jnp.where(edge, moved[j - 1] if j > 0 else 0.0, moved[j]) for j in range(tiles)], axis=1
    )


def moved_left(value):
    tiles = value.shape[-1] // 128
    moved = [pltpu.roll(value[:, 128 * j : 128 * (j + 1)], 127, 1) for j in range(tiles)]
    edge = lax.broadcasted_iota(jnp.int32, moved[0].shape, 1) == 127
    return jnp.concatenate(
        [
            jnp.where(edge, moved[j + 1] if j < tiles - 1 else 0.0, moved[j])
            for j in range(tiles)
        ],
        axis=1,
    )


def half_silu(half):
    return half + half * jnp.tanh(half)


def table_product(source, high_ref, low_ref):
    rows = source.shape[0]
    high = source.astype(jnp.bfloat16)
    low = (source - high.astype(jnp.float32)).astype(jnp.bfloat16)
    both = jnp.dot(
        jnp.concatenate([high, low], axis=0), high_ref[...], preferred_element_type=jnp.float32
    )
    rest = jnp.dot(high, low_ref[...], preferred_element_type=jnp.float32)
    return both[:rows] + both[rows:] + rest


def halves_swapped(value):
    return pltpu.roll(value, 4, value.ndim - 2)


def upper_half(value):
    return lax.broadcasted_iota(jnp.int32, value.shape, value.ndim - 2) < 4


def signed_swap(value, top, bottom):
    sign = jnp.where(upper_half(value), top, bottom)
    return sign * halves_swapped(value)


def stacked_parts(value):
    return jnp.concatenate([value[..., 0, :, :], value[..., 1, :, :]], axis=-2)


def turned_tiles(value, shift, store):
    tiles = value.shape[-1] // 128
    whole, part = shift // 128, lax.rem(shift, 128)
    moved = [
        pltpu.roll(value[..., 128 * j : 128 * (j + 1)], part, value.ndim - 1) for j in range(tiles)
    ]
    lane = lax.broadcasted_iota(jnp.int32, moved[0].shape, value.ndim - 1)
    for j in range(tiles):
        store(lax.rem(j + whole, tiles), jnp.where(lane < part, moved[j - 1], moved[j]))


def fill_weights(first_raw, mid_raw, last_raw, first_sum, last_sum, first_ref, wide_ref, last_ref):
    channels = mid_raw.shape[-1]
    two = 2 * channels
    first_sum[...] = jnp.zeros_like(first_sum)
    last_sum[...] = jnp.zeros_like(last_sum)
    for d in range(3):
        for u in range(3):
            for t in range(3):
                block = first_raw[d, u, t].astype(jnp.float32) * 0.5
                for i in range(2):
                    for r in range(4):
                        row = (t * 3 + d) * 16 + i * 8 + u + r
                        first_sum[row : row + 1, r * channels : (r + 1) * channels] = block[
                            i : i + 1
                        ]
                block = last_raw[d, u, t].astype(jnp.float32)
                for o in range(2):
                    for r in range(4):
                        row = (d * 3 + t) * 8 + o * 4 + r
                        col = (r + u) * channels
                        last_sum[row : row + 1, col : col + channels] = block[o : o + 1]
    first_ref[...] = first_sum[...].T[:, : first_ref.shape[1]].astype(jnp.bfloat16)
    last_ref[...] = last_sum[...].astype(jnp.bfloat16)
    half_weight = jnp.bfloat16(0.5)
    for t in range(3):
        for r in range(2):
            row = (t * 2 + r) * channels
            for d in range(3):
                for pair in range(2):
                    blocks = []
                    for q in (2 * pair, 2 * pair + 1):
                        if 0 <= q - r <= 2:
                            blocks.append(mid_raw[d, q - r, t] * half_weight)
                        else:
                            blocks.append(jnp.zeros((channels, channels), jnp.bfloat16))
                    col = (d * 4 + 2 * pair) * channels
                    wide_ref[row : row + channels, col : col + two] = jnp.concatenate(
                        blocks, axis=1
                    )


def preparation_kernel(
    size_ref, steps_hbm, order_hbm, coil_hbm,
    turned_ref, scalars_ref, high_ref, low_ref,
    steps_ref, order_ref, coil_ref, factors_ref, sems, coil_sems,
):
    all_positions, slices, coils, _, rows, columns = coil_ref.shape
    unit = columns // 8
    block = coils * 2 * rows
    copies = [
        pltpu.make_async_copy(steps_hbm, steps_ref, sems.at[0]),
        pltpu.make_async_copy(order_hbm, order_ref, sems.at[1]),
    ] + [
        pltpu.make_async_copy(coil_hbm.at[g], coil_ref.at[g], coil_sems.at[g])
        for g in range(all_positions)
    ]
    for copy in copies:
        copy.start()
    fill_factors(factors_ref)
    build_tables(factors_ref, high_ref, low_ref)
    scalars_ref[all_positions:, :] = jnp.full(
        (scalars_ref.shape[0] - all_positions, 128), size_ref[0], jnp.float32
    )
    for copy in copies:
        copy.wait()
    for g in range(all_positions):
        shift = steps_ref[order_ref[g]] * unit
        scalars_ref[g : g + 1, :] = jnp.full((1, 128), shift, jnp.int32).astype(jnp.float32)
        for s in range(slices):

            def store_coil(j, value, s=s, g=g):
                turned_ref[j, g, s] = value.reshape(block, 128).astype(jnp.bfloat16)

            turned_tiles(stacked_parts(coil_ref[g, s].astype(jnp.float32)), shift, store_coil)


def preparation(step_size, coil_maps, caipi_steps, band_order):
    all_positions, slices, coils, _, rows, columns = coil_maps.shape
    f32, bf16 = jnp.float32, jnp.bfloat16
    hbm = pl.BlockSpec(memory_space=pltpu.HBM)
    vmem = pl.BlockSpec(memory_space=pltpu.VMEM)
    turned_shape = (columns // 128, all_positions, slices, coils * 2 * rows, 128)
    return pl.pallas_call(
        preparation_kernel,
        out_shape=(
            jax.ShapeDtypeStruct(turned_shape, bf16),
            jax.ShapeDtypeStruct((2 * all_positions, 128), f32),
            jax.ShapeDtypeStruct((columns, 2 * columns), bf16),
            jax.ShapeDtypeStruct((columns, 2 * columns), bf16),
        ),
        in_specs=[pl.BlockSpec(memory_space=pltpu.SMEM)] + [hbm] * 3,
        out_specs=(vmem,) * 4,
        scratch_shapes=[
            pltpu.SMEM(caipi_steps.shape, jnp.int32),
            pltpu.SMEM(band_order.shape, jnp.int32),
            pltpu.VMEM(coil_maps.shape, bf16),
            pltpu.VMEM((2 * (columns // 16 + 16), columns), f32),
            pltpu.SemaphoreType.DMA((2,)),
            pltpu.SemaphoreType.DMA((all_positions,)),
        ],
        compiler_params=pltpu.CompilerParams(vmem_limit_bytes=40 * 2**20),
        cost_estimate=pl.CostEstimate(
            flops=4 * 10**9, bytes_accessed=4 * 10**6, transcendentals=0
        ),
    )(step_size, *in_hbm(caipi_steps, band_order, coil_maps))


def consistency_kernel(
    own_ref, one_ref, two_ref, three_ref, turned_ref, scalars_ref, high_ref, low_ref,
    kspace_hbm, mask_hbm,
    own_out, one_out, two_out, three_out,
    kspace_ref, mask_ref, real_ref, imag_ref, field_ref, swap_ref, sum_ref, sems,
):
    tiles, all_positions, slices, _, _ = turned_ref.shape
    _, coils, _, rows, columns = kspace_ref.shape
    doubled, positions = 2 * rows, all_positions // 4
    copies = [
        pltpu.make_async_copy(kspace_hbm, kspace_ref, sems.at[0]),
        pltpu.make_async_copy(mask_hbm, mask_ref, sems.at[1]),
    ]
    for copy in copies:
        copy.start()
    size = scalars_ref[all_positions : all_positions + 1, :]
    owners = []
    for x in range(4):
        first = lax.bitwise_xor(lax.axis_index("band"), jnp.int32(x)) * positions
        for p in range(positions):
            shift = jnp.max(scalars_ref[pl.ds(first + p, 1), :]).astype(jnp.int32)
            owners.append((x, p, first + p, shift))

    def coil_of(j, g, s):
        return turned_ref[j, g, s].astype(jnp.float32).reshape(coils, doubled, 128)

    images = (own_ref, one_ref, two_ref, three_ref)
    for k, (x, p, g, shift) in enumerate(owners):

        def store_image(j, value, k=k):
            other = halves_swapped(value)
            top = upper_half(value)
            real_ref[j, k] = jnp.where(top, value, other)
            imag_ref[j, k] = jnp.where(top, other, value)

        image = images[x][p * slices : (p + 1) * slices].astype(jnp.float32)
        turned_tiles(image, shift, store_image)
    for copy in copies:
        copy.wait()

    block = coils * doubled
    halves = [range(0, slices // 2), range(slices // 2, slices)]

    def rows_of(half):
        return slice(half[0] * block, (half[-1] + 1) * block)

    def collapse(half):
        for j in range(tiles):
            for s in half:
                with_real = jnp.zeros((coils, doubled, 128), jnp.float32)
                with_imag = jnp.zeros((coils, doubled, 128), jnp.float32)
                for k, (_, _, g, _) in enumerate(owners):
                    coil = coil_of(j, g, s)
                    with_real += coil * real_ref[j, k, s]
                    with_imag += coil * imag_ref[j, k, s]
                total = with_real + signed_swap(with_imag, -1.0, 1.0)
                field_ref[s * block : (s + 1) * block, 128 * j : 128 * (j + 1)] = total.reshape(
                    block, 128
                )

    def transformed(source, half, top, bottom):
        product = table_product(source, high_ref, low_ref)
        grouped = (len(half), coils, doubled, columns)
        with_cos = product[:, :columns].reshape(grouped)
        with_sin = product[:, columns:].reshape(grouped)
        return with_cos + signed_swap(with_sin, top, bottom)

    def project(half):
        spectrum = transformed(field_ref[rows_of(half)], half, 1.0, -1.0)
        keep = mask_ref[...].astype(jnp.float32)[half[0] : half[-1] + 1]
        keep = keep.reshape(len(half), 1, 1, columns)
        data = stacked_parts(kspace_ref[half[0] : half[-1] + 1])
        residual = (keep * (spectrum - data)).reshape(len(half) * block, columns)
        back = transformed(residual, half, -1.0, 1.0)
        field_ref[rows_of(half)] = back.reshape(len(half) * block, columns)
        swap_ref[rows_of(half)] = halves_swapped(back).reshape(len(half) * block, columns)

    def combine(half):
        for j in range(tiles):
            for s in half:
                place = (slice(s * block, (s + 1) * block), slice(128 * j, 128 * (j + 1)))
                field = field_ref[place].reshape(coils, doubled, 128)
                swapped = swap_ref[place].reshape(coils, doubled, 128)
                for k, (_, _, g, _) in enumerate(owners):
                    coil = coil_of(j, g, s)
                    straight = jnp.sum(coil * field, axis=0)
                    crossed = jnp.sum(coil * swapped, axis=0)
                    straight = straight + halves_swapped(straight)
                    crossed = halves_swapped(crossed) - crossed
                    sum_ref[k, s, :, 128 * j : 128 * (j + 1)] = size * jnp.where(
                        upper_half(straight), straight, crossed
                    )

    for half in halves:
        collapse(half)
    for half in halves:
        project(half)
    for half in halves:
        combine(half)

    outs = (own_out, one_out, two_out, three_out)
    for k, (x, p, _, shift) in enumerate(owners):
        back_shift = lax.rem(columns - shift, columns)
        outs[x][p] = pltpu.roll(sum_ref[k], back_shift, 2).astype(jnp.bfloat16)


def partial_consistency(images, prepared, measured_kspace, sample_mask):
    tiles, all_positions, slices, _, _ = prepared[0].shape
    _, coils, _, rows, columns = measured_kspace.shape
    doubled = 2 * rows
    total = slices * coils * doubled
    hbm = pl.BlockSpec(memory_space=pltpu.HBM)
    vmem = pl.BlockSpec(memory_space=pltpu.VMEM)
    image_shape = (tiles, all_positions, slices, doubled, 128)
    part = jax.ShapeDtypeStruct((all_positions // 4, slices, doubled, columns), jnp.bfloat16)
    return pl.pallas_call(
        consistency_kernel,
        out_shape=(part,) * 4,
        in_specs=[vmem] * 8 + [hbm] * 2,
        out_specs=(vmem,) * 4,
        scratch_shapes=[
            pltpu.VMEM(measured_kspace.shape, jnp.float32),
            pltpu.VMEM(sample_mask.shape, jnp.int32),
            pltpu.VMEM(image_shape, jnp.float32),
            pltpu.VMEM(image_shape, jnp.float32),
            pltpu.VMEM((total, columns), jnp.float32),
            pltpu.VMEM((total, columns), jnp.float32),
            pltpu.VMEM((all_positions, slices, doubled, columns), jnp.float32),
            pltpu.SemaphoreType.DMA((2,)),
        ],
        compiler_params=pltpu.CompilerParams(vmem_limit_bytes=40 * 2**20),
        cost_estimate=pl.CostEstimate(
            flops=4 * 10**9, bytes_accessed=4 * 10**6, transcendentals=0
        ),
    )(*images, *prepared, *in_hbm(measured_kspace, sample_mask))


def network_kernel(
    window_ref, scalars_ref, first_hbm, mid_hbm, last_hbm, image_hbm, noise_hbm,
    out_ref,
    first_raw, mid_raw, last_raw, image_ref, noise_ref,
    first_sum, last_sum, first_ref, wide_ref, last_ref, taps_ref, f1_ref, f2_ref, part_a, part_b, score_ref, sems,
):
    channels = mid_raw.shape[-1]
    out_slices, _, rows, columns = out_ref.shape
    slices1, slices2 = out_slices + 4, out_slices + 2
    pairs = (
        (first_hbm, first_raw), (mid_hbm, mid_raw), (last_hbm, last_raw),
        (image_hbm, image_ref), (noise_hbm, noise_ref),
    )
    copies = [pltpu.make_async_copy(src, dst, sems.at[i]) for i, (src, dst) in enumerate(pairs)]
    for copy in copies:
        copy.start()

    def inside(axis, end):
        edge = lax.axis_size(axis) - 1 if end else 0
        return jnp.where(lax.axis_index(axis) == edge, 0.0, 1.0).astype(jnp.float32)

    low_slice, high_slice = inside("band", False), inside("band", True)
    low_row, high_row = inside("slab", False), inside("slab", True)
    four, two = 4 * channels, 2 * channels

    for g in range(2):
        base = window_ref[g].astype(jnp.float32)
        taps_ref[g, 0] = moved_right(base).astype(jnp.bfloat16)
        taps_ref[g, 1] = window_ref[g]
        taps_ref[g, 2] = moved_left(base).astype(jnp.bfloat16)

    for copy in copies[:3]:
        copy.wait()
    fill_weights(
        first_raw, mid_raw, last_raw, first_sum, last_sum, first_ref, wide_ref, last_ref
    )

    def first_layer(z):
        source = jnp.concatenate(
            [
                jnp.concatenate([taps_ref[g, t, 16 * z : 16 * z + 48, :] for t in range(3)], axis=0)
                for g in range(2)
            ],
            axis=1,
        )
        half = jnp.dot(first_ref[...], source, preferred_element_type=jnp.float32)
        for r in range(8):
            begin = (r % 4) * channels
            first = columns * (r // 4)
            value = half_silu(half[begin : begin + channels, first : first + columns])
            factors = []
            if z < 2:
                factors.append(low_slice)
            if z >= slices1 - 2:
                factors.append(high_slice)
            if r < 2:
                factors.append(low_row)
            if r >= 6:
                factors.append(high_row)
            for factor in factors:
                value = value * factor
            f1_ref[z, r * channels : (r + 1) * channels, :] = value.astype(jnp.bfloat16)

    def second_product(z, pair, part_ref):
        source = jnp.concatenate(
            [
                f1_ref[z + a : z + a + 3, two * pair : two * pair + four, :].reshape(
                    3 * four, columns
                )
                for a in range(2)
            ],
            axis=1,
        )
        part_ref[...] = jnp.dot(wide_ref[...], source, preferred_element_type=jnp.float32)

    def second_layer(z, pair, part_ref):
        for a in range(2):
            first = columns * a
            for r in range(2):
                row = r * channels
                half = (
                    moved_right(part_ref[row : row + channels, first : first + columns])
                    + part_ref[two + row : two + row + channels, first : first + columns]
                    + moved_left(
                        part_ref[four + row : four + row + channels, first : first + columns]
                    )
                )
                value = half_silu(half)
                factors = []
                if z + a == 0:
                    factors.append(low_slice)
                if z + a == slices2 - 1:
                    factors.append(high_slice)
                if pair == 0 and r == 0:
                    factors.append(low_row)
                if pair == 2 and r == 1:
                    factors.append(high_row)
                for factor in factors:
                    value = value * factor
                place = two * pair + r * channels
                f2_ref[z + a, place : place + channels, :] = value.astype(jnp.bfloat16)

    def third_product(z):
        source = jnp.concatenate([f2_ref[z], f2_ref[z + 1]], axis=1)
        score_ref[z // 2] = jnp.dot(last_ref[...], source, preferred_element_type=jnp.float32)

    for z in range(4):
        first_layer(z)
    waiting = None
    parts = (part_a, part_b)
    count = 0
    for z in range(0, slices2, 2):
        for pair in range(3):
            second_product(z, pair, parts[count % 2])
            if pair < 2 and z + 4 + pair < slices1:
                first_layer(z + 4 + pair)
            if waiting is not None:
                second_layer(*waiting)
                if waiting[1] == 2:
                    third_product(waiting[0])
            waiting = (z, pair, parts[count % 2])
            count += 1
    second_layer(*waiting)
    third_product(waiting[0])

    for copy in copies[3:]:
        copy.wait()
    size = scalars_ref[scalars_ref.shape[0] - 1 :, :]
    size = jnp.concatenate([size] * (columns // 128), axis=1)
    noise_scale = jnp.sqrt(2.0 * size)
    for z in range(out_slices):
        taps = []
        for t in range(3):
            total = None
            for d in range(3):
                row, first = (3 * d + t) * 8, columns * ((z + d) % 2)
                piece = score_ref[(z + d) // 2, row : row + 8, first : first + columns]
                total = piece if total is None else total + piece
            taps.append(total)
        score = size * (moved_right(taps[0]) + taps[1] + moved_left(taps[2]))
        for part in range(2):
            out_ref[z, part] = (
                image_ref[z, part]
                + score[part * rows : (part + 1) * rows]
                + noise_scale * noise_ref[z, part]
            )


def stepped_without_data(
    windows, scalars, current_image, langevin_noise, weight_in, weight_mid, weight_out
):
    channels = weight_mid.shape[0]
    first = jnp.transpose(weight_in, (2, 3, 4, 1, 0))
    mid = jnp.transpose(weight_mid, (2, 3, 4, 0, 1))
    last = jnp.transpose(weight_out, (2, 3, 4, 0, 1))
    slices0, columns = windows.shape[1] // 16, windows.shape[-1]
    out_slices = slices0 - 6
    local = (out_slices,) + current_image.shape[2:]
    hbm = pl.BlockSpec(memory_space=pltpu.HBM)
    vmem = pl.BlockSpec(memory_space=pltpu.VMEM)
    return pl.pallas_call(
        network_kernel,
        out_shape=jax.ShapeDtypeStruct(local, jnp.float32),
        in_specs=[vmem] * 2 + [hbm] * 5,
        out_specs=vmem,
        scratch_shapes=[
            pltpu.VMEM(first.shape, jnp.bfloat16),
            pltpu.VMEM(mid.shape, jnp.bfloat16),
            pltpu.VMEM(last.shape, jnp.bfloat16),
            pltpu.VMEM(local, jnp.float32),
            pltpu.VMEM(local, jnp.float32),
            pltpu.VMEM((256, 4 * channels), jnp.float32),
            pltpu.VMEM((72, 6 * channels), jnp.float32),
            pltpu.VMEM((4 * channels, 144), jnp.bfloat16),
            pltpu.VMEM((6 * channels, 12 * channels), jnp.bfloat16),
            pltpu.VMEM((72, 6 * channels), jnp.bfloat16),
            pltpu.VMEM((2, 3, slices0 * 16, columns), jnp.bfloat16),
            pltpu.VMEM((out_slices + 4, 8 * channels, columns), jnp.bfloat16),
            pltpu.VMEM((out_slices + 2, 6 * channels, columns), jnp.bfloat16),
            pltpu.VMEM((6 * channels, 2 * columns), jnp.float32),
            pltpu.VMEM((6 * channels, 2 * columns), jnp.float32),
            pltpu.VMEM((out_slices // 2 + 1, 72, 2 * columns), jnp.float32),
            pltpu.SemaphoreType.DMA((5,)),
        ],
        compiler_params=pltpu.CompilerParams(vmem_limit_bytes=40 * 2**20),
        cost_estimate=pl.CostEstimate(
            flops=10**10, bytes_accessed=2 * 10**6, transcendentals=4 * 10**6
        ),
    )(
        windows, scalars,
        *in_hbm(first, mid, last, current_image.reshape(local), langevin_noise.reshape(local)),
    ).reshape(current_image.shape)


def per_device(
    current_image, langevin_noise, step_size, coil_maps, measured_kspace, sample_mask,
    caipi_steps, band_order, weight_in, weight_mid, weight_out,
):
    positions, group_slices, _, row_count, columns = current_image.shape
    local_slices = positions * group_slices
    band, bands = lax.axis_index("band"), lax.axis_size("band")
    own = current_image.astype(jnp.bfloat16).reshape(local_slices, 2 * row_count, columns)
    routes = [[(i, i ^ x) for i in range(bands)] for x in range(1, 4)]
    images = [own] + [lax.ppermute(own, "band", route) for route in routes]
    prepared = preparation(step_size, coil_maps, caipi_steps, band_order)

    odd = band % 2 == 1
    under = jnp.where(odd, images[1], images[3])[local_slices - 3 :]
    over = jnp.where(odd, images[3], images[1])[:3]
    under = jnp.where(band == 0, jnp.zeros_like(under), under)
    over = jnp.where(band == bands - 1, jnp.zeros_like(over), over)
    tall = jnp.concatenate([under, own, over], axis=0)
    tall = tall.reshape(-1, 2, row_count, columns)
    below, above = exchanged_rows(tall, 3)
    sums = partial_consistency(images, prepared, measured_kspace, sample_mask)
    sums, below, above = lax.optimization_barrier((sums, below, above))
    arrived = [lax.ppermute(part, "band", route) for part, route in zip(sums[1:], routes)]
    field = jnp.concatenate([below, tall, above, jnp.zeros_like(above[:, :, :2])], axis=2)
    windows = jnp.stack(
        [field[:, :, 4 * g : 4 * g + 8].reshape(-1, columns) for g in range(2)], axis=0
    )
    base = stepped_without_data(
        windows, prepared[1], current_image, langevin_noise, weight_in, weight_mid, weight_out
    )
    total = sums[0].astype(jnp.float32)
    for part in arrived:
        total = total + part.astype(jnp.float32)
    return base - total.reshape(base.shape)


def solution(mesh):
    band5 = P("band", None, None, "slab", None)
    in_specs = (
        band5,
        band5,
        P(),
        P(None, None, "band", None, "slab", None),
        P(None, "band", None, "slab", None),
        P(), P(), P(), P(), P(), P(),
    )
    return jax.shard_map(
        per_device, mesh=mesh, in_specs=in_specs, out_specs=band5, check_vma=False
    )
```

```python
import functools
import math

import jax
import jax.numpy as jnp
from jax import lax
from jax.experimental import pallas as pl
from jax.experimental.pallas import tpu as pltpu
from jax.sharding import PartitionSpec as P


def exchanged_rows(tall, width):
    count = lax.axis_size("slab")
    odd = lax.axis_index("slab") % 2 == 1
    head, tail = tall[:, :, :width, :], tall[:, :, tall.shape[2] - width :, :]
    arrived = []
    for first in range(2):
        route = []
        for i in range(first, count - 1, 2):
            route += [(i, i + 1), (i + 1, i)]
        sent = jnp.where(odd, head, tail) if first == 0 else jnp.where(odd, tail, head)
        arrived.append(lax.ppermute(sent, "slab", route))
    below = jnp.where(odd, arrived[0], arrived[1])
    above = jnp.where(odd, arrived[1], arrived[0])
    return below, above


def in_hbm(*arrays):
    return [pltpu.with_memory_space_constraint(array, pltpu.HBM) for array in arrays]


def series(square, coefficients):
    total = jnp.full_like(square, coefficients[-1])
    for coefficient in coefficients[-2::-1]:
        total = total * square + coefficient
    return total


def fill_factors(factors_ref):
    rows, columns = factors_ref.shape
    near = 16
    count = columns // near
    half = count + near
    row = lax.broadcasted_iota(jnp.int32, (half, columns), 0)
    row = jnp.where(row < count, near * row, row - count).astype(jnp.float32)
    phase = row * lax.broadcasted_iota(jnp.int32, (half, columns), 1).astype(jnp.float32)
    phase = phase - columns * jnp.floor(phase * (1.0 / columns) + 0.5)
    angle = phase * (math.pi / columns)
    square = angle * angle
    sine = angle * series(square, [(-1.0) ** k / math.factorial(2 * k + 1) for k in range(7)])
    cosine = series(square, [(-1.0) ** k / math.factorial(2 * k) for k in range(8)])
    scale = 1.0 / math.sqrt(columns)
    waves = (1.0 - 2.0 * sine * sine, 2.0 * sine * cosine)
    for part, wave in enumerate(waves):
        begin = count * part
        factors_ref[begin : begin + count, :] = scale * wave[:count]
        begin = 2 * count + near * part
        factors_ref[begin : begin + near, :] = wave[count:]


def build_tables(factors_ref, high_ref, low_ref):
    columns = factors_ref.shape[1]
    near = 16
    count = columns // near
    near_cos = factors_ref[2 * count : 2 * count + near, :]
    near_sin = factors_ref[2 * count + near :, :]
    for a in range(count):
        far_cos = factors_ref[a : a + 1, :]
        far_sin = factors_ref[count + a : count + a + 1, :]
        tables = (far_cos * near_cos - far_sin * near_sin, far_sin * near_cos + far_cos * near_sin)
        rows = slice(near * a, near * (a + 1))
        for part, table in enumerate(tables):
            high = table.astype(jnp.bfloat16)
            lanes = slice(columns * part, columns * (part + 1))
            high_ref[rows, lanes] = high
            low_ref[rows, lanes] = (table - high.astype(jnp.float32)).astype(jnp.bfloat16)


def moved_right(value):
    tiles = value.shape[-1] // 128
    moved = [pltpu.roll(value[:, 128 * j : 128 * (j + 1)], 1, 1) for j in range(tiles)]
    edge = lax.broadcasted_iota(jnp.int32, moved[0].shape, 1) == 0
    return jnp.concatenate(
        [jnp.where(edge, moved[j - 1] if j > 0 else 0.0, moved[j]) for j in range(tiles)], axis=1
    )


def moved_left(value):
    tiles = value.shape[-1] // 128
    moved = [pltpu.roll(value[:, 128 * j : 128 * (j + 1)], 127, 1) for j in range(tiles)]
    edge = lax.broadcasted_iota(jnp.int32, moved[0].shape, 1) == 127
    return jnp.concatenate(
        [
            jnp.where(edge, moved[j + 1] if j < tiles - 1 else 0.0, moved[j])
            for j in range(tiles)
        ],
        axis=1,
    )


def half_silu(half):
    return half + half * jnp.tanh(half)


def table_product(source, high_ref, low_ref):
    rows = source.shape[0]
    high = source.astype(jnp.bfloat16)
    low = (source - high.astype(jnp.float32)).astype(jnp.bfloat16)
    both = jnp.dot(
        jnp.concatenate([high, low], axis=0), high_ref[...], preferred_element_type=jnp.float32
    )
    rest = jnp.dot(high, low_ref[...], preferred_element_type=jnp.float32)
    return both[:rows] + both[rows:] + rest


def halves_swapped(value):
    return pltpu.roll(value, 4, value.ndim - 2)


def upper_half(value):
    return lax.broadcasted_iota(jnp.int32, value.shape, value.ndim - 2) < 4


def signed_swap(value, top, bottom):
    sign = jnp.where(upper_half(value), top, bottom)
    return sign * halves_swapped(value)


def stacked_parts(value):
    return jnp.concatenate([value[..., 0, :, :], value[..., 1, :, :]], axis=-2)


def turned_tiles(value, shift, store):
    tiles = value.shape[-1] // 128
    whole, part = shift // 128, lax.rem(shift, 128)
    moved = [
        pltpu.roll(value[..., 128 * j : 128 * (j + 1)], part, value.ndim - 1) for j in range(tiles)
    ]
    lane = lax.broadcasted_iota(jnp.int32, moved[0].shape, value.ndim - 1)
    for j in range(tiles):
        store(lax.rem(j + whole, tiles), jnp.where(lane < part, moved[j - 1], moved[j]))


def fill_weights(first_raw, mid_raw, last_raw, first_sum, last_sum, first_ref, wide_ref, last_ref):
    channels = mid_raw.shape[-1]
    two = 2 * channels
    first_sum[...] = jnp.zeros_like(first_sum)
    last_sum[...] = jnp.zeros_like(last_sum)
    for d in range(3):
        for u in range(3):
            for t in range(3):
                block = first_raw[d, u, t].astype(jnp.float32) * 0.5
                for i in range(2):
                    for r in range(4):
                        row = (t * 3 + d) * 16 + i * 8 + u + r
                        first_sum[row : row + 1, r * channels : (r + 1) * channels] = block[
                            i : i + 1
                        ]
                block = last_raw[d, u, t].astype(jnp.float32)
                for o in range(2):
                    for r in range(4):
                        row = (d * 3 + t) * 8 + o * 4 + r
                        col = (r + u) * channels
                        last_sum[row : row + 1, col : col + channels] = block[o : o + 1]
    first_ref[...] = first_sum[...].T[:, : first_ref.shape[1]].astype(jnp.bfloat16)
    last_ref[...] = last_sum[...].astype(jnp.bfloat16)
    half_weight = jnp.bfloat16(0.5)
    for t in range(3):
        for r in range(2):
            row = (t * 2 + r) * channels
            for d in range(3):
                for pair in range(2):
                    blocks = []
                    for q in (2 * pair, 2 * pair + 1):
                        if 0 <= q - r <= 2:
                            blocks.append(mid_raw[d, q - r, t] * half_weight)
                        else:
                            blocks.append(jnp.zeros((channels, channels), jnp.bfloat16))
                    col = (d * 4 + 2 * pair) * channels
                    wide_ref[row : row + channels, col : col + two] = jnp.concatenate(
                        blocks, axis=1
                    )


def preparation_kernel(
    size_ref, steps_hbm, order_hbm, coil_hbm,
    turned_ref, scalars_ref, high_ref, low_ref,
    steps_ref, order_ref, coil_ref, factors_ref, sems, coil_sems,
):
    all_positions, slices, coils, _, rows, columns = coil_ref.shape
    unit = columns // 8
    block = coils * 2 * rows
    copies = [
        pltpu.make_async_copy(steps_hbm, steps_ref, sems.at[0]),
        pltpu.make_async_copy(order_hbm, order_ref, sems.at[1]),
    ] + [
        pltpu.make_async_copy(coil_hbm.at[g], coil_ref.at[g], coil_sems.at[g])
        for g in range(all_positions)
    ]
    for copy in copies:
        copy.start()
    fill_factors(factors_ref)
    build_tables(factors_ref, high_ref, low_ref)
    scalars_ref[all_positions:, :] = jnp.full(
        (scalars_ref.shape[0] - all_positions, 128), size_ref[0], jnp.float32
    )
    for copy in copies:
        copy.wait()
    for g in range(all_positions):
        shift = steps_ref[order_ref[g]] * unit
        scalars_ref[g : g + 1, :] = jnp.full((1, 128), shift, jnp.int32).astype(jnp.float32)
        for s in range(slices):

            def store_coil(j, value, s=s, g=g):
                turned_ref[j, g, s] = value.reshape(block, 128).astype(jnp.bfloat16)

            turned_tiles(stacked_parts(coil_ref[g, s].astype(jnp.float32)), shift, store_coil)


def preparation(step_size, coil_maps, caipi_steps, band_order):
    all_positions, slices, coils, _, rows, columns = coil_maps.shape
    f32, bf16 = jnp.float32, jnp.bfloat16
    hbm = pl.BlockSpec(memory_space=pltpu.HBM)
    vmem = pl.BlockSpec(memory_space=pltpu.VMEM)
    turned_shape = (columns // 128, all_positions, slices, coils * 2 * rows, 128)
    return pl.pallas_call(
        preparation_kernel,
        out_shape=(
            jax.ShapeDtypeStruct(turned_shape, bf16),
            jax.ShapeDtypeStruct((2 * all_positions, 128), f32),
            jax.ShapeDtypeStruct((columns, 2 * columns), bf16),
            jax.ShapeDtypeStruct((columns, 2 * columns), bf16),
        ),
        in_specs=[pl.BlockSpec(memory_space=pltpu.SMEM)] + [hbm] * 3,
        out_specs=(vmem,) * 4,
        scratch_shapes=[
            pltpu.SMEM(caipi_steps.shape, jnp.int32),
            pltpu.SMEM(band_order.shape, jnp.int32),
            pltpu.VMEM(coil_maps.shape, bf16),
            pltpu.VMEM((2 * (columns // 16 + 16), columns), f32),
            pltpu.SemaphoreType.DMA((2,)),
            pltpu.SemaphoreType.DMA((all_positions,)),
        ],
        compiler_params=pltpu.CompilerParams(vmem_limit_bytes=40 * 2**20),
        cost_estimate=pl.CostEstimate(
            flops=4 * 10**9, bytes_accessed=4 * 10**6, transcendentals=0
        ),
    )(step_size, *in_hbm(caipi_steps, band_order, coil_maps))


def consistency_kernel(
    own_ref, one_ref, two_ref, three_ref, turned_ref, scalars_ref, high_ref, low_ref,
    kspace_hbm, mask_hbm, first_hbm, mid_hbm, last_hbm,
    own_out, one_out, two_out, three_out, first_ref, wide_ref, last_ref,
    kspace_ref, mask_ref, first_raw, mid_raw, last_raw, first_sum, last_sum,
    real_ref, imag_ref, field_ref, swap_ref, sum_ref, sems,
):
    tiles, all_positions, slices, _, _ = turned_ref.shape
    _, coils, _, rows, columns = kspace_ref.shape
    doubled, positions = 2 * rows, all_positions // 4
    copies = [
        pltpu.make_async_copy(kspace_hbm, kspace_ref, sems.at[0]),
        pltpu.make_async_copy(mask_hbm, mask_ref, sems.at[1]),
        pltpu.make_async_copy(first_hbm, first_raw, sems.at[2]),
        pltpu.make_async_copy(mid_hbm, mid_raw, sems.at[3]),
        pltpu.make_async_copy(last_hbm, last_raw, sems.at[4]),
    ]
    for copy in copies:
        copy.start()
    size = scalars_ref[all_positions : all_positions + 1, :]
    owners = []
    for x in range(4):
        first = lax.bitwise_xor(lax.axis_index("band"), jnp.int32(x)) * positions
        for p in range(positions):
            shift = jnp.max(scalars_ref[pl.ds(first + p, 1), :]).astype(jnp.int32)
            owners.append((x, p, first + p, shift))

    def coil_of(j, g, s):
        return turned_ref[j, g, s].astype(jnp.float32).reshape(coils, doubled, 128)

    images = (own_ref, one_ref, two_ref, three_ref)
    for k, (x, p, g, shift) in enumerate(owners):

        def store_image(j, value, k=k):
            other = halves_swapped(value)
            top = upper_half(value)
            real_ref[j, k] = jnp.where(top, value, other)
            imag_ref[j, k] = jnp.where(top, other, value)

        image = images[x][p * slices : (p + 1) * slices].astype(jnp.float32)
        turned_tiles(image, shift, store_image)
    for copy in copies:
        copy.wait()

    block = coils * doubled
    halves = [range(0, slices // 2), range(slices // 2, slices)]

    def rows_of(half):
        return slice(half[0] * block, (half[-1] + 1) * block)

    def collapse(half):
        for j in range(tiles):
            for s in half:
                with_real = jnp.zeros((coils, doubled, 128), jnp.float32)
                with_imag = jnp.zeros((coils, doubled, 128), jnp.float32)
                for k, (_, _, g, _) in enumerate(owners):
                    coil = coil_of(j, g, s)
                    with_real += coil * real_ref[j, k, s]
                    with_imag += coil * imag_ref[j, k, s]
                total = with_real + signed_swap(with_imag, -1.0, 1.0)
                field_ref[s * block : (s + 1) * block, 128 * j : 128 * (j + 1)] = total.reshape(
                    block, 128
                )

    def transformed(source, half, top, bottom):
        product = table_product(source, high_ref, low_ref)
        grouped = (len(half), coils, doubled, columns)
        with_cos = product[:, :columns].reshape(grouped)
        with_sin = product[:, columns:].reshape(grouped)
        return with_cos + signed_swap(with_sin, top, bottom)

    def project(half):
        spectrum = transformed(field_ref[rows_of(half)], half, 1.0, -1.0)
        keep = mask_ref[...].astype(jnp.float32)[half[0] : half[-1] + 1]
        keep = keep.reshape(len(half), 1, 1, columns)
        data = stacked_parts(kspace_ref[half[0] : half[-1] + 1])
        residual = (keep * (spectrum - data)).reshape(len(half) * block, columns)
        back = transformed(residual, half, -1.0, 1.0)
        field_ref[rows_of(half)] = back.reshape(len(half) * block, columns)
        swap_ref[rows_of(half)] = halves_swapped(back).reshape(len(half) * block, columns)

    def combine(half):
        for j in range(tiles):
            for s in half:
                place = (slice(s * block, (s + 1) * block), slice(128 * j, 128 * (j + 1)))
                field = field_ref[place].reshape(coils, doubled, 128)
                swapped = swap_ref[place].reshape(coils, doubled, 128)
                for k, (_, _, g, _) in enumerate(owners):
                    coil = coil_of(j, g, s)
                    straight = jnp.sum(coil * field, axis=0)
                    crossed = jnp.sum(coil * swapped, axis=0)
                    straight = straight + halves_swapped(straight)
                    crossed = halves_swapped(crossed) - crossed
                    sum_ref[k, s, :, 128 * j : 128 * (j + 1)] = size * jnp.where(
                        upper_half(straight), straight, crossed
                    )

    for half in halves:
        collapse(half)
    project(halves[0])
    fill_weights(
        first_raw, mid_raw, last_raw, first_sum, last_sum, first_ref, wide_ref, last_ref
    )
    project(halves[1])
    for half in halves:
        combine(half)

    outs = (own_out, one_out, two_out, three_out)
    for k, (x, p, _, shift) in enumerate(owners):
        back_shift = lax.rem(columns - shift, columns)
        outs[x][p] = pltpu.roll(sum_ref[k], back_shift, 2).astype(jnp.bfloat16)


def partial_consistency(
    images, prepared, measured_kspace, sample_mask, weight_in, weight_mid, weight_out
):
    tiles, all_positions, slices, _, _ = prepared[0].shape
    _, coils, _, rows, columns = measured_kspace.shape
    channels = weight_mid.shape[0]
    first = jnp.transpose(weight_in, (2, 3, 4, 1, 0))
    mid = jnp.transpose(weight_mid, (2, 3, 4, 0, 1))
    last = jnp.transpose(weight_out, (2, 3, 4, 0, 1))
    doubled = 2 * rows
    total = slices * coils * doubled
    f32, bf16 = jnp.float32, jnp.bfloat16
    hbm = pl.BlockSpec(memory_space=pltpu.HBM)
    vmem = pl.BlockSpec(memory_space=pltpu.VMEM)
    image_shape = (tiles, all_positions, slices, doubled, 128)
    part = jax.ShapeDtypeStruct((all_positions // 4, slices, doubled, columns), bf16)
    *sums, first, mid, last = pl.pallas_call(
        consistency_kernel,
        out_shape=(part,) * 4
        + (
            jax.ShapeDtypeStruct((4 * channels, 144), bf16),
            jax.ShapeDtypeStruct((6 * channels, 12 * channels), bf16),
            jax.ShapeDtypeStruct((72, 6 * channels), bf16),
        ),
        in_specs=[vmem] * 8 + [hbm] * 5,
        out_specs=(vmem,) * 7,
        scratch_shapes=[
            pltpu.VMEM(measured_kspace.shape, f32),
            pltpu.VMEM(sample_mask.shape, jnp.int32),
            pltpu.VMEM(first.shape, bf16),
            pltpu.VMEM(mid.shape, bf16),
            pltpu.VMEM(last.shape, bf16),
            pltpu.VMEM((256, 4 * channels), f32),
            pltpu.VMEM((72, 6 * channels), f32),
            pltpu.VMEM(image_shape, f32),
            pltpu.VMEM(image_shape, f32),
            pltpu.VMEM((total, columns), f32),
            pltpu.VMEM((total, columns), f32),
            pltpu.VMEM((all_positions, slices, doubled, columns), f32),
            pltpu.SemaphoreType.DMA((5,)),
        ],
        compiler_params=pltpu.CompilerParams(vmem_limit_bytes=40 * 2**20),
        cost_estimate=pl.CostEstimate(
            flops=4 * 10**9, bytes_accessed=4 * 10**6, transcendentals=0
        ),
    )(*images, *prepared, *in_hbm(measured_kspace, sample_mask, first, mid, last))
    return sums, (first, mid, last)


def network_kernel(
    window_ref, scalars_ref, first_ref, wide_ref, last_ref, image_hbm, noise_hbm,
    out_ref,
    image_ref, noise_ref, taps_ref, f1_ref, f2_ref, part_a, part_b, score_ref, sems,
):
    channels = first_ref.shape[0] // 4
    out_slices, _, rows, columns = out_ref.shape
    slices1, slices2 = out_slices + 4, out_slices + 2
    pairs = (
        (image_hbm, image_ref), (noise_hbm, noise_ref),
    )
    copies = [pltpu.make_async_copy(src, dst, sems.at[i]) for i, (src, dst) in enumerate(pairs)]
    for copy in copies:
        copy.start()

    def inside(axis, end):
        edge = lax.axis_size(axis) - 1 if end else 0
        return jnp.where(lax.axis_index(axis) == edge, 0.0, 1.0).astype(jnp.float32)

    low_slice, high_slice = inside("band", False), inside("band", True)
    low_row, high_row = inside("slab", False), inside("slab", True)
    four, two = 4 * channels, 2 * channels

    for g in range(2):
        base = window_ref[g].astype(jnp.float32)
        taps_ref[g, 0] = moved_right(base).astype(jnp.bfloat16)
        taps_ref[g, 1] = window_ref[g]
        taps_ref[g, 2] = moved_left(base).astype(jnp.bfloat16)

    def first_layer(z):
        source = jnp.concatenate(
            [
                jnp.concatenate([taps_ref[g, t, 16 * z : 16 * z + 48, :] for t in range(3)], axis=0)
                for g in range(2)
            ],
            axis=1,
        )
        half = jnp.dot(first_ref[...], source, preferred_element_type=jnp.float32)
        for r in range(8):
            begin = (r % 4) * channels
            first = columns * (r // 4)
            value = half_silu(half[begin : begin + channels, first : first + columns])
            factors = []
            if z < 2:
                factors.append(low_slice)
            if z >= slices1 - 2:
                factors.append(high_slice)
            if r < 2:
                factors.append(low_row)
            if r >= 6:
                factors.append(high_row)
            for factor in factors:
                value = value * factor
            f1_ref[z, r * channels : (r + 1) * channels, :] = value.astype(jnp.bfloat16)

    def second_product(z, pair, part_ref):
        source = jnp.concatenate(
            [
                f1_ref[z + a : z + a + 3, two * pair : two * pair + four, :].reshape(
                    3 * four, columns
                )
                for a in range(2)
            ],
            axis=1,
        )
        part_ref[...] = jnp.dot(wide_ref[...], source, preferred_element_type=jnp.float32)

    def second_layer(z, pair, part_ref):
        for a in range(2):
            first = columns * a
            for r in range(2):
                row = r * channels
                half = (
                    moved_right(part_ref[row : row + channels, first : first + columns])
                    + part_ref[two + row : two + row + channels, first : first + columns]
                    + moved_left(
                        part_ref[four + row : four + row + channels, first : first + columns]
                    )
                )
                value = half_silu(half)
                factors = []
                if z + a == 0:
                    factors.append(low_slice)
                if z + a == slices2 - 1:
                    factors.append(high_slice)
                if pair == 0 and r == 0:
                    factors.append(low_row)
                if pair == 2 and r == 1:
                    factors.append(high_row)
                for factor in factors:
                    value = value * factor
                place = two * pair + r * channels
                f2_ref[z + a, place : place + channels, :] = value.astype(jnp.bfloat16)

    def third_product(z):
        source = jnp.concatenate([f2_ref[z], f2_ref[z + 1]], axis=1)
        score_ref[z // 2] = jnp.dot(last_ref[...], source, preferred_element_type=jnp.float32)

    def finish(first_slice, end):
        for z in range(max(first_slice, 0), end):
            taps = []
            for t in range(3):
                total = None
                for d in range(3):
                    row, first = (3 * d + t) * 8, columns * ((z + d) % 2)
                    piece = score_ref[(z + d) // 2, row : row + 8, first : first + columns]
                    total = piece if total is None else total + piece
                taps.append(total)
            score = size * (moved_right(taps[0]) + taps[1] + moved_left(taps[2]))
            for part in range(2):
                out_ref[z, part] = (
                    image_ref[z, part]
                    + score[part * rows : (part + 1) * rows]
                    + noise_scale * noise_ref[z, part]
                )

    for z in range(4):
        first_layer(z)
    for copy in copies:
        copy.wait()
    size = scalars_ref[scalars_ref.shape[0] - 1 :, :]
    size = jnp.concatenate([size] * (columns // 128), axis=1)
    noise_scale = jnp.sqrt(2.0 * size)
    waiting = None
    parts = (part_a, part_b)
    count = 0
    for z in range(0, slices2, 2):
        for pair in range(3):
            second_product(z, pair, parts[count % 2])
            if pair < 2 and z + 4 + pair < slices1:
                first_layer(z + 4 + pair)
            if waiting is not None:
                second_layer(*waiting)
                if waiting[1] == 2:
                    third_product(waiting[0])
                    finish(waiting[0] - 2, waiting[0])
            waiting = (z, pair, parts[count % 2])
            count += 1
    second_layer(*waiting)
    third_product(waiting[0])
    finish(waiting[0] - 2, out_slices)


def stepped_without_data(windows, scalars, weights, current_image, langevin_noise):
    channels = weights[0].shape[0] // 4
    slices0, columns = windows.shape[1] // 16, windows.shape[-1]
    out_slices = slices0 - 6
    local = (out_slices,) + current_image.shape[2:]
    hbm = pl.BlockSpec(memory_space=pltpu.HBM)
    vmem = pl.BlockSpec(memory_space=pltpu.VMEM)
    return pl.pallas_call(
        network_kernel,
        out_shape=jax.ShapeDtypeStruct(local, jnp.float32),
        in_specs=[vmem] * 5 + [hbm] * 2,
        out_specs=vmem,
        scratch_shapes=[
            pltpu.VMEM(local, jnp.float32),
            pltpu.VMEM(local, jnp.float32),
            pltpu.VMEM((2, 3, slices0 * 16, columns), jnp.bfloat16),
            pltpu.VMEM((out_slices + 4, 8 * channels, columns), jnp.bfloat16),
            pltpu.VMEM((out_slices + 2, 6 * channels, columns), jnp.bfloat16),
            pltpu.VMEM((6 * channels, 2 * columns), jnp.float32),
            pltpu.VMEM((6 * channels, 2 * columns), jnp.float32),
            pltpu.VMEM((out_slices // 2 + 1, 72, 2 * columns), jnp.float32),
            pltpu.SemaphoreType.DMA((2,)),
        ],
        compiler_params=pltpu.CompilerParams(vmem_limit_bytes=40 * 2**20),
        cost_estimate=pl.CostEstimate(
            flops=10**10, bytes_accessed=2 * 10**6, transcendentals=4 * 10**6
        ),
    )(
        windows, scalars, *weights,
        *in_hbm(current_image.reshape(local), langevin_noise.reshape(local)),
    ).reshape(current_image.shape)


def per_device(
    current_image, langevin_noise, step_size, coil_maps, measured_kspace, sample_mask,
    caipi_steps, band_order, weight_in, weight_mid, weight_out,
):
    positions, group_slices, _, row_count, columns = current_image.shape
    local_slices = positions * group_slices
    band, bands = lax.axis_index("band"), lax.axis_size("band")
    own = current_image.astype(jnp.bfloat16).reshape(local_slices, 2 * row_count, columns)
    routes = [[(i, i ^ x) for i in range(bands)] for x in range(1, 4)]
    across = [lax.ppermute(own, "band", route) for route in routes[1:]]
    images = [own, lax.ppermute(own, "band", routes[0])] + across
    prepared = preparation(step_size, coil_maps, caipi_steps, band_order)

    odd = band % 2 == 1
    under = jnp.where(odd, images[1], images[3])[local_slices - 3 :]
    over = jnp.where(odd, images[3], images[1])[:3]
    under = jnp.where(band == 0, jnp.zeros_like(under), under)
    over = jnp.where(band == bands - 1, jnp.zeros_like(over), over)
    tall = jnp.concatenate([under, own, over], axis=0)
    tall = tall.reshape(-1, 2, row_count, columns)
    below, above = exchanged_rows(tall, 3)
    sums, weights = partial_consistency(
        images, prepared, measured_kspace, sample_mask, weight_in, weight_mid, weight_out
    )
    sums, below, above = lax.optimization_barrier((sums, below, above))
    arrived = [lax.ppermute(part, "band", route) for part, route in zip(sums[1:], routes)]
    field = jnp.concatenate([below, tall, above, jnp.zeros_like(above[:, :, :2])], axis=2)
    windows = jnp.stack(
        [field[:, :, 4 * g : 4 * g + 8].reshape(-1, columns) for g in range(2)], axis=0
    )
    base = stepped_without_data(
        windows, prepared[1], weights, current_image, langevin_noise
    )
    total = sums[0].astype(jnp.float32)
    for part in arrived:
        total = total + part.astype(jnp.float32)
    return base - total.reshape(base.shape)


def solution(mesh):
    band5 = P("band", None, None, "slab", None)
    in_specs = (
        band5,
        band5,
        P(),
        P(None, None, "band", None, "slab", None),
        P(None, "band", None, "slab", None),
        P(), P(), P(), P(), P(), P(),
    )
    return jax.shard_map(
        per_device, mesh=mesh, in_specs=in_specs, out_specs=band5, check_vma=False
    )
```

```python
import functools
import math

import jax
import jax.numpy as jnp
from jax import lax
from jax.experimental import pallas as pl
from jax.experimental.pallas import tpu as pltpu
from jax.sharding import PartitionSpec as P


def exchanged_rows(tall, width):
    count = lax.axis_size("slab")
    odd = lax.axis_index("slab") % 2 == 1
    head, tail = tall[:, :, :width, :], tall[:, :, tall.shape[2] - width :, :]
    arrived = {}
    for first in (1, 0):
        route = []
        for i in range(first, count - 1, 2):
            route += [(i, i + 1), (i + 1, i)]
        sent = jnp.where(odd, head, tail) if first == 0 else jnp.where(odd, tail, head)
        arrived[first] = lax.ppermute(sent, "slab", route)
    below = jnp.where(odd, arrived[0], arrived[1])
    above = jnp.where(odd, arrived[1], arrived[0])
    return below, above


def in_hbm(*arrays):
    return [pltpu.with_memory_space_constraint(array, pltpu.HBM) for array in arrays]


def series(square, coefficients):
    total = jnp.full_like(square, coefficients[-1])
    for coefficient in coefficients[-2::-1]:
        total = total * square + coefficient
    return total


def fill_factors(factors_ref):
    rows, columns = factors_ref.shape
    near = 16
    count = columns // near
    half = count + near
    row = lax.broadcasted_iota(jnp.int32, (half, columns), 0)
    row = jnp.where(row < count, near * row, row - count).astype(jnp.float32)
    phase = row * lax.broadcasted_iota(jnp.int32, (half, columns), 1).astype(jnp.float32)
    phase = phase - columns * jnp.floor(phase * (1.0 / columns) + 0.5)
    angle = phase * (math.pi / columns)
    square = angle * angle
    sine = angle * series(square, [(-1.0) ** k / math.factorial(2 * k + 1) for k in range(7)])
    cosine = series(square, [(-1.0) ** k / math.factorial(2 * k) for k in range(8)])
    scale = 1.0 / math.sqrt(columns)
    waves = (1.0 - 2.0 * sine * sine, 2.0 * sine * cosine)
    for part, wave in enumerate(waves):
        begin = count * part
        factors_ref[begin : begin + count, :] = scale * wave[:count]
        begin = 2 * count + near * part
        factors_ref[begin : begin + near, :] = wave[count:]


def build_tables(factors_ref, high_ref, low_ref):
    columns = factors_ref.shape[1]
    near = 16
    count = columns // near
    near_cos = factors_ref[2 * count : 2 * count + near, :]
    near_sin = factors_ref[2 * count + near :, :]
    for a in range(count):
        far_cos = factors_ref[a : a + 1, :]
        far_sin = factors_ref[count + a : count + a + 1, :]
        tables = (far_cos * near_cos - far_sin * near_sin, far_sin * near_cos + far_cos * near_sin)
        rows = slice(near * a, near * (a + 1))
        for part, table in enumerate(tables):
            high = table.astype(jnp.bfloat16)
            lanes = slice(columns * part, columns * (part + 1))
            high_ref[rows, lanes] = high
            low_ref[rows, lanes] = (table - high.astype(jnp.float32)).astype(jnp.bfloat16)


def moved_right(value):
    tiles = value.shape[-1] // 128
    moved = [pltpu.roll(value[:, 128 * j : 128 * (j + 1)], 1, 1) for j in range(tiles)]
    edge = lax.broadcasted_iota(jnp.int32, moved[0].shape, 1) == 0
    return jnp.concatenate(
        [jnp.where(edge, moved[j - 1] if j > 0 else 0.0, moved[j]) for j in range(tiles)], axis=1
    )


def moved_left(value):
    tiles = value.shape[-1] // 128
    moved = [pltpu.roll(value[:, 128 * j : 128 * (j + 1)], 127, 1) for j in range(tiles)]
    edge = lax.broadcasted_iota(jnp.int32, moved[0].shape, 1) == 127
    return jnp.concatenate(
        [
            jnp.where(edge, moved[j + 1] if j < tiles - 1 else 0.0, moved[j])
            for j in range(tiles)
        ],
        axis=1,
    )


def half_silu(half):
    return half + half * jnp.tanh(half)


def table_product(source, high_ref, low_ref):
    rows = source.shape[0]
    high = source.astype(jnp.bfloat16)
    low = (source - high.astype(jnp.float32)).astype(jnp.bfloat16)
    both = jnp.dot(
        jnp.concatenate([high, low], axis=0), high_ref[...], preferred_element_type=jnp.float32
    )
    rest = jnp.dot(high, low_ref[...], preferred_element_type=jnp.float32)
    return both[:rows] + both[rows:] + rest


def halves_swapped(value):
    return pltpu.roll(value, 4, value.ndim - 2)


def upper_half(value):
    return lax.broadcasted_iota(jnp.int32, value.shape, value.ndim - 2) < 4


def signed_swap(value, top, bottom):
    sign = jnp.where(upper_half(value), top, bottom)
    return sign * halves_swapped(value)


def stacked_parts(value):
    return jnp.concatenate([value[..., 0, :, :], value[..., 1, :, :]], axis=-2)


def turned_tiles(value, shift, store):
    tiles = value.shape[-1] // 128
    whole, part = shift // 128, lax.rem(shift, 128)
    moved = [
        pltpu.roll(value[..., 128 * j : 128 * (j + 1)], part, value.ndim - 1) for j in range(tiles)
    ]
    lane = lax.broadcasted_iota(jnp.int32, moved[0].shape, value.ndim - 1)
    for j in range(tiles):
        store(lax.rem(j + whole, tiles), jnp.where(lane < part, moved[j - 1], moved[j]))


def fill_weights(
    first_raw, mid_raw, last_raw, first_sum, last_sum, form_ref, first_ref, wide_ref, last_ref
):
    channels = mid_raw.shape[-1]
    two = 2 * channels
    first_sum[...] = jnp.zeros_like(first_sum)
    last_sum[...] = jnp.zeros_like(last_sum)
    for d in range(3):
        for u in range(3):
            for t in range(3):
                block = first_raw[d, u, t].astype(jnp.float32) * 0.5
                for i in range(2):
                    for r in range(4):
                        row = (t * 3 + d) * 16 + i * 8 + u + r
                        first_sum[row : row + 1, r * channels : (r + 1) * channels] = block[
                            i : i + 1
                        ]
                block = last_raw[d, u, t].astype(jnp.float32)
                for o in range(2):
                    for r in range(4):
                        row = (d * 3 + t) * 8 + o * 4 + r
                        col = (r + u) * channels
                        last_sum[row : row + 1, col : col + channels] = block[o : o + 1]
    first_ref[...] = first_sum[...].T[:, : first_ref.shape[1]].astype(jnp.bfloat16)
    last_ref[...] = last_sum[...].astype(jnp.bfloat16)
    for u in range(3):
        for t in range(3):
            low, mid, high = (0.5 * mid_raw[d, u, t].astype(jnp.float32) for d in range(3))
            ends = 0.5 * (low + high)
            forms = (low, ends + 0.5 * mid, ends - 0.5 * mid, high)
            for k, form in enumerate(forms):
                form_ref[k, t, u] = form.astype(jnp.bfloat16)
    for k in range(4):
        for t in range(3):
            for r in range(2):
                row = (t * 2 + r) * channels
                for pair in range(2):
                    blocks = []
                    for q in (2 * pair, 2 * pair + 1):
                        if 0 <= q - r <= 2:
                            blocks.append(form_ref[k, t, q - r])
                        else:
                            blocks.append(jnp.zeros((channels, channels), jnp.bfloat16))
                    wide_ref[k, row : row + channels, two * pair : two * (pair + 1)] = (
                        jnp.concatenate(blocks, axis=1)
                    )


def preparation_kernel(
    size_ref, steps_hbm, order_hbm, coil_hbm,
    turned_ref, scalars_ref, high_ref, low_ref,
    steps_ref, order_ref, coil_ref, factors_ref, sems, coil_sems,
):
    all_positions, slices, coils, _, rows, columns = coil_ref.shape
    unit = columns // 8
    block = coils * 2 * rows
    copies = [
        pltpu.make_async_copy(steps_hbm, steps_ref, sems.at[0]),
        pltpu.make_async_copy(order_hbm, order_ref, sems.at[1]),
    ] + [
        pltpu.make_async_copy(coil_hbm.at[g], coil_ref.at[g], coil_sems.at[g])
        for g in range(all_positions)
    ]
    for copy in copies:
        copy.start()
    fill_factors(factors_ref)
    build_tables(factors_ref, high_ref, low_ref)
    scalars_ref[all_positions:, :] = jnp.full(
        (scalars_ref.shape[0] - all_positions, 128), size_ref[0], jnp.float32
    )
    for copy in copies:
        copy.wait()
    for g in range(all_positions):
        shift = steps_ref[order_ref[g]] * unit
        scalars_ref[g : g + 1, :] = jnp.full((1, 128), shift, jnp.int32).astype(jnp.float32)
        for s in range(slices):

            def store_coil(j, value, s=s, g=g):
                turned_ref[j, g, s] = value.reshape(block, 128).astype(jnp.bfloat16)

            turned_tiles(stacked_parts(coil_ref[g, s].astype(jnp.float32)), shift, store_coil)


def preparation(step_size, coil_maps, caipi_steps, band_order):
    all_positions, slices, coils, _, rows, columns = coil_maps.shape
    f32, bf16 = jnp.float32, jnp.bfloat16
    hbm = pl.BlockSpec(memory_space=pltpu.HBM)
    vmem = pl.BlockSpec(memory_space=pltpu.VMEM)
    turned_shape = (columns // 128, all_positions, slices, coils * 2 * rows, 128)
    return pl.pallas_call(
        preparation_kernel,
        out_shape=(
            jax.ShapeDtypeStruct(turned_shape, bf16),
            jax.ShapeDtypeStruct((2 * all_positions, 128), f32),
            jax.ShapeDtypeStruct((columns, 2 * columns), bf16),
            jax.ShapeDtypeStruct((columns, 2 * columns), bf16),
        ),
        in_specs=[pl.BlockSpec(memory_space=pltpu.SMEM)] + [hbm] * 3,
        out_specs=(vmem,) * 4,
        scratch_shapes=[
            pltpu.SMEM(caipi_steps.shape, jnp.int32),
            pltpu.SMEM(band_order.shape, jnp.int32),
            pltpu.VMEM(coil_maps.shape, bf16),
            pltpu.VMEM((2 * (columns // 16 + 16), columns), f32),
            pltpu.SemaphoreType.DMA((2,)),
            pltpu.SemaphoreType.DMA((all_positions,)),
        ],
        compiler_params=pltpu.CompilerParams(vmem_limit_bytes=40 * 2**20),
        cost_estimate=pl.CostEstimate(
            flops=4 * 10**9, bytes_accessed=4 * 10**6, transcendentals=0
        ),
    )(step_size, *in_hbm(caipi_steps, band_order, coil_maps))


def consistency_kernel(
    own_ref, one_ref, two_ref, three_ref, turned_ref, scalars_ref, high_ref, low_ref,
    kspace_hbm, mask_hbm,
    own_out, one_out, two_out, three_out,
    kspace_ref, mask_ref, real_ref, imag_ref, field_ref, swap_ref, sum_ref, sems,
):
    tiles, all_positions, slices, _, _ = turned_ref.shape
    _, coils, _, rows, columns = kspace_ref.shape
    doubled, positions = 2 * rows, all_positions // 4
    copies = [
        pltpu.make_async_copy(kspace_hbm, kspace_ref, sems.at[0]),
        pltpu.make_async_copy(mask_hbm, mask_ref, sems.at[1]),
    ]
    for copy in copies:
        copy.start()
    size = scalars_ref[all_positions : all_positions + 1, :]
    owners = []
    for x in range(4):
        first = lax.bitwise_xor(lax.axis_index("band"), jnp.int32(x)) * positions
        for p in range(positions):
            shift = jnp.max(scalars_ref[pl.ds(first + p, 1), :]).astype(jnp.int32)
            owners.append((x, p, first + p, shift))

    def coil_of(j, g, s):
        return turned_ref[j, g, s].astype(jnp.float32).reshape(coils, doubled, 128)

    images = (own_ref, one_ref, two_ref, three_ref)
    for k, (x, p, g, shift) in enumerate(owners):

        def store_image(j, value, k=k):
            other = halves_swapped(value)
            top = upper_half(value)
            real_ref[j, k] = jnp.where(top, value, other)
            imag_ref[j, k] = jnp.where(top, other, value)

        image = images[x][p * slices : (p + 1) * slices].astype(jnp.float32)
        turned_tiles(image, shift, store_image)
    for copy in copies:
        copy.wait()

    block = coils * doubled
    halves = [range(0, slices // 2), range(slices // 2, slices)]

    def rows_of(half):
        return slice(half[0] * block, (half[-1] + 1) * block)

    def collapse(half):
        for j in range(tiles):
            for s in half:
                with_real = jnp.zeros((coils, doubled, 128), jnp.float32)
                with_imag = jnp.zeros((coils, doubled, 128), jnp.float32)
                for k, (_, _, g, _) in enumerate(owners):
                    coil = coil_of(j, g, s)
                    with_real += coil * real_ref[j, k, s]
                    with_imag += coil * imag_ref[j, k, s]
                total = with_real + signed_swap(with_imag, -1.0, 1.0)
                field_ref[s * block : (s + 1) * block, 128 * j : 128 * (j + 1)] = total.reshape(
                    block, 128
                )

    def transformed(source, half, top, bottom):
        product = table_product(source, high_ref, low_ref)
        grouped = (len(half), coils, doubled, columns)
        with_cos = product[:, :columns].reshape(grouped)
        with_sin = product[:, columns:].reshape(grouped)
        return with_cos + signed_swap(with_sin, top, bottom)

    def project(half):
        spectrum = transformed(field_ref[rows_of(half)], half, 1.0, -1.0)
        keep = mask_ref[...].astype(jnp.float32)[half[0] : half[-1] + 1]
        keep = keep.reshape(len(half), 1, 1, columns)
        data = stacked_parts(kspace_ref[half[0] : half[-1] + 1])
        residual = (keep * (spectrum - data)).reshape(len(half) * block, columns)
        back = transformed(residual, half, -1.0, 1.0)
        field_ref[rows_of(half)] = back.reshape(len(half) * block, columns)
        swap_ref[rows_of(half)] = halves_swapped(back).reshape(len(half) * block, columns)

    def combine(half):
        for j in range(tiles):
            for s in half:
                place = (slice(s * block, (s + 1) * block), slice(128 * j, 128 * (j + 1)))
                field = field_ref[place].reshape(coils, doubled, 128)
                swapped = swap_ref[place].reshape(coils, doubled, 128)
                for k, (_, _, g, _) in enumerate(owners):
                    coil = coil_of(j, g, s)
                    straight = jnp.sum(coil * field, axis=0)
                    crossed = jnp.sum(coil * swapped, axis=0)
                    straight = straight + halves_swapped(straight)
                    crossed = halves_swapped(crossed) - crossed
                    sum_ref[k, s, :, 128 * j : 128 * (j + 1)] = size * jnp.where(
                        upper_half(straight), straight, crossed
                    )

    for half in halves:
        collapse(half)
    for half in halves:
        project(half)
    for half in halves:
        combine(half)

    outs = (own_out, one_out, two_out, three_out)
    for k, (x, p, _, shift) in enumerate(owners):
        back_shift = lax.rem(columns - shift, columns)
        outs[x][p] = pltpu.roll(sum_ref[k], back_shift, 2).astype(jnp.bfloat16)


def partial_consistency(images, prepared, measured_kspace, sample_mask):
    tiles, all_positions, slices, _, _ = prepared[0].shape
    _, coils, _, rows, columns = measured_kspace.shape
    doubled = 2 * rows
    total = slices * coils * doubled
    hbm = pl.BlockSpec(memory_space=pltpu.HBM)
    vmem = pl.BlockSpec(memory_space=pltpu.VMEM)
    image_shape = (tiles, all_positions, slices, doubled, 128)
    part = jax.ShapeDtypeStruct((all_positions // 4, slices, doubled, columns), jnp.bfloat16)
    return pl.pallas_call(
        consistency_kernel,
        out_shape=(part,) * 4,
        in_specs=[vmem] * 8 + [hbm] * 2,
        out_specs=(vmem,) * 4,
        scratch_shapes=[
            pltpu.VMEM(measured_kspace.shape, jnp.float32),
            pltpu.VMEM(sample_mask.shape, jnp.int32),
            pltpu.VMEM(image_shape, jnp.float32),
            pltpu.VMEM(image_shape, jnp.float32),
            pltpu.VMEM((total, columns), jnp.float32),
            pltpu.VMEM((total, columns), jnp.float32),
            pltpu.VMEM((all_positions, slices, doubled, columns), jnp.float32),
            pltpu.SemaphoreType.DMA((2,)),
        ],
        compiler_params=pltpu.CompilerParams(vmem_limit_bytes=40 * 2**20),
        cost_estimate=pl.CostEstimate(
            flops=4 * 10**9, bytes_accessed=4 * 10**6, transcendentals=0
        ),
    )(*images, *prepared, *in_hbm(measured_kspace, sample_mask))


def network_kernel(
    window_ref, scalars_ref, first_hbm, mid_hbm, last_hbm, image_hbm, noise_hbm,
    out_ref,
    first_raw, mid_raw, last_raw, image_ref, noise_ref,
    first_sum, last_sum, form_ref, first_ref, wide_ref, last_ref, taps_ref, f1_ref, form1_ref, f2_ref,
    part_a, part_b, score_ref, sems,
):
    channels = mid_raw.shape[-1]
    out_slices, _, rows, columns = out_ref.shape
    slices1, slices2 = out_slices + 4, out_slices + 2
    pairs = (
        (first_hbm, first_raw), (mid_hbm, mid_raw), (last_hbm, last_raw),
        (image_hbm, image_ref), (noise_hbm, noise_ref),
    )
    copies = [pltpu.make_async_copy(src, dst, sems.at[i]) for i, (src, dst) in enumerate(pairs)]
    for copy in copies:
        copy.start()

    def inside(axis, end):
        edge = lax.axis_size(axis) - 1 if end else 0
        return jnp.where(lax.axis_index(axis) == edge, 0.0, 1.0).astype(jnp.float32)

    low_slice, high_slice = inside("band", False), inside("band", True)
    low_row, high_row = inside("slab", False), inside("slab", True)
    four, two = 4 * channels, 2 * channels
    parts = (part_a, part_b)

    for g in range(2):
        base = window_ref[g].astype(jnp.float32)
        taps_ref[g, 0] = moved_right(base).astype(jnp.bfloat16)
        taps_ref[g, 1] = window_ref[g]
        taps_ref[g, 2] = moved_left(base).astype(jnp.bfloat16)

    for copy in copies[:3]:
        copy.wait()
    fill_weights(
        first_raw, mid_raw, last_raw, first_sum, last_sum, form_ref, first_ref, wide_ref, last_ref
    )

    def first_layer(z):
        source = jnp.concatenate(
            [
                jnp.concatenate([taps_ref[g, t, 16 * z : 16 * z + 48, :] for t in range(3)], axis=0)
                for g in range(2)
            ],
            axis=1,
        )
        half = jnp.dot(first_ref[...], source, preferred_element_type=jnp.float32)
        for r in range(8):
            begin = (r % 4) * channels
            first = columns * (r // 4)
            value = half_silu(half[begin : begin + channels, first : first + columns])
            factors = []
            if z < 2:
                factors.append(low_slice)
            if z >= slices1 - 2:
                factors.append(high_slice)
            if r < 2:
                factors.append(low_row)
            if r >= 6:
                factors.append(high_row)
            for factor in factors:
                value = value * factor
            f1_ref[z, r * channels : (r + 1) * channels, :] = value.astype(jnp.bfloat16)

    def transform(z):
        layers = [f1_ref[z + d] for d in range(4)]
        forms = (
            layers[0] - layers[2],
            layers[1] + layers[2],
            layers[2] - layers[1],
            layers[1] - layers[3],
        )
        for k, form in enumerate(forms):
            form1_ref[z // 2 % 2, k] = form

    def second_product(z, k):
        source = jnp.concatenate(
            [form1_ref[z // 2 % 2, k, two * pair : two * pair + four, :] for pair in range(3)],
            axis=1,
        )
        parts[z // 2 % 2][k] = jnp.dot(
            wide_ref[k], source, preferred_element_type=jnp.float32
        )

    def second_layer(z, pair):
        part_ref = parts[z // 2 % 2]
        lanes = slice(columns * pair, columns * (pair + 1))
        for r in range(2):
            sums = ([], [])
            for t in range(3):
                row = t * two + r * channels
                one, two_, three, four_ = (
                    part_ref[k, row : row + channels, lanes] for k in range(4)
                )
                sums[0].append(one + two_ + three)
                sums[1].append(two_ - three - four_)
            for a in range(2):
                half = moved_right(sums[a][0]) + sums[a][1] + moved_left(sums[a][2])
                value = half_silu(half)
                factors = []
                if z + a == 0:
                    factors.append(low_slice)
                if z + a == slices2 - 1:
                    factors.append(high_slice)
                if pair == 0 and r == 0:
                    factors.append(low_row)
                if pair == 2 and r == 1:
                    factors.append(high_row)
                for factor in factors:
                    value = value * factor
                place = two * pair + r * channels
                f2_ref[z + a, place : place + channels, :] = value.astype(jnp.bfloat16)

    def third_product(z):
        source = jnp.concatenate([f2_ref[z], f2_ref[z + 1]], axis=1)
        score_ref[z // 2] = jnp.dot(last_ref[...], source, preferred_element_type=jnp.float32)

    for z in range(4):
        first_layer(z)
    transform(0)
    for z in range(0, slices2, 2):
        later = z + 4
        second_product(z, 0)
        if later < slices1:
            first_layer(later)
        second_product(z, 1)
        if later + 1 < slices1:
            first_layer(later + 1)
        second_product(z, 2)
        if z > 0:
            second_layer(z - 2, 0)
            second_layer(z - 2, 1)
        second_product(z, 3)
        if z > 0:
            second_layer(z - 2, 2)
            third_product(z - 2)
        if later < slices1:
            transform(z + 2)
    for pair in range(3):
        second_layer(slices2 - 2, pair)
    third_product(slices2 - 2)

    for copy in copies[3:]:
        copy.wait()
    size = scalars_ref[scalars_ref.shape[0] - 1 :, :]
    size = jnp.concatenate([size] * (columns // 128), axis=1)
    noise_scale = jnp.sqrt(2.0 * size)
    for z in range(out_slices):
        taps = []
        for t in range(3):
            total = None
            for d in range(3):
                row, first = (3 * d + t) * 8, columns * ((z + d) % 2)
                piece = score_ref[(z + d) // 2, row : row + 8, first : first + columns]
                total = piece if total is None else total + piece
            taps.append(total)
        score = size * (moved_right(taps[0]) + taps[1] + moved_left(taps[2]))
        for part in range(2):
            out_ref[z, part] = (
                image_ref[z, part]
                + score[part * rows : (part + 1) * rows]
                + noise_scale * noise_ref[z, part]
            )


def stepped_without_data(
    windows, scalars, current_image, langevin_noise, weight_in, weight_mid, weight_out
):
    channels = weight_mid.shape[0]
    first = jnp.transpose(weight_in, (2, 3, 4, 1, 0))
    mid = jnp.transpose(weight_mid, (2, 3, 4, 0, 1))
    last = jnp.transpose(weight_out, (2, 3, 4, 0, 1))
    slices0, columns = windows.shape[1] // 16, windows.shape[-1]
    out_slices = slices0 - 6
    local = (out_slices,) + current_image.shape[2:]
    hbm = pl.BlockSpec(memory_space=pltpu.HBM)
    vmem = pl.BlockSpec(memory_space=pltpu.VMEM)
    return pl.pallas_call(
        network_kernel,
        out_shape=jax.ShapeDtypeStruct(local, jnp.float32),
        in_specs=[vmem] * 2 + [hbm] * 5,
        out_specs=vmem,
        scratch_shapes=[
            pltpu.VMEM(first.shape, jnp.bfloat16),
            pltpu.VMEM(mid.shape, jnp.bfloat16),
            pltpu.VMEM(last.shape, jnp.bfloat16),
            pltpu.VMEM(local, jnp.float32),
            pltpu.VMEM(local, jnp.float32),
            pltpu.VMEM((256, 4 * channels), jnp.float32),
            pltpu.VMEM((72, 6 * channels), jnp.float32),
            pltpu.VMEM((4, 3, 3, channels, channels), jnp.bfloat16),
            pltpu.VMEM((4 * channels, 144), jnp.bfloat16),
            pltpu.VMEM((4, 6 * channels, 4 * channels), jnp.bfloat16),
            pltpu.VMEM((72, 6 * channels), jnp.bfloat16),
            pltpu.VMEM((2, 3, slices0 * 16, columns), jnp.bfloat16),
            pltpu.VMEM((out_slices + 4, 8 * channels, columns), jnp.bfloat16),
            pltpu.VMEM((2, 4, 8 * channels, columns), jnp.bfloat16),
            pltpu.VMEM((out_slices + 2, 6 * channels, columns), jnp.bfloat16),
            pltpu.VMEM((4, 6 * channels, 3 * columns), jnp.float32),
            pltpu.VMEM((4, 6 * channels, 3 * columns), jnp.float32),
            pltpu.VMEM((out_slices // 2 + 1, 72, 2 * columns), jnp.float32),
            pltpu.SemaphoreType.DMA((5,)),
        ],
        compiler_params=pltpu.CompilerParams(vmem_limit_bytes=40 * 2**20),
        cost_estimate=pl.CostEstimate(
            flops=10**10, bytes_accessed=2 * 10**6, transcendentals=4 * 10**6
        ),
    )(
        windows, scalars,
        *in_hbm(first, mid, last, current_image.reshape(local), langevin_noise.reshape(local)),
    ).reshape(current_image.shape)


def per_device(
    current_image, langevin_noise, step_size, coil_maps, measured_kspace, sample_mask,
    caipi_steps, band_order, weight_in, weight_mid, weight_out,
):
    positions, group_slices, _, row_count, columns = current_image.shape
    local_slices = positions * group_slices
    band, bands = lax.axis_index("band"), lax.axis_size("band")
    own = current_image.astype(jnp.bfloat16).reshape(local_slices, 2 * row_count, columns)
    routes = [[(i, i ^ x) for i in range(bands)] for x in range(1, 4)]
    images = [own] + [lax.ppermute(own, "band", route) for route in routes]
    prepared = preparation(step_size, coil_maps, caipi_steps, band_order)

    odd = band % 2 == 1
    under = jnp.where(odd, images[1], images[3])[local_slices - 3 :]
    over = jnp.where(odd, images[3], images[1])[:3]
    under = jnp.where(band == 0, jnp.zeros_like(under), under)
    over = jnp.where(band == bands - 1, jnp.zeros_like(over), over)
    tall = jnp.concatenate([under, own, over], axis=0)
    tall = tall.reshape(-1, 2, row_count, columns)
    below, above = exchanged_rows(tall, 3)
    sums = partial_consistency(images, prepared, measured_kspace, sample_mask)
    sums, below, above = lax.optimization_barrier((sums, below, above))
    arrived = [lax.ppermute(part, "band", route) for part, route in zip(sums[1:], routes)]
    field = jnp.concatenate([below, tall, above, jnp.zeros_like(above[:, :, :2])], axis=2)
    windows = jnp.stack(
        [field[:, :, 4 * g : 4 * g + 8].reshape(-1, columns) for g in range(2)], axis=0
    )
    base = stepped_without_data(
        windows, prepared[1], current_image, langevin_noise, weight_in, weight_mid, weight_out
    )
    total = sums[0].astype(jnp.float32)
    for part in arrived:
        total = total + part.astype(jnp.float32)
    return base - total.reshape(base.shape)


def solution(mesh):
    band5 = P("band", None, None, "slab", None)
    in_specs = (
        band5,
        band5,
        P(),
        P(None, None, "band", None, "slab", None),
        P(None, "band", None, "slab", None),
        P(), P(), P(), P(), P(), P(),
    )
    return jax.shard_map(
        per_device, mesh=mesh, in_specs=in_specs, out_specs=band5, check_vma=False
    )
```

```python
import functools
import math

import jax
import jax.numpy as jnp
from jax import lax
from jax.experimental import pallas as pl
from jax.experimental.pallas import tpu as pltpu
from jax.sharding import PartitionSpec as P


def exchanged_rows(tall, width):
    count = lax.axis_size("slab")
    odd = lax.axis_index("slab") % 2 == 1
    head, tail = tall[:, :, :width, :], tall[:, :, tall.shape[2] - width :, :]
    arrived = []
    for first in range(2):
        route = []
        for i in range(first, count - 1, 2):
            route += [(i, i + 1), (i + 1, i)]
        sent = jnp.where(odd, head, tail) if first == 0 else jnp.where(odd, tail, head)
        arrived.append(lax.ppermute(sent, "slab", route))
    below = jnp.where(odd, arrived[0], arrived[1])
    above = jnp.where(odd, arrived[1], arrived[0])
    return below, above


def in_hbm(*arrays):
    return [pltpu.with_memory_space_constraint(array, pltpu.HBM) for array in arrays]


def series(square, coefficients):
    total = jnp.full_like(square, coefficients[-1])
    for coefficient in coefficients[-2::-1]:
        total = total * square + coefficient
    return total


def fill_factors(factors_ref):
    rows, columns = factors_ref.shape
    near = 16
    count = columns // near
    half = count + near
    row = lax.broadcasted_iota(jnp.int32, (half, columns), 0)
    row = jnp.where(row < count, near * row, row - count).astype(jnp.float32)
    phase = row * lax.broadcasted_iota(jnp.int32, (half, columns), 1).astype(jnp.float32)
    phase = phase - columns * jnp.floor(phase * (1.0 / columns) + 0.5)
    angle = phase * (math.pi / columns)
    square = angle * angle
    sine = angle * series(square, [(-1.0) ** k / math.factorial(2 * k + 1) for k in range(7)])
    cosine = series(square, [(-1.0) ** k / math.factorial(2 * k) for k in range(8)])
    scale = 1.0 / math.sqrt(columns)
    waves = (1.0 - 2.0 * sine * sine, 2.0 * sine * cosine)
    for part, wave in enumerate(waves):
        begin = count * part
        factors_ref[begin : begin + count, :] = scale * wave[:count]
        begin = 2 * count + near * part
        factors_ref[begin : begin + near, :] = wave[count:]


def build_tables(factors_ref, high_ref, low_ref):
    columns = factors_ref.shape[1]
    near = 16
    count = columns // near
    near_cos = factors_ref[2 * count : 2 * count + near, :]
    near_sin = factors_ref[2 * count + near :, :]
    for a in range(count):
        far_cos = factors_ref[a : a + 1, :]
        far_sin = factors_ref[count + a : count + a + 1, :]
        tables = (far_cos * near_cos - far_sin * near_sin, far_sin * near_cos + far_cos * near_sin)
        rows = slice(near * a, near * (a + 1))
        for part, table in enumerate(tables):
            high = table.astype(jnp.bfloat16)
            lanes = slice(columns * part, columns * (part + 1))
            high_ref[rows, lanes] = high
            low_ref[rows, lanes] = (table - high.astype(jnp.float32)).astype(jnp.bfloat16)


def moved_right(value):
    tiles = value.shape[-1] // 128
    moved = [pltpu.roll(value[:, 128 * j : 128 * (j + 1)], 1, 1) for j in range(tiles)]
    edge = lax.broadcasted_iota(jnp.int32, moved[0].shape, 1) == 0
    return jnp.concatenate(
        [jnp.where(edge, moved[j - 1] if j > 0 else 0.0, moved[j]) for j in range(tiles)], axis=1
    )


def moved_left(value):
    tiles = value.shape[-1] // 128
    moved = [pltpu.roll(value[:, 128 * j : 128 * (j + 1)], 127, 1) for j in range(tiles)]
    edge = lax.broadcasted_iota(jnp.int32, moved[0].shape, 1) == 127
    return jnp.concatenate(
        [
            jnp.where(edge, moved[j + 1] if j < tiles - 1 else 0.0, moved[j])
            for j in range(tiles)
        ],
        axis=1,
    )


def silu(value):
    return value * pl.reciprocal(1.0 + jnp.exp(-value), approx=True)


def table_product(source, high_ref, low_ref):
    rows = source.shape[0]
    high = source.astype(jnp.bfloat16)
    low = (source - high.astype(jnp.float32)).astype(jnp.bfloat16)
    both = jnp.dot(
        jnp.concatenate([high, low], axis=0), high_ref[...], preferred_element_type=jnp.float32
    )
    rest = jnp.dot(high, low_ref[...], preferred_element_type=jnp.float32)
    return both[:rows] + both[rows:] + rest


def halves_swapped(value):
    return pltpu.roll(value, 4, value.ndim - 2)


def upper_half(value):
    return lax.broadcasted_iota(jnp.int32, value.shape, value.ndim - 2) < 4


def signed_swap(value, top, bottom):
    sign = jnp.where(upper_half(value), top, bottom)
    return sign * halves_swapped(value)


def stacked_parts(value):
    return jnp.concatenate([value[..., 0, :, :], value[..., 1, :, :]], axis=-2)


def turned_tiles(value, shift, store):
    tiles = value.shape[-1] // 128
    whole, part = shift // 128, lax.rem(shift, 128)
    moved = [
        pltpu.roll(value[..., 128 * j : 128 * (j + 1)], part, value.ndim - 1) for j in range(tiles)
    ]
    lane = lax.broadcasted_iota(jnp.int32, moved[0].shape, value.ndim - 1)
    for j in range(tiles):
        store(lax.rem(j + whole, tiles), jnp.where(lane < part, moved[j - 1], moved[j]))


def fill_weights(first_raw, mid_raw, last_raw, first_sum, last_sum, first_ref, wide_ref, last_ref):
    channels = mid_raw.shape[-1]
    two = 2 * channels
    first_sum[...] = jnp.zeros_like(first_sum)
    last_sum[...] = jnp.zeros_like(last_sum)
    for d in range(3):
        for u in range(3):
            for t in range(3):
                block = first_raw[d, u, t].astype(jnp.float32)
                for i in range(2):
                    for r in range(4):
                        row = (t * 3 + d) * 16 + i * 8 + u + r
                        first_sum[row : row + 1, r * channels : (r + 1) * channels] = block[
                            i : i + 1
                        ]
                block = last_raw[d, u, t].astype(jnp.float32)
                for o in range(2):
                    for r in range(4):
                        row = (d * 3 + t) * 8 + o * 4 + r
                        col = (r + u) * channels
                        last_sum[row : row + 1, col : col + channels] = block[o : o + 1]
    first_ref[...] = first_sum[...].T[:, : first_ref.shape[1]].astype(jnp.bfloat16)
    last_ref[...] = last_sum[...].astype(jnp.bfloat16)
    for t in range(3):
        for r in range(2):
            row = (t * 2 + r) * channels
            for d in range(3):
                for pair in range(2):
                    blocks = []
                    for q in (2 * pair, 2 * pair + 1):
                        if 0 <= q - r <= 2:
                            blocks.append(mid_raw[d, q - r, t])
                        else:
                            blocks.append(jnp.zeros((channels, channels), jnp.bfloat16))
                    col = (d * 4 + 2 * pair) * channels
                    wide_ref[row : row + channels, col : col + two] = jnp.concatenate(
                        blocks, axis=1
                    )


def preparation_kernel(
    size_ref, steps_hbm, order_hbm, coil_hbm,
    turned_ref, scalars_ref, high_ref, low_ref,
    steps_ref, order_ref, coil_ref, factors_ref, sems, coil_sems,
):
    all_positions, slices, coils, _, rows, columns = coil_ref.shape
    unit = columns // 8
    block = coils * 2 * rows
    copies = [
        pltpu.make_async_copy(steps_hbm, steps_ref, sems.at[0]),
        pltpu.make_async_copy(order_hbm, order_ref, sems.at[1]),
    ] + [
        pltpu.make_async_copy(coil_hbm.at[g], coil_ref.at[g], coil_sems.at[g])
        for g in range(all_positions)
    ]
    for copy in copies:
        copy.start()
    fill_factors(factors_ref)
    build_tables(factors_ref, high_ref, low_ref)
    scalars_ref[all_positions:, :] = jnp.full(
        (scalars_ref.shape[0] - all_positions, 128), size_ref[0], jnp.float32
    )
    for copy in copies:
        copy.wait()
    for g in range(all_positions):
        shift = steps_ref[order_ref[g]] * unit
        scalars_ref[g : g + 1, :] = jnp.full((1, 128), shift, jnp.int32).astype(jnp.float32)
        for s in range(slices):

            def store_coil(j, value, s=s, g=g):
                turned_ref[j, g, s] = value.reshape(block, 128).astype(jnp.bfloat16)

            turned_tiles(stacked_parts(coil_ref[g, s].astype(jnp.float32)), shift, store_coil)


def preparation(step_size, coil_maps, caipi_steps, band_order):
    all_positions, slices, coils, _, rows, columns = coil_maps.shape
    f32, bf16 = jnp.float32, jnp.bfloat16
    hbm = pl.BlockSpec(memory_space=pltpu.HBM)
    vmem = pl.BlockSpec(memory_space=pltpu.VMEM)
    turned_shape = (columns // 128, all_positions, slices, coils * 2 * rows, 128)
    return pl.pallas_call(
        preparation_kernel,
        out_shape=(
            jax.ShapeDtypeStruct(turned_shape, bf16),
            jax.ShapeDtypeStruct((2 * all_positions, 128), f32),
            jax.ShapeDtypeStruct((columns, 2 * columns), bf16),
            jax.ShapeDtypeStruct((columns, 2 * columns), bf16),
        ),
        in_specs=[pl.BlockSpec(memory_space=pltpu.SMEM)] + [hbm] * 3,
        out_specs=(vmem,) * 4,
        scratch_shapes=[
            pltpu.SMEM(caipi_steps.shape, jnp.int32),
            pltpu.SMEM(band_order.shape, jnp.int32),
            pltpu.VMEM(coil_maps.shape, bf16),
            pltpu.VMEM((2 * (columns // 16 + 16), columns), f32),
            pltpu.SemaphoreType.DMA((2,)),
            pltpu.SemaphoreType.DMA((all_positions,)),
        ],
        compiler_params=pltpu.CompilerParams(vmem_limit_bytes=40 * 2**20),
        cost_estimate=pl.CostEstimate(
            flops=4 * 10**9, bytes_accessed=4 * 10**6, transcendentals=0
        ),
    )(step_size, *in_hbm(caipi_steps, band_order, coil_maps))


def consistency_kernel(
    own_ref, one_ref, two_ref, three_ref, turned_ref, scalars_ref, high_ref, low_ref,
    kspace_hbm, mask_hbm,
    own_out, one_out, two_out, three_out,
    kspace_ref, mask_ref, real_ref, imag_ref, field_ref, swap_ref, sum_ref, sems,
):
    tiles, all_positions, slices, _, _ = turned_ref.shape
    _, coils, _, rows, columns = kspace_ref.shape
    doubled, positions = 2 * rows, all_positions // 4
    copies = [
        pltpu.make_async_copy(kspace_hbm, kspace_ref, sems.at[0]),
        pltpu.make_async_copy(mask_hbm, mask_ref, sems.at[1]),
    ]
    for copy in copies:
        copy.start()
    size = scalars_ref[all_positions : all_positions + 1, :]
    owners = []
    for x in range(4):
        first = lax.bitwise_xor(lax.axis_index("band"), jnp.int32(x)) * positions
        for p in range(positions):
            shift = jnp.max(scalars_ref[pl.ds(first + p, 1), :]).astype(jnp.int32)
            owners.append((x, p, first + p, shift))

    def coil_of(j, g, s):
        return turned_ref[j, g, s].astype(jnp.float32).reshape(coils, doubled, 128)

    images = (own_ref, one_ref, two_ref, three_ref)
    for k, (x, p, g, shift) in enumerate(owners):

        def store_image(j, value, k=k):
            other = halves_swapped(value)
            top = upper_half(value)
            real_ref[j, k] = jnp.where(top, value, other)
            imag_ref[j, k] = jnp.where(top, other, value)

        image = images[x][p * slices : (p + 1) * slices].astype(jnp.float32)
        turned_tiles(image, shift, store_image)
    for copy in copies:
        copy.wait()

    block = coils * doubled
    halves = [range(0, slices // 2), range(slices // 2, slices)]

    def rows_of(half):
        return slice(half[0] * block, (half[-1] + 1) * block)

    def collapse(half):
        for j in range(tiles):
            for s in half:
                with_real = jnp.zeros((coils, doubled, 128), jnp.float32)
                with_imag = jnp.zeros((coils, doubled, 128), jnp.float32)
                for k, (_, _, g, _) in enumerate(owners):
                    coil = coil_of(j, g, s)
                    with_real += coil * real_ref[j, k, s]
                    with_imag += coil * imag_ref[j, k, s]
                total = with_real + signed_swap(with_imag, -1.0, 1.0)
                field_ref[s * block : (s + 1) * block, 128 * j : 128 * (j + 1)] = total.reshape(
                    block, 128
                )

    def transformed(source, half, top, bottom):
        product = table_product(source, high_ref, low_ref)
        grouped = (len(half), coils, doubled, columns)
        with_cos = product[:, :columns].reshape(grouped)
        with_sin = product[:, columns:].reshape(grouped)
        return with_cos + signed_swap(with_sin, top, bottom)

    def project(half):
        spectrum = transformed(field_ref[rows_of(half)], half, 1.0, -1.0)
        keep = mask_ref[...].astype(jnp.float32)[half[0] : half[-1] + 1]
        keep = keep.reshape(len(half), 1, 1, columns)
        data = stacked_parts(kspace_ref[half[0] : half[-1] + 1])
        residual = (keep * (spectrum - data)).reshape(len(half) * block, columns)
        back = transformed(residual, half, -1.0, 1.0)
        field_ref[rows_of(half)] = back.reshape(len(half) * block, columns)
        swap_ref[rows_of(half)] = halves_swapped(back).reshape(len(half) * block, columns)

    def combine(half):
        for j in range(tiles):
            for s in half:
                place = (slice(s * block, (s + 1) * block), slice(128 * j, 128 * (j + 1)))
                field = field_ref[place].reshape(coils, doubled, 128)
                swapped = swap_ref[place].reshape(coils, doubled, 128)
                for k, (_, _, g, _) in enumerate(owners):
                    coil = coil_of(j, g, s)
                    straight = jnp.sum(coil * field, axis=0)
                    crossed = jnp.sum(coil * swapped, axis=0)
                    straight = straight + halves_swapped(straight)
                    crossed = halves_swapped(crossed) - crossed
                    sum_ref[k, s, :, 128 * j : 128 * (j + 1)] = size * jnp.where(
                        upper_half(straight), straight, crossed
                    )

    for half in halves:
        collapse(half)
    for half in halves:
        project(half)
    for half in halves:
        combine(half)

    outs = (own_out, one_out, two_out, three_out)
    for k, (x, p, _, shift) in enumerate(owners):
        back_shift = lax.rem(columns - shift, columns)
        outs[x][p] = pltpu.roll(sum_ref[k], back_shift, 2).astype(jnp.bfloat16)


def partial_consistency(images, prepared, measured_kspace, sample_mask):
    tiles, all_positions, slices, _, _ = prepared[0].shape
    _, coils, _, rows, columns = measured_kspace.shape
    doubled = 2 * rows
    total = slices * coils * doubled
    hbm = pl.BlockSpec(memory_space=pltpu.HBM)
    vmem = pl.BlockSpec(memory_space=pltpu.VMEM)
    image_shape = (tiles, all_positions, slices, doubled, 128)
    part = jax.ShapeDtypeStruct((all_positions // 4, slices, doubled, columns), jnp.bfloat16)
    return pl.pallas_call(
        consistency_kernel,
        out_shape=(part,) * 4,
        in_specs=[vmem] * 8 + [hbm] * 2,
        out_specs=(vmem,) * 4,
        scratch_shapes=[
            pltpu.VMEM(measured_kspace.shape, jnp.float32),
            pltpu.VMEM(sample_mask.shape, jnp.int32),
            pltpu.VMEM(image_shape, jnp.float32),
            pltpu.VMEM(image_shape, jnp.float32),
            pltpu.VMEM((total, columns), jnp.float32),
            pltpu.VMEM((total, columns), jnp.float32),
            pltpu.VMEM((all_positions, slices, doubled, columns), jnp.float32),
            pltpu.SemaphoreType.DMA((2,)),
        ],
        compiler_params=pltpu.CompilerParams(vmem_limit_bytes=40 * 2**20),
        cost_estimate=pl.CostEstimate(
            flops=4 * 10**9, bytes_accessed=4 * 10**6, transcendentals=0
        ),
    )(*images, *prepared, *in_hbm(measured_kspace, sample_mask))


def network_kernel(
    window_ref, scalars_ref, first_hbm, mid_hbm, last_hbm, image_hbm, noise_hbm,
    out_ref,
    first_raw, mid_raw, last_raw, image_ref, noise_ref,
    first_sum, last_sum, first_ref, wide_ref, last_ref, taps_ref, f1_ref, f2_ref, part_a, part_b, score_ref, sems,
):
    channels = mid_raw.shape[-1]
    out_slices, _, rows, columns = out_ref.shape
    slices1, slices2 = out_slices + 4, out_slices + 2
    pairs = (
        (first_hbm, first_raw), (mid_hbm, mid_raw), (last_hbm, last_raw),
        (image_hbm, image_ref), (noise_hbm, noise_ref),
    )
    copies = [pltpu.make_async_copy(src, dst, sems.at[i]) for i, (src, dst) in enumerate(pairs)]
    for copy in copies:
        copy.start()

    def inside(axis, end):
        edge = lax.axis_size(axis) - 1 if end else 0
        return jnp.where(lax.axis_index(axis) == edge, 0.0, 1.0).astype(jnp.float32)

    low_slice, high_slice = inside("band", False), inside("band", True)
    low_row, high_row = inside("slab", False), inside("slab", True)
    four, two = 4 * channels, 2 * channels

    for g in range(2):
        base = window_ref[g].astype(jnp.float32)
        taps_ref[g, 0] = moved_right(base).astype(jnp.bfloat16)
        taps_ref[g, 1] = window_ref[g]
        taps_ref[g, 2] = moved_left(base).astype(jnp.bfloat16)

    for copy in copies[:3]:
        copy.wait()
    fill_weights(
        first_raw, mid_raw, last_raw, first_sum, last_sum, first_ref, wide_ref, last_ref
    )

    def first_layer(z):
        source = jnp.concatenate(
            [
                jnp.concatenate([taps_ref[g, t, 16 * z : 16 * z + 48, :] for t in range(3)], axis=0)
                for g in range(2)
            ],
            axis=1,
        )
        half = jnp.dot(first_ref[...], source, preferred_element_type=jnp.float32)
        for r in range(8):
            begin = (r % 4) * channels
            first = columns * (r // 4)
            value = silu(half[begin : begin + channels, first : first + columns])
            factors = []
            if z < 2:
                factors.append(low_slice)
            if z >= slices1 - 2:
                factors.append(high_slice)
            if r < 2:
                factors.append(low_row)
            if r >= 6:
                factors.append(high_row)
            for factor in factors:
                value = value * factor
            f1_ref[z, r * channels : (r + 1) * channels, :] = value.astype(jnp.bfloat16)

    def second_product(z, pair, part_ref):
        source = jnp.concatenate(
            [
                f1_ref[z + a : z + a + 3, two * pair : two * pair + four, :].reshape(
                    3 * four, columns
                )
                for a in range(2)
            ],
            axis=1,
        )
        part_ref[...] = jnp.dot(wide_ref[...], source, preferred_element_type=jnp.float32)

    def second_layer(z, pair, part_ref):
        for a in range(2):
            first = columns * a
            for r in range(2):
                row = r * channels
                half = (
                    moved_right(part_ref[row : row + channels, first : first + columns])
                    + part_ref[two + row : two + row + channels, first : first + columns]
                    + moved_left(
                        part_ref[four + row : four + row + channels, first : first + columns]
                    )
                )
                value = silu(half)
                factors = []
                if z + a == 0:
                    factors.append(low_slice)
                if z + a == slices2 - 1:
                    factors.append(high_slice)
                if pair == 0 and r == 0:
                    factors.append(low_row)
                if pair == 2 and r == 1:
                    factors.append(high_row)
                for factor in factors:
                    value = value * factor
                place = two * pair + r * channels
                f2_ref[z + a, place : place + channels, :] = value.astype(jnp.bfloat16)

    def third_product(z):
        source = jnp.concatenate([f2_ref[z], f2_ref[z + 1]], axis=1)
        score_ref[z // 2] = jnp.dot(last_ref[...], source, preferred_element_type=jnp.float32)

    for z in range(4):
        first_layer(z)
    waiting = None
    parts = (part_a, part_b)
    count = 0
    for z in range(0, slices2, 2):
        for pair in range(3):
            second_product(z, pair, parts[count % 2])
            if pair < 2 and z + 4 + pair < slices1:
                first_layer(z + 4 + pair)
            if waiting is not None:
                second_layer(*waiting)
                if waiting[1] == 2:
                    third_product(waiting[0])
            waiting = (z, pair, parts[count % 2])
            count += 1
    second_layer(*waiting)
    third_product(waiting[0])

    for copy in copies[3:]:
        copy.wait()
    size = scalars_ref[scalars_ref.shape[0] - 1 :, :]
    size = jnp.concatenate([size] * (columns // 128), axis=1)
    noise_scale = jnp.sqrt(2.0 * size)
    for z in range(out_slices):
        taps = []
        for t in range(3):
            total = None
            for d in range(3):
                row, first = (3 * d + t) * 8, columns * ((z + d) % 2)
                piece = score_ref[(z + d) // 2, row : row + 8, first : first + columns]
                total = piece if total is None else total + piece
            taps.append(total)
        score = size * (moved_right(taps[0]) + taps[1] + moved_left(taps[2]))
        for part in range(2):
            out_ref[z, part] = (
                image_ref[z, part]
                + score[part * rows : (part + 1) * rows]
                + noise_scale * noise_ref[z, part]
            )


def stepped_without_data(
    windows, scalars, current_image, langevin_noise, weight_in, weight_mid, weight_out
):
    channels = weight_mid.shape[0]
    first = jnp.transpose(weight_in, (2, 3, 4, 1, 0))
    mid = jnp.transpose(weight_mid, (2, 3, 4, 0, 1))
    last = jnp.transpose(weight_out, (2, 3, 4, 0, 1))
    slices0, columns = windows.shape[1] // 16, windows.shape[-1]
    out_slices = slices0 - 6
    local = (out_slices,) + current_image.shape[2:]
    hbm = pl.BlockSpec(memory_space=pltpu.HBM)
    vmem = pl.BlockSpec(memory_space=pltpu.VMEM)
    return pl.pallas_call(
        network_kernel,
        out_shape=jax.ShapeDtypeStruct(local, jnp.float32),
        in_specs=[vmem] * 2 + [hbm] * 5,
        out_specs=vmem,
        scratch_shapes=[
            pltpu.VMEM(first.shape, jnp.bfloat16),
            pltpu.VMEM(mid.shape, jnp.bfloat16),
            pltpu.VMEM(last.shape, jnp.bfloat16),
            pltpu.VMEM(local, jnp.float32),
            pltpu.VMEM(local, jnp.float32),
            pltpu.VMEM((256, 4 * channels), jnp.float32),
            pltpu.VMEM((72, 6 * channels), jnp.float32),
            pltpu.VMEM((4 * channels, 144), jnp.bfloat16),
            pltpu.VMEM((6 * channels, 12 * channels), jnp.bfloat16),
            pltpu.VMEM((72, 6 * channels), jnp.bfloat16),
            pltpu.VMEM((2, 3, slices0 * 16, columns), jnp.bfloat16),
            pltpu.VMEM((out_slices + 4, 8 * channels, columns), jnp.bfloat16),
            pltpu.VMEM((out_slices + 2, 6 * channels, columns), jnp.bfloat16),
            pltpu.VMEM((6 * channels, 2 * columns), jnp.float32),
            pltpu.VMEM((6 * channels, 2 * columns), jnp.float32),
            pltpu.VMEM((out_slices // 2 + 1, 72, 2 * columns), jnp.float32),
            pltpu.SemaphoreType.DMA((5,)),
        ],
        compiler_params=pltpu.CompilerParams(vmem_limit_bytes=40 * 2**20),
        cost_estimate=pl.CostEstimate(
            flops=10**10, bytes_accessed=2 * 10**6, transcendentals=4 * 10**6
        ),
    )(
        windows, scalars,
        *in_hbm(first, mid, last, current_image.reshape(local), langevin_noise.reshape(local)),
    ).reshape(current_image.shape)


def per_device(
    current_image, langevin_noise, step_size, coil_maps, measured_kspace, sample_mask,
    caipi_steps, band_order, weight_in, weight_mid, weight_out,
):
    positions, group_slices, _, row_count, columns = current_image.shape
    local_slices = positions * group_slices
    band, bands = lax.axis_index("band"), lax.axis_size("band")
    own = current_image.astype(jnp.bfloat16).reshape(local_slices, 2 * row_count, columns)
    routes = [[(i, i ^ x) for i in range(bands)] for x in range(1, 4)]
    images = [own] + [lax.ppermute(own, "band", route) for route in routes]
    prepared = preparation(step_size, coil_maps, caipi_steps, band_order)

    odd = band % 2 == 1
    under = jnp.where(odd, images[1], images[3])[local_slices - 3 :]
    over = jnp.where(odd, images[3], images[1])[:3]
    under = jnp.where(band == 0, jnp.zeros_like(under), under)
    over = jnp.where(band == bands - 1, jnp.zeros_like(over), over)
    tall = jnp.concatenate([under, own, over], axis=0)
    tall = tall.reshape(-1, 2, row_count, columns)
    below, above = exchanged_rows(tall, 3)
    sums = partial_consistency(images, prepared, measured_kspace, sample_mask)
    sums, below, above = lax.optimization_barrier((sums, below, above))
    arrived = [lax.ppermute(part, "band", route) for part, route in zip(sums[1:], routes)]
    field = jnp.concatenate([below, tall, above, jnp.zeros_like(above[:, :, :2])], axis=2)
    windows = jnp.stack(
        [field[:, :, 4 * g : 4 * g + 8].reshape(-1, columns) for g in range(2)], axis=0
    )
    base = stepped_without_data(
        windows, prepared[1], current_image, langevin_noise, weight_in, weight_mid, weight_out
    )
    total = sums[0].astype(jnp.float32)
    for part in arrived:
        total = total + part.astype(jnp.float32)
    return base - total.reshape(base.shape)


def solution(mesh):
    band5 = P("band", None, None, "slab", None)
    in_specs = (
        band5,
        band5,
        P(),
        P(None, None, "band", None, "slab", None),
        P(None, "band", None, "slab", None),
        P(), P(), P(), P(), P(), P(),
    )
    return jax.shard_map(
        per_device, mesh=mesh, in_specs=in_specs, out_specs=band5, check_vma=False
    )
```

```python
import functools
import math

import jax
import jax.numpy as jnp
from jax import lax
from jax.experimental import pallas as pl
from jax.experimental.pallas import tpu as pltpu
from jax.sharding import PartitionSpec as P


def exchanged_rows(tall, width):
    count = lax.axis_size("slab")
    odd = lax.axis_index("slab") % 2 == 1
    head, tail = tall[:, :, :width, :], tall[:, :, tall.shape[2] - width :, :]
    arrived = []
    for first in range(2):
        route = []
        for i in range(first, count - 1, 2):
            route += [(i, i + 1), (i + 1, i)]
        sent = jnp.where(odd, head, tail) if first == 0 else jnp.where(odd, tail, head)
        arrived.append(lax.ppermute(sent, "slab", route))
    below = jnp.where(odd, arrived[0], arrived[1])
    above = jnp.where(odd, arrived[1], arrived[0])
    return below, above


def in_hbm(*arrays):
    return [pltpu.with_memory_space_constraint(array, pltpu.HBM) for array in arrays]


def series(square, coefficients):
    total = jnp.full_like(square, coefficients[-1])
    for coefficient in coefficients[-2::-1]:
        total = total * square + coefficient
    return total


def fill_factors(factors_ref):
    rows, columns = factors_ref.shape
    near = 16
    count = columns // near
    half = count + near
    row = lax.broadcasted_iota(jnp.int32, (half, columns), 0)
    row = jnp.where(row < count, near * row, row - count).astype(jnp.float32)
    phase = row * lax.broadcasted_iota(jnp.int32, (half, columns), 1).astype(jnp.float32)
    phase = phase - columns * jnp.floor(phase * (1.0 / columns) + 0.5)
    angle = phase * (math.pi / columns)
    square = angle * angle
    sine = angle * series(square, [(-1.0) ** k / math.factorial(2 * k + 1) for k in range(7)])
    cosine = series(square, [(-1.0) ** k / math.factorial(2 * k) for k in range(8)])
    scale = 1.0 / math.sqrt(columns)
    waves = (1.0 - 2.0 * sine * sine, 2.0 * sine * cosine)
    for part, wave in enumerate(waves):
        begin = count * part
        factors_ref[begin : begin + count, :] = scale * wave[:count]
        begin = 2 * count + near * part
        factors_ref[begin : begin + near, :] = wave[count:]


def build_tables(factors_ref, high_ref, low_ref):
    columns = factors_ref.shape[1]
    near = 16
    count = columns // near
    near_cos = factors_ref[2 * count : 2 * count + near, :]
    near_sin = factors_ref[2 * count + near :, :]
    for a in range(count):
        far_cos = factors_ref[a : a + 1, :]
        far_sin = factors_ref[count + a : count + a + 1, :]
        tables = (far_cos * near_cos - far_sin * near_sin, far_sin * near_cos + far_cos * near_sin)
        rows = slice(near * a, near * (a + 1))
        for part, table in enumerate(tables):
            high = table.astype(jnp.bfloat16)
            lanes = slice(columns * part, columns * (part + 1))
            high_ref[rows, lanes] = high
            low_ref[rows, lanes] = (table - high.astype(jnp.float32)).astype(jnp.bfloat16)


def moved_right(value):
    tiles = value.shape[-1] // 128
    moved = [pltpu.roll(value[:, 128 * j : 128 * (j + 1)], 1, 1) for j in range(tiles)]
    edge = lax.broadcasted_iota(jnp.int32, moved[0].shape, 1) == 0
    return jnp.concatenate(
        [jnp.where(edge, moved[j - 1] if j > 0 else 0.0, moved[j]) for j in range(tiles)], axis=1
    )


def moved_left(value):
    tiles = value.shape[-1] // 128
    moved = [pltpu.roll(value[:, 128 * j : 128 * (j + 1)], 127, 1) for j in range(tiles)]
    edge = lax.broadcasted_iota(jnp.int32, moved[0].shape, 1) == 127
    return jnp.concatenate(
        [
            jnp.where(edge, moved[j + 1] if j < tiles - 1 else 0.0, moved[j])
            for j in range(tiles)
        ],
        axis=1,
    )


def half_silu(half):
    return half + half * jnp.tanh(half)


def table_product(source, high_ref, low_ref):
    rows = source.shape[0]
    high = source.astype(jnp.bfloat16)
    low = (source - high.astype(jnp.float32)).astype(jnp.bfloat16)
    both = jnp.dot(
        jnp.concatenate([high, low], axis=0), high_ref[...], preferred_element_type=jnp.float32
    )
    rest = jnp.dot(high, low_ref[...], preferred_element_type=jnp.float32)
    return both[:rows] + both[rows:] + rest


def halves_swapped(value):
    return pltpu.roll(value, 4, value.ndim - 2)


def upper_half(value):
    return lax.broadcasted_iota(jnp.int32, value.shape, value.ndim - 2) < 4


def signed_swap(value, top, bottom):
    sign = jnp.where(upper_half(value), top, bottom)
    return sign * halves_swapped(value)


def stacked_parts(value):
    return jnp.concatenate([value[..., 0, :, :], value[..., 1, :, :]], axis=-2)


def turned_tiles(value, shift, store):
    tiles = value.shape[-1] // 128
    whole, part = shift // 128, lax.rem(shift, 128)
    moved = [
        pltpu.roll(value[..., 128 * j : 128 * (j + 1)], part, value.ndim - 1) for j in range(tiles)
    ]
    lane = lax.broadcasted_iota(jnp.int32, moved[0].shape, value.ndim - 1)
    for j in range(tiles):
        store(lax.rem(j + whole, tiles), jnp.where(lane < part, moved[j - 1], moved[j]))


def fill_first(first_raw, first_sum, first_ref):
    channels = first_raw.shape[-1]
    first_sum[...] = jnp.zeros_like(first_sum)
    for d in range(3):
        for u in range(3):
            for t in range(3):
                block = first_raw[d, u, t].astype(jnp.float32) * 0.5
                for i in range(2):
                    for r in range(4):
                        row = (t * 3 + d) * 16 + i * 8 + u + r
                        first_sum[row : row + 1, r * channels : (r + 1) * channels] = block[
                            i : i + 1
                        ]
    first_ref[...] = first_sum[...].T[:, : first_ref.shape[1]].astype(jnp.bfloat16)


def fill_others(mid_raw, last_raw, last_sum, wide_ref, last_ref):
    channels = mid_raw.shape[-1]
    two = 2 * channels
    last_sum[...] = jnp.zeros_like(last_sum)
    for d in range(3):
        for u in range(3):
            for t in range(3):
                block = last_raw[d, u, t].astype(jnp.float32)
                for o in range(2):
                    for r in range(4):
                        row = (d * 3 + t) * 8 + o * 4 + r
                        col = (r + u) * channels
                        last_sum[row : row + 1, col : col + channels] = block[o : o + 1]
    last_ref[...] = last_sum[...].astype(jnp.bfloat16)
    half_weight = jnp.bfloat16(0.5)
    for t in range(3):
        for r in range(2):
            row = (t * 2 + r) * channels
            for d in range(3):
                for pair in range(2):
                    blocks = []
                    for q in (2 * pair, 2 * pair + 1):
                        if 0 <= q - r <= 2:
                            blocks.append(mid_raw[d, q - r, t] * half_weight)
                        else:
                            blocks.append(jnp.zeros((channels, channels), jnp.bfloat16))
                    col = (d * 4 + 2 * pair) * channels
                    wide_ref[row : row + channels, col : col + two] = jnp.concatenate(
                        blocks, axis=1
                    )


def preparation_kernel(
    size_ref, steps_hbm, order_hbm, coil_hbm,
    turned_ref, scalars_ref, high_ref, low_ref,
    steps_ref, order_ref, coil_ref, factors_ref, sems, coil_sems,
):
    all_positions, slices, coils, _, rows, columns = coil_ref.shape
    unit = columns // 8
    block = coils * 2 * rows
    copies = [
        pltpu.make_async_copy(steps_hbm, steps_ref, sems.at[0]),
        pltpu.make_async_copy(order_hbm, order_ref, sems.at[1]),
    ] + [
        pltpu.make_async_copy(coil_hbm.at[g], coil_ref.at[g], coil_sems.at[g])
        for g in range(all_positions)
    ]
    for copy in copies:
        copy.start()
    fill_factors(factors_ref)
    build_tables(factors_ref, high_ref, low_ref)
    scalars_ref[all_positions:, :] = jnp.full(
        (scalars_ref.shape[0] - all_positions, 128), size_ref[0], jnp.float32
    )
    for copy in copies:
        copy.wait()
    for g in range(all_positions):
        shift = steps_ref[order_ref[g]] * unit
        scalars_ref[g : g + 1, :] = jnp.full((1, 128), shift, jnp.int32).astype(jnp.float32)
        for s in range(slices):

            def store_coil(j, value, s=s, g=g):
                turned_ref[j, g, s] = value.reshape(block, 128).astype(jnp.bfloat16)

            turned_tiles(stacked_parts(coil_ref[g, s].astype(jnp.float32)), shift, store_coil)


def preparation(step_size, coil_maps, caipi_steps, band_order):
    all_positions, slices, coils, _, rows, columns = coil_maps.shape
    f32, bf16 = jnp.float32, jnp.bfloat16
    hbm = pl.BlockSpec(memory_space=pltpu.HBM)
    vmem = pl.BlockSpec(memory_space=pltpu.VMEM)
    turned_shape = (columns // 128, all_positions, slices, coils * 2 * rows, 128)
    return pl.pallas_call(
        preparation_kernel,
        out_shape=(
            jax.ShapeDtypeStruct(turned_shape, bf16),
            jax.ShapeDtypeStruct((2 * all_positions, 128), f32),
            jax.ShapeDtypeStruct((columns, 2 * columns), bf16),
            jax.ShapeDtypeStruct((columns, 2 * columns), bf16),
        ),
        in_specs=[pl.BlockSpec(memory_space=pltpu.SMEM)] + [hbm] * 3,
        out_specs=(vmem,) * 4,
        scratch_shapes=[
            pltpu.SMEM(caipi_steps.shape, jnp.int32),
            pltpu.SMEM(band_order.shape, jnp.int32),
            pltpu.VMEM(coil_maps.shape, bf16),
            pltpu.VMEM((2 * (columns // 16 + 16), columns), f32),
            pltpu.SemaphoreType.DMA((2,)),
            pltpu.SemaphoreType.DMA((all_positions,)),
        ],
        compiler_params=pltpu.CompilerParams(vmem_limit_bytes=40 * 2**20),
        cost_estimate=pl.CostEstimate(
            flops=4 * 10**9, bytes_accessed=4 * 10**6, transcendentals=0
        ),
    )(step_size, *in_hbm(caipi_steps, band_order, coil_maps))


def consistency_kernel(
    own_ref, one_ref, two_ref, three_ref, turned_ref, scalars_ref, high_ref, low_ref,
    kspace_hbm, mask_hbm,
    own_out, one_out, two_out, three_out,
    kspace_ref, mask_ref, real_ref, imag_ref, field_ref, swap_ref, sum_ref, sems,
):
    tiles, all_positions, slices, _, _ = turned_ref.shape
    _, coils, _, rows, columns = kspace_ref.shape
    doubled, positions = 2 * rows, all_positions // 4
    copies = [
        pltpu.make_async_copy(kspace_hbm, kspace_ref, sems.at[0]),
        pltpu.make_async_copy(mask_hbm, mask_ref, sems.at[1]),
    ]
    for copy in copies:
        copy.start()
    size = scalars_ref[all_positions : all_positions + 1, :]
    owners = []
    for x in range(4):
        first = lax.bitwise_xor(lax.axis_index("band"), jnp.int32(x)) * positions
        for p in range(positions):
            shift = jnp.max(scalars_ref[pl.ds(first + p, 1), :]).astype(jnp.int32)
            owners.append((x, p, first + p, shift))

    def coil_of(j, g, s):
        return turned_ref[j, g, s].astype(jnp.float32).reshape(coils, doubled, 128)

    images = (own_ref, one_ref, two_ref, three_ref)
    for k, (x, p, g, shift) in enumerate(owners):

        def store_image(j, value, k=k):
            other = halves_swapped(value)
            top = upper_half(value)
            real_ref[j, k] = jnp.where(top, value, other)
            imag_ref[j, k] = jnp.where(top, other, value)

        image = images[x][p * slices : (p + 1) * slices].astype(jnp.float32)
        turned_tiles(image, shift, store_image)
    for copy in copies:
        copy.wait()

    block = coils * doubled
    halves = [range(0, slices // 2), range(slices // 2, slices)]

    def rows_of(half):
        return slice(half[0] * block, (half[-1] + 1) * block)

    def collapse(half):
        for j in range(tiles):
            for s in half:
                with_real = jnp.zeros((coils, doubled, 128), jnp.float32)
                with_imag = jnp.zeros((coils, doubled, 128), jnp.float32)
                for k, (_, _, g, _) in enumerate(owners):
                    coil = coil_of(j, g, s)
                    with_real += coil * real_ref[j, k, s]
                    with_imag += coil * imag_ref[j, k, s]
                total = with_real + signed_swap(with_imag, -1.0, 1.0)
                field_ref[s * block : (s + 1) * block, 128 * j : 128 * (j + 1)] = total.reshape(
                    block, 128
                )

    def transformed(source, half, top, bottom):
        product = table_product(source, high_ref, low_ref)
        grouped = (len(half), coils, doubled, columns)
        with_cos = product[:, :columns].reshape(grouped)
        with_sin = product[:, columns:].reshape(grouped)
        return with_cos + signed_swap(with_sin, top, bottom)

    def project(half):
        spectrum = transformed(field_ref[rows_of(half)], half, 1.0, -1.0)
        keep = mask_ref[...].astype(jnp.float32)[half[0] : half[-1] + 1]
        keep = keep.reshape(len(half), 1, 1, columns)
        data = stacked_parts(kspace_ref[half[0] : half[-1] + 1])
        residual = (keep * (spectrum - data)).reshape(len(half) * block, columns)
        back = transformed(residual, half, -1.0, 1.0)
        field_ref[rows_of(half)] = back.reshape(len(half) * block, columns)
        swap_ref[rows_of(half)] = halves_swapped(back).reshape(len(half) * block, columns)

    def combine(half):
        for j in range(tiles):
            for s in half:
                place = (slice(s * block, (s + 1) * block), slice(128 * j, 128 * (j + 1)))
                field = field_ref[place].reshape(coils, doubled, 128)
                swapped = swap_ref[place].reshape(coils, doubled, 128)
                for k, (_, _, g, _) in enumerate(owners):
                    coil = coil_of(j, g, s)
                    straight = jnp.sum(coil * field, axis=0)
                    crossed = jnp.sum(coil * swapped, axis=0)
                    straight = straight + halves_swapped(straight)
                    crossed = halves_swapped(crossed) - crossed
                    sum_ref[k, s, :, 128 * j : 128 * (j + 1)] = size * jnp.where(
                        upper_half(straight), straight, crossed
                    )

    for half in halves:
        collapse(half)
    for half in halves:
        project(half)
    for half in halves:
        combine(half)

    outs = (own_out, one_out, two_out, three_out)
    for k, (x, p, _, shift) in enumerate(owners):
        back_shift = lax.rem(columns - shift, columns)
        outs[x][p] = pltpu.roll(sum_ref[k], back_shift, 2).astype(jnp.bfloat16)


def partial_consistency(images, prepared, measured_kspace, sample_mask):
    tiles, all_positions, slices, _, _ = prepared[0].shape
    _, coils, _, rows, columns = measured_kspace.shape
    doubled = 2 * rows
    total = slices * coils * doubled
    hbm = pl.BlockSpec(memory_space=pltpu.HBM)
    vmem = pl.BlockSpec(memory_space=pltpu.VMEM)
    image_shape = (tiles, all_positions, slices, doubled, 128)
    part = jax.ShapeDtypeStruct((all_positions // 4, slices, doubled, columns), jnp.bfloat16)
    return pl.pallas_call(
        consistency_kernel,
        out_shape=(part,) * 4,
        in_specs=[vmem] * 8 + [hbm] * 2,
        out_specs=(vmem,) * 4,
        scratch_shapes=[
            pltpu.VMEM(measured_kspace.shape, jnp.float32),
            pltpu.VMEM(sample_mask.shape, jnp.int32),
            pltpu.VMEM(image_shape, jnp.float32),
            pltpu.VMEM(image_shape, jnp.float32),
            pltpu.VMEM((total, columns), jnp.float32),
            pltpu.VMEM((total, columns), jnp.float32),
            pltpu.VMEM((all_positions, slices, doubled, columns), jnp.float32),
            pltpu.SemaphoreType.DMA((2,)),
        ],
        compiler_params=pltpu.CompilerParams(vmem_limit_bytes=40 * 2**20),
        cost_estimate=pl.CostEstimate(
            flops=4 * 10**9, bytes_accessed=4 * 10**6, transcendentals=0
        ),
    )(*images, *prepared, *in_hbm(measured_kspace, sample_mask))


def network_kernel(
    window_ref, scalars_ref, first_hbm, mid_hbm, last_hbm, image_hbm, noise_hbm,
    out_ref,
    first_raw, mid_raw, last_raw, image_ref, noise_ref,
    first_sum, last_sum, first_ref, wide_ref, last_ref, taps_ref, f1_ref, f2_ref, part_a, part_b, score_ref, sems,
):
    channels = mid_raw.shape[-1]
    out_slices, _, rows, columns = out_ref.shape
    slices1, slices2 = out_slices + 4, out_slices + 2
    pairs = (
        (first_hbm, first_raw), (mid_hbm, mid_raw), (last_hbm, last_raw),
        (image_hbm, image_ref), (noise_hbm, noise_ref),
    )
    copies = [pltpu.make_async_copy(src, dst, sems.at[i]) for i, (src, dst) in enumerate(pairs)]
    for copy in copies:
        copy.start()

    def inside(axis, end):
        edge = lax.axis_size(axis) - 1 if end else 0
        return jnp.where(lax.axis_index(axis) == edge, 0.0, 1.0).astype(jnp.float32)

    low_slice, high_slice = inside("band", False), inside("band", True)
    low_row, high_row = inside("slab", False), inside("slab", True)
    four, two = 4 * channels, 2 * channels

    for g in range(2):
        base = window_ref[g].astype(jnp.float32)
        taps_ref[g, 0] = moved_right(base).astype(jnp.bfloat16)
        taps_ref[g, 1] = window_ref[g]
        taps_ref[g, 2] = moved_left(base).astype(jnp.bfloat16)

    for copy in copies[:3]:
        copy.wait()
    fill_first(first_raw, first_sum, first_ref)

    def first_layer(z):
        source = jnp.concatenate(
            [
                jnp.concatenate([taps_ref[g, t, 16 * z : 16 * z + 48, :] for t in range(3)], axis=0)
                for g in range(2)
            ],
            axis=1,
        )
        half = jnp.dot(first_ref[...], source, preferred_element_type=jnp.float32)
        for r in range(8):
            begin = (r % 4) * channels
            first = columns * (r // 4)
            value = half_silu(half[begin : begin + channels, first : first + columns])
            factors = []
            if z < 2:
                factors.append(low_slice)
            if z >= slices1 - 2:
                factors.append(high_slice)
            if r < 2:
                factors.append(low_row)
            if r >= 6:
                factors.append(high_row)
            for factor in factors:
                value = value * factor
            f1_ref[z, r * channels : (r + 1) * channels, :] = value.astype(jnp.bfloat16)

    def second_product(z, pair, part_ref):
        source = jnp.concatenate(
            [
                f1_ref[z + a : z + a + 3, two * pair : two * pair + four, :].reshape(
                    3 * four, columns
                )
                for a in range(2)
            ],
            axis=1,
        )
        part_ref[...] = jnp.dot(wide_ref[...], source, preferred_element_type=jnp.float32)

    def second_layer(z, pair, part_ref):
        for a in range(2):
            first = columns * a
            for r in range(2):
                row = r * channels
                half = (
                    moved_right(part_ref[row : row + channels, first : first + columns])
                    + part_ref[two + row : two + row + channels, first : first + columns]
                    + moved_left(
                        part_ref[four + row : four + row + channels, first : first + columns]
                    )
                )
                value = half_silu(half)
                factors = []
                if z + a == 0:
                    factors.append(low_slice)
                if z + a == slices2 - 1:
                    factors.append(high_slice)
                if pair == 0 and r == 0:
                    factors.append(low_row)
                if pair == 2 and r == 1:
                    factors.append(high_row)
                for factor in factors:
                    value = value * factor
                place = two * pair + r * channels
                f2_ref[z + a, place : place + channels, :] = value.astype(jnp.bfloat16)

    def third_product(z):
        source = jnp.concatenate([f2_ref[z], f2_ref[z + 1]], axis=1)
        score_ref[z // 2] = jnp.dot(last_ref[...], source, preferred_element_type=jnp.float32)

    fill_others(mid_raw, last_raw, last_sum, wide_ref, last_ref)
    for z in range(4):
        first_layer(z)
    waiting = None
    parts = (part_a, part_b)
    count = 0
    for z in range(0, slices2, 2):
        for pair in range(3):
            second_product(z, pair, parts[count % 2])
            if pair < 2 and z + 4 + pair < slices1:
                first_layer(z + 4 + pair)
            if waiting is not None:
                second_layer(*waiting)
                if waiting[1] == 2:
                    third_product(waiting[0])
            waiting = (z, pair, parts[count % 2])
            count += 1
    second_layer(*waiting)
    third_product(waiting[0])

    for copy in copies[3:]:
        copy.wait()
    size = scalars_ref[scalars_ref.shape[0] - 1 :, :]
    size = jnp.concatenate([size] * (columns // 128), axis=1)
    noise_scale = jnp.sqrt(2.0 * size)
    for z in range(out_slices):
        taps = []
        for t in range(3):
            total = None
            for d in range(3):
                row, first = (3 * d + t) * 8, columns * ((z + d) % 2)
                piece = score_ref[(z + d) // 2, row : row + 8, first : first + columns]
                total = piece if total is None else total + piece
            taps.append(total)
        score = size * (moved_right(taps[0]) + taps[1] + moved_left(taps[2]))
        for part in range(2):
            out_ref[z, part] = (
                image_ref[z, part]
                + score[part * rows : (part + 1) * rows]
                + noise_scale * noise_ref[z, part]
            )


def stepped_without_data(
    windows, scalars, current_image, langevin_noise, weight_in, weight_mid, weight_out
):
    channels = weight_mid.shape[0]
    first = jnp.transpose(weight_in, (2, 3, 4, 1, 0))
    mid = jnp.transpose(weight_mid, (2, 3, 4, 0, 1))
    last = jnp.transpose(weight_out, (2, 3, 4, 0, 1))
    slices0, columns = windows.shape[1] // 16, windows.shape[-1]
    out_slices = slices0 - 6
    local = (out_slices,) + current_image.shape[2:]
    hbm = pl.BlockSpec(memory_space=pltpu.HBM)
    vmem = pl.BlockSpec(memory_space=pltpu.VMEM)
    return pl.pallas_call(
        network_kernel,
        out_shape=jax.ShapeDtypeStruct(local, jnp.float32),
        in_specs=[vmem] * 2 + [hbm] * 5,
        out_specs=vmem,
        scratch_shapes=[
            pltpu.VMEM(first.shape, jnp.bfloat16),
            pltpu.VMEM(mid.shape, jnp.bfloat16),
            pltpu.VMEM(last.shape, jnp.bfloat16),
            pltpu.VMEM(local, jnp.float32),
            pltpu.VMEM(local, jnp.float32),
            pltpu.VMEM((256, 4 * channels), jnp.float32),
            pltpu.VMEM((72, 6 * channels), jnp.float32),
            pltpu.VMEM((4 * channels, 144), jnp.bfloat16),
            pltpu.VMEM((6 * channels, 12 * channels), jnp.bfloat16),
            pltpu.VMEM((72, 6 * channels), jnp.bfloat16),
            pltpu.VMEM((2, 3, slices0 * 16, columns), jnp.bfloat16),
            pltpu.VMEM((out_slices + 4, 8 * channels, columns), jnp.bfloat16),
            pltpu.VMEM((out_slices + 2, 6 * channels, columns), jnp.bfloat16),
            pltpu.VMEM((6 * channels, 2 * columns), jnp.float32),
            pltpu.VMEM((6 * channels, 2 * columns), jnp.float32),
            pltpu.VMEM((out_slices // 2 + 1, 72, 2 * columns), jnp.float32),
            pltpu.SemaphoreType.DMA((5,)),
        ],
        compiler_params=pltpu.CompilerParams(vmem_limit_bytes=40 * 2**20),
        cost_estimate=pl.CostEstimate(
            flops=10**10, bytes_accessed=2 * 10**6, transcendentals=4 * 10**6
        ),
    )(
        windows, scalars,
        *in_hbm(first, mid, last, current_image.reshape(local), langevin_noise.reshape(local)),
    ).reshape(current_image.shape)


def per_device(
    current_image, langevin_noise, step_size, coil_maps, measured_kspace, sample_mask,
    caipi_steps, band_order, weight_in, weight_mid, weight_out,
):
    positions, group_slices, _, row_count, columns = current_image.shape
    local_slices = positions * group_slices
    band, bands = lax.axis_index("band"), lax.axis_size("band")
    own = current_image.astype(jnp.bfloat16).reshape(local_slices, 2 * row_count, columns)
    routes = [[(i, i ^ x) for i in range(bands)] for x in range(1, 4)]
    images = [own] + [lax.ppermute(own, "band", route) for route in routes]
    prepared = preparation(step_size, coil_maps, caipi_steps, band_order)

    odd = band % 2 == 1
    under = jnp.where(odd, images[1], images[3])[local_slices - 3 :]
    over = jnp.where(odd, images[3], images[1])[:3]
    under = jnp.where(band == 0, jnp.zeros_like(under), under)
    over = jnp.where(band == bands - 1, jnp.zeros_like(over), over)
    tall = jnp.concatenate([under, own, over], axis=0)
    tall = tall.reshape(-1, 2, row_count, columns)
    below, above = exchanged_rows(tall, 3)
    sums = partial_consistency(images, prepared, measured_kspace, sample_mask)
    sums, below, above = lax.optimization_barrier((sums, below, above))
    arrived = [lax.ppermute(part, "band", route) for part, route in zip(sums[1:], routes)]
    field = jnp.concatenate([below, tall, above, above[:, :, :2]], axis=2)
    windows = jnp.stack(
        [field[:, :, 4 * g : 4 * g + 8].reshape(-1, columns) for g in range(2)], axis=0
    )
    base = stepped_without_data(
        windows, prepared[1], current_image, langevin_noise, weight_in, weight_mid, weight_out
    )
    total = sums[0].astype(jnp.float32)
    for part in arrived:
        total = total + part.astype(jnp.float32)
    return base - total.reshape(base.shape)


def solution(mesh):
    band5 = P("band", None, None, "slab", None)
    in_specs = (
        band5,
        band5,
        P(),
        P(None, None, "band", None, "slab", None),
        P(None, "band", None, "slab", None),
        P(), P(), P(), P(), P(), P(),
    )
    return jax.shard_map(
        per_device, mesh=mesh, in_specs=in_specs, out_specs=band5, check_vma=False
    )
```

```python
import functools
import math

import jax
import jax.numpy as jnp
from jax import lax
from jax.experimental import pallas as pl
from jax.experimental.pallas import tpu as pltpu
from jax.sharding import PartitionSpec as P


def exchanged_rows(tall, width):
    count = lax.axis_size("slab")
    odd = lax.axis_index("slab") % 2 == 1
    head, tail = tall[:, :, :width, :], tall[:, :, tall.shape[2] - width :, :]
    arrived = []
    for first in range(2):
        route = []
        for i in range(first, count - 1, 2):
            route += [(i, i + 1), (i + 1, i)]
        sent = jnp.where(odd, head, tail) if first == 0 else jnp.where(odd, tail, head)
        arrived.append(lax.ppermute(sent, "slab", route))
    below = jnp.where(odd, arrived[0], arrived[1])
    above = jnp.where(odd, arrived[1], arrived[0])
    return below, above


def in_hbm(*arrays):
    return [pltpu.with_memory_space_constraint(array, pltpu.HBM) for array in arrays]


def series(square, coefficients):
    total = jnp.full_like(square, coefficients[-1])
    for coefficient in coefficients[-2::-1]:
        total = total * square + coefficient
    return total


def fill_factors(factors_ref):
    rows, columns = factors_ref.shape
    near = 16
    count = columns // near
    half = count + near
    row = lax.broadcasted_iota(jnp.int32, (half, columns), 0)
    row = jnp.where(row < count, near * row, row - count).astype(jnp.float32)
    phase = row * lax.broadcasted_iota(jnp.int32, (half, columns), 1).astype(jnp.float32)
    phase = phase - columns * jnp.floor(phase * (1.0 / columns) + 0.5)
    angle = phase * (math.pi / columns)
    square = angle * angle
    sine = angle * series(square, [(-1.0) ** k / math.factorial(2 * k + 1) for k in range(7)])
    cosine = series(square, [(-1.0) ** k / math.factorial(2 * k) for k in range(8)])
    scale = 1.0 / math.sqrt(columns)
    waves = (1.0 - 2.0 * sine * sine, 2.0 * sine * cosine)
    for part, wave in enumerate(waves):
        begin = count * part
        factors_ref[begin : begin + count, :] = scale * wave[:count]
        begin = 2 * count + near * part
        factors_ref[begin : begin + near, :] = wave[count:]


def build_tables(factors_ref, high_ref, low_ref):
    columns = factors_ref.shape[1]
    near = 16
    count = columns // near
    near_cos = factors_ref[2 * count : 2 * count + near, :]
    near_sin = factors_ref[2 * count + near :, :]
    for a in range(count):
        far_cos = factors_ref[a : a + 1, :]
        far_sin = factors_ref[count + a : count + a + 1, :]
        tables = (far_cos * near_cos - far_sin * near_sin, far_sin * near_cos + far_cos * near_sin)
        rows = slice(near * a, near * (a + 1))
        for part, table in enumerate(tables):
            high = table.astype(jnp.bfloat16)
            lanes = slice(columns * part, columns * (part + 1))
            high_ref[rows, lanes] = high
            low_ref[rows, lanes] = (table - high.astype(jnp.float32)).astype(jnp.bfloat16)


def moved_right(value):
    tiles = value.shape[-1] // 128
    moved = [pltpu.roll(value[:, 128 * j : 128 * (j + 1)], 1, 1) for j in range(tiles)]
    edge = lax.broadcasted_iota(jnp.int32, moved[0].shape, 1) == 0
    return jnp.concatenate(
        [jnp.where(edge, moved[j - 1] if j > 0 else 0.0, moved[j]) for j in range(tiles)], axis=1
    )


def moved_left(value):
    tiles = value.shape[-1] // 128
    moved = [pltpu.roll(value[:, 128 * j : 128 * (j + 1)], 127, 1) for j in range(tiles)]
    edge = lax.broadcasted_iota(jnp.int32, moved[0].shape, 1) == 127
    return jnp.concatenate(
        [
            jnp.where(edge, moved[j + 1] if j < tiles - 1 else 0.0, moved[j])
            for j in range(tiles)
        ],
        axis=1,
    )


def half_silu(half):
    return half + half * jnp.tanh(half)


def table_product(source, high_ref, low_ref):
    rows = source.shape[0]
    high = source.astype(jnp.bfloat16)
    low = (source - high.astype(jnp.float32)).astype(jnp.bfloat16)
    both = jnp.dot(
        jnp.concatenate([high, low], axis=0), high_ref[...], preferred_element_type=jnp.float32
    )
    rest = jnp.dot(high, low_ref[...], preferred_element_type=jnp.float32)
    return both[:rows] + both[rows:] + rest


def halves_swapped(value):
    return pltpu.roll(value, 4, value.ndim - 2)


def upper_half(value):
    return lax.broadcasted_iota(jnp.int32, value.shape, value.ndim - 2) < 4


def signed_swap(value, top, bottom):
    sign = jnp.where(upper_half(value), top, bottom)
    return sign * halves_swapped(value)


def stacked_parts(value):
    return jnp.concatenate([value[..., 0, :, :], value[..., 1, :, :]], axis=-2)


def turned_tiles(value, shift, store):
    tiles = value.shape[-1] // 128
    whole, part = shift // 128, lax.rem(shift, 128)
    moved = [
        pltpu.roll(value[..., 128 * j : 128 * (j + 1)], part, value.ndim - 1) for j in range(tiles)
    ]
    lane = lax.broadcasted_iota(jnp.int32, moved[0].shape, value.ndim - 1)
    for j in range(tiles):
        store(lax.rem(j + whole, tiles), jnp.where(lane < part, moved[j - 1], moved[j]))


def fill_weights(first_raw, mid_raw, last_raw, first_sum, last_sum, first_ref, wide_ref, last_ref):
    channels = mid_raw.shape[-1]
    two = 2 * channels
    first_sum[...] = jnp.zeros_like(first_sum)
    last_sum[...] = jnp.zeros_like(last_sum)
    for d in range(3):
        for u in range(3):
            for t in range(3):
                block = first_raw[d, u, t].astype(jnp.float32) * 0.5
                for i in range(2):
                    for r in range(4):
                        row = (t * 3 + d) * 16 + i * 8 + u + r
                        first_sum[row : row + 1, r * channels : (r + 1) * channels] = block[
                            i : i + 1
                        ]
                block = last_raw[d, u, t].astype(jnp.float32)
                for o in range(2):
                    for r in range(4):
                        row = (d * 3 + t) * 8 + o * 4 + r
                        col = (r + u) * channels
                        last_sum[row : row + 1, col : col + channels] = block[o : o + 1]
    first_ref[...] = first_sum[...].T[:, : first_ref.shape[1]].astype(jnp.bfloat16)
    last_ref[...] = last_sum[...].astype(jnp.bfloat16)
    half_weight = jnp.bfloat16(0.5)
    for t in range(3):
        for r in range(2):
            row = (t * 2 + r) * channels
            for d in range(3):
                for pair in range(2):
                    blocks = []
                    for q in (2 * pair, 2 * pair + 1):
                        if 0 <= q - r <= 2:
                            blocks.append(mid_raw[d, q - r, t] * half_weight)
                        else:
                            blocks.append(jnp.zeros((channels, channels), jnp.bfloat16))
                    col = (d * 4 + 2 * pair) * channels
                    wide_ref[row : row + channels, col : col + two] = jnp.concatenate(
                        blocks, axis=1
                    )


def preparation_kernel(
    size_ref, steps_hbm, order_hbm, coil_hbm,
    turned_ref, scalars_ref, high_ref, low_ref,
    steps_ref, order_ref, coil_ref, factors_ref, sems, coil_sems,
):
    all_positions, slices, coils, _, rows, columns = coil_ref.shape
    unit = columns // 8
    block = coils * 2 * rows
    copies = [
        pltpu.make_async_copy(steps_hbm, steps_ref, sems.at[0]),
        pltpu.make_async_copy(order_hbm, order_ref, sems.at[1]),
    ] + [
        pltpu.make_async_copy(coil_hbm.at[g], coil_ref.at[g], coil_sems.at[g])
        for g in range(all_positions)
    ]
    for copy in copies:
        copy.start()
    fill_factors(factors_ref)
    build_tables(factors_ref, high_ref, low_ref)
    scalars_ref[all_positions:, :] = jnp.full(
        (scalars_ref.shape[0] - all_positions, 128), size_ref[0], jnp.float32
    )
    for copy in copies:
        copy.wait()
    for g in range(all_positions):
        shift = steps_ref[order_ref[g]] * unit
        scalars_ref[g : g + 1, :] = jnp.full((1, 128), shift, jnp.int32).astype(jnp.float32)
        for s in range(slices):

            def store_coil(j, value, s=s, g=g):
                turned_ref[j, g, s] = value.reshape(block, 128).astype(jnp.bfloat16)

            turned_tiles(stacked_parts(coil_ref[g, s].astype(jnp.float32)), shift, store_coil)


def preparation(step_size, coil_maps, caipi_steps, band_order):
    all_positions, slices, coils, _, rows, columns = coil_maps.shape
    f32, bf16 = jnp.float32, jnp.bfloat16
    hbm = pl.BlockSpec(memory_space=pltpu.HBM)
    vmem = pl.BlockSpec(memory_space=pltpu.VMEM)
    turned_shape = (columns // 128, all_positions, slices, coils * 2 * rows, 128)
    return pl.pallas_call(
        preparation_kernel,
        out_shape=(
            jax.ShapeDtypeStruct(turned_shape, bf16),
            jax.ShapeDtypeStruct((2 * all_positions, 128), f32),
            jax.ShapeDtypeStruct((columns, 2 * columns), bf16),
            jax.ShapeDtypeStruct((columns, 2 * columns), bf16),
        ),
        in_specs=[pl.BlockSpec(memory_space=pltpu.SMEM)] + [hbm] * 3,
        out_specs=(vmem,) * 4,
        scratch_shapes=[
            pltpu.SMEM(caipi_steps.shape, jnp.int32),
            pltpu.SMEM(band_order.shape, jnp.int32),
            pltpu.VMEM(coil_maps.shape, bf16),
            pltpu.VMEM((2 * (columns // 16 + 16), columns), f32),
            pltpu.SemaphoreType.DMA((2,)),
            pltpu.SemaphoreType.DMA((all_positions,)),
        ],
        compiler_params=pltpu.CompilerParams(vmem_limit_bytes=40 * 2**20),
        cost_estimate=pl.CostEstimate(
            flops=4 * 10**9, bytes_accessed=4 * 10**6, transcendentals=0
        ),
    )(step_size, *in_hbm(caipi_steps, band_order, coil_maps))


def consistency_kernel(
    own_ref, one_ref, two_ref, three_ref, turned_ref, scalars_ref, high_ref, low_ref,
    kspace_hbm, mask_hbm,
    own_out, one_out, two_out, three_out,
    kspace_ref, mask_ref, real_ref, imag_ref, field_ref, swap_ref, sum_ref, sems,
):
    tiles, all_positions, slices, _, _ = turned_ref.shape
    _, coils, _, rows, columns = kspace_ref.shape
    doubled, positions = 2 * rows, all_positions // 4
    copies = [
        pltpu.make_async_copy(kspace_hbm, kspace_ref, sems.at[0]),
        pltpu.make_async_copy(mask_hbm, mask_ref, sems.at[1]),
    ]
    for copy in copies:
        copy.start()
    size = scalars_ref[all_positions : all_positions + 1, :]
    owners = []
    for x in range(4):
        first = lax.bitwise_xor(lax.axis_index("band"), jnp.int32(x)) * positions
        for p in range(positions):
            shift = jnp.max(scalars_ref[pl.ds(first + p, 1), :]).astype(jnp.int32)
            owners.append((x, p, first + p, shift))

    def coil_of(j, g, s):
        return turned_ref[j, g, s].astype(jnp.float32).reshape(coils, doubled, 128)

    images = (own_ref, one_ref, two_ref, three_ref)
    for k, (x, p, g, shift) in enumerate(owners):

        def store_image(j, value, k=k):
            other = halves_swapped(value)
            top = upper_half(value)
            real_ref[j, k] = jnp.where(top, value, other)
            imag_ref[j, k] = jnp.where(top, other, value)

        image = images[x][p * slices : (p + 1) * slices].astype(jnp.float32)
        turned_tiles(image, shift, store_image)
    for copy in copies:
        copy.wait()

    block = coils * doubled
    halves = [range(0, slices // 2), range(slices // 2, slices)]

    def rows_of(half):
        return slice(half[0] * block, (half[-1] + 1) * block)

    def collapse(half):
        for j in range(tiles):
            for s in half:
                with_real = jnp.zeros((coils, doubled, 128), jnp.float32)
                with_imag = jnp.zeros((coils, doubled, 128), jnp.float32)
                for k, (_, _, g, _) in enumerate(owners):
                    coil = coil_of(j, g, s)
                    with_real += coil * real_ref[j, k, s]
                    with_imag += coil * imag_ref[j, k, s]
                total = with_real + signed_swap(with_imag, -1.0, 1.0)
                field_ref[s * block : (s + 1) * block, 128 * j : 128 * (j + 1)] = total.reshape(
                    block, 128
                )

    def transformed(source, half, top, bottom):
        product = table_product(source, high_ref, low_ref)
        grouped = (len(half), coils, doubled, columns)
        with_cos = product[:, :columns].reshape(grouped)
        with_sin = product[:, columns:].reshape(grouped)
        return with_cos + signed_swap(with_sin, top, bottom)

    def project(half):
        spectrum = transformed(field_ref[rows_of(half)], half, 1.0, -1.0)
        keep = mask_ref[...].astype(jnp.float32)[half[0] : half[-1] + 1]
        keep = keep.reshape(len(half), 1, 1, columns)
        data = stacked_parts(kspace_ref[half[0] : half[-1] + 1])
        residual = (keep * (spectrum - data)).reshape(len(half) * block, columns)
        back = transformed(residual, half, -1.0, 1.0)
        field_ref[rows_of(half)] = back.reshape(len(half) * block, columns)
        swap_ref[rows_of(half)] = halves_swapped(back).reshape(len(half) * block, columns)

    def combine(half):
        for j in range(tiles):
            for s in half:
                place = (slice(s * block, (s + 1) * block), slice(128 * j, 128 * (j + 1)))
                field = field_ref[place].reshape(coils, doubled, 128)
                swapped = swap_ref[place].reshape(coils, doubled, 128)
                for k, (_, _, g, _) in enumerate(owners):
                    coil = coil_of(j, g, s)
                    straight = jnp.sum(coil * field, axis=0)
                    crossed = jnp.sum(coil * swapped, axis=0)
                    straight = straight + halves_swapped(straight)
                    crossed = halves_swapped(crossed) - crossed
                    sum_ref[k, s, :, 128 * j : 128 * (j + 1)] = size * jnp.where(
                        upper_half(straight), straight, crossed
                    )

    collapse(halves[0])
    project(halves[0])
    collapse(halves[1])
    combine(halves[0])
    project(halves[1])
    combine(halves[1])

    outs = (own_out, one_out, two_out, three_out)
    for k, (x, p, _, shift) in enumerate(owners):
        back_shift = lax.rem(columns - shift, columns)
        outs[x][p] = pltpu.roll(sum_ref[k], back_shift, 2).astype(jnp.bfloat16)


def partial_consistency(images, prepared, measured_kspace, sample_mask):
    tiles, all_positions, slices, _, _ = prepared[0].shape
    _, coils, _, rows, columns = measured_kspace.shape
    doubled = 2 * rows
    total = slices * coils * doubled
    hbm = pl.BlockSpec(memory_space=pltpu.HBM)
    vmem = pl.BlockSpec(memory_space=pltpu.VMEM)
    image_shape = (tiles, all_positions, slices, doubled, 128)
    part = jax.ShapeDtypeStruct((all_positions // 4, slices, doubled, columns), jnp.bfloat16)
    return pl.pallas_call(
        consistency_kernel,
        out_shape=(part,) * 4,
        in_specs=[vmem] * 8 + [hbm] * 2,
        out_specs=(vmem,) * 4,
        scratch_shapes=[
            pltpu.VMEM(measured_kspace.shape, jnp.float32),
            pltpu.VMEM(sample_mask.shape, jnp.int32),
            pltpu.VMEM(image_shape, jnp.float32),
            pltpu.VMEM(image_shape, jnp.float32),
            pltpu.VMEM((total, columns), jnp.float32),
            pltpu.VMEM((total, columns), jnp.float32),
            pltpu.VMEM((all_positions, slices, doubled, columns), jnp.float32),
            pltpu.SemaphoreType.DMA((2,)),
        ],
        compiler_params=pltpu.CompilerParams(vmem_limit_bytes=40 * 2**20),
        cost_estimate=pl.CostEstimate(
            flops=4 * 10**9, bytes_accessed=4 * 10**6, transcendentals=0
        ),
    )(*images, *prepared, *in_hbm(measured_kspace, sample_mask))


def network_kernel(
    window_ref, scalars_ref, first_hbm, mid_hbm, last_hbm, image_hbm, noise_hbm,
    out_ref,
    first_raw, mid_raw, last_raw, image_ref, noise_ref,
    first_sum, last_sum, first_ref, wide_ref, last_ref, taps_ref, f1_ref, f2_ref, part_a, part_b, score_ref, sems,
):
    channels = mid_raw.shape[-1]
    out_slices, _, rows, columns = out_ref.shape
    slices1, slices2 = out_slices + 4, out_slices + 2
    pairs = (
        (first_hbm, first_raw), (mid_hbm, mid_raw), (last_hbm, last_raw),
        (image_hbm, image_ref), (noise_hbm, noise_ref),
    )
    copies = [pltpu.make_async_copy(src, dst, sems.at[i]) for i, (src, dst) in enumerate(pairs)]
    for copy in copies:
        copy.start()

    def inside(axis, end):
        edge = lax.axis_size(axis) - 1 if end else 0
        return jnp.where(lax.axis_index(axis) == edge, 0.0, 1.0).astype(jnp.float32)

    low_slice, high_slice = inside("band", False), inside("band", True)
    low_row, high_row = inside("slab", False), inside("slab", True)
    four, two = 4 * channels, 2 * channels

    for g in range(2):
        base = window_ref[g].astype(jnp.float32)
        taps_ref[g, 0] = moved_right(base).astype(jnp.bfloat16)
        taps_ref[g, 1] = window_ref[g]
        taps_ref[g, 2] = moved_left(base).astype(jnp.bfloat16)

    for copy in copies[:3]:
        copy.wait()
    fill_weights(
        first_raw, mid_raw, last_raw, first_sum, last_sum, first_ref, wide_ref, last_ref
    )

    def first_layer(z):
        source = jnp.concatenate(
            [
                jnp.concatenate([taps_ref[g, t, 16 * z : 16 * z + 48, :] for t in range(3)], axis=0)
                for g in range(2)
            ],
            axis=1,
        )
        half = jnp.dot(first_ref[...], source, preferred_element_type=jnp.float32)
        for r in range(8):
            begin = (r % 4) * channels
            first = columns * (r // 4)
            value = half_silu(half[begin : begin + channels, first : first + columns])
            factors = []
            if z < 2:
                factors.append(low_slice)
            if z >= slices1 - 2:
                factors.append(high_slice)
            if r < 2:
                factors.append(low_row)
            if r >= 6:
                factors.append(high_row)
            for factor in factors:
                value = value * factor
            f1_ref[z, r * channels : (r + 1) * channels, :] = value.astype(jnp.bfloat16)

    def second_product(z, pair, part_ref):
        source = jnp.concatenate(
            [
                f1_ref[z + a : z + a + 3, two * pair : two * pair + four, :].reshape(
                    3 * four, columns
                )
                for a in range(2)
            ],
            axis=1,
        )
        part_ref[...] = jnp.dot(wide_ref[...], source, preferred_element_type=jnp.float32)

    def second_layer(z, pair, part_ref):
        for a in range(2):
            first = columns * a
            for r in range(2):
                row = r * channels
                half = (
                    moved_right(part_ref[row : row + channels, first : first + columns])
                    + part_ref[two + row : two + row + channels, first : first + columns]
                    + moved_left(
                        part_ref[four + row : four + row + channels, first : first + columns]
                    )
                )
                value = half_silu(half)
                factors = []
                if z + a == 0:
                    factors.append(low_slice)
                if z + a == slices2 - 1:
                    factors.append(high_slice)
                if pair == 0 and r == 0:
                    factors.append(low_row)
                if pair == 2 and r == 1:
                    factors.append(high_row)
                for factor in factors:
                    value = value * factor
                place = two * pair + r * channels
                f2_ref[z + a, place : place + channels, :] = value.astype(jnp.bfloat16)

    def third_product(z):
        source = jnp.concatenate([f2_ref[z], f2_ref[z + 1]], axis=1)
        score_ref[z // 2] = jnp.dot(last_ref[...], source, preferred_element_type=jnp.float32)

    for z in range(4):
        first_layer(z)
    waiting = None
    parts = (part_a, part_b)
    count = 0
    for z in range(0, slices2, 2):
        for pair in range(3):
            second_product(z, pair, parts[count % 2])
            if pair < 2 and z + 4 + pair < slices1:
                first_layer(z + 4 + pair)
            if waiting is not None:
                second_layer(*waiting)
                if waiting[1] == 2:
                    third_product(waiting[0])
            waiting = (z, pair, parts[count % 2])
            count += 1
    second_layer(*waiting)
    third_product(waiting[0])

    for copy in copies[3:]:
        copy.wait()
    size = scalars_ref[scalars_ref.shape[0] - 1 :, :]
    size = jnp.concatenate([size] * (columns // 128), axis=1)
    noise_scale = jnp.sqrt(2.0 * size)
    for z in range(out_slices):
        taps = []
        for t in range(3):
            total = None
            for d in range(3):
                row, first = (3 * d + t) * 8, columns * ((z + d) % 2)
                piece = score_ref[(z + d) // 2, row : row + 8, first : first + columns]
                total = piece if total is None else total + piece
            taps.append(total)
        score = size * (moved_right(taps[0]) + taps[1] + moved_left(taps[2]))
        for part in range(2):
            out_ref[z, part] = (
                image_ref[z, part]
                + score[part * rows : (part + 1) * rows]
                + noise_scale * noise_ref[z, part]
            )


def stepped_without_data(
    windows, scalars, current_image, langevin_noise, weight_in, weight_mid, weight_out
):
    channels = weight_mid.shape[0]
    first = jnp.transpose(weight_in, (2, 3, 4, 1, 0))
    mid = jnp.transpose(weight_mid, (2, 3, 4, 0, 1))
    last = jnp.transpose(weight_out, (2, 3, 4, 0, 1))
    slices0, columns = windows.shape[1] // 16, windows.shape[-1]
    out_slices = slices0 - 6
    local = (out_slices,) + current_image.shape[2:]
    hbm = pl.BlockSpec(memory_space=pltpu.HBM)
    vmem = pl.BlockSpec(memory_space=pltpu.VMEM)
    return pl.pallas_call(
        network_kernel,
        out_shape=jax.ShapeDtypeStruct(local, jnp.float32),
        in_specs=[vmem] * 2 + [hbm] * 5,
        out_specs=vmem,
        scratch_shapes=[
            pltpu.VMEM(first.shape, jnp.bfloat16),
            pltpu.VMEM(mid.shape, jnp.bfloat16),
            pltpu.VMEM(last.shape, jnp.bfloat16),
            pltpu.VMEM(local, jnp.float32),
            pltpu.VMEM(local, jnp.float32),
            pltpu.VMEM((256, 4 * channels), jnp.float32),
            pltpu.VMEM((72, 6 * channels), jnp.float32),
            pltpu.VMEM((4 * channels, 144), jnp.bfloat16),
            pltpu.VMEM((6 * channels, 12 * channels), jnp.bfloat16),
            pltpu.VMEM((72, 6 * channels), jnp.bfloat16),
            pltpu.VMEM((2, 3, slices0 * 16, columns), jnp.bfloat16),
            pltpu.VMEM((out_slices + 4, 8 * channels, columns), jnp.bfloat16),
            pltpu.VMEM((out_slices + 2, 6 * channels, columns), jnp.bfloat16),
            pltpu.VMEM((6 * channels, 2 * columns), jnp.float32),
            pltpu.VMEM((6 * channels, 2 * columns), jnp.float32),
            pltpu.VMEM((out_slices // 2 + 1, 72, 2 * columns), jnp.float32),
            pltpu.SemaphoreType.DMA((5,)),
        ],
        compiler_params=pltpu.CompilerParams(vmem_limit_bytes=40 * 2**20),
        cost_estimate=pl.CostEstimate(
            flops=10**10, bytes_accessed=2 * 10**6, transcendentals=4 * 10**6
        ),
    )(
        windows, scalars,
        *in_hbm(first, mid, last, current_image.reshape(local), langevin_noise.reshape(local)),
    ).reshape(current_image.shape)


def per_device(
    current_image, langevin_noise, step_size, coil_maps, measured_kspace, sample_mask,
    caipi_steps, band_order, weight_in, weight_mid, weight_out,
):
    positions, group_slices, _, row_count, columns = current_image.shape
    local_slices = positions * group_slices
    band, bands = lax.axis_index("band"), lax.axis_size("band")
    own = current_image.astype(jnp.bfloat16).reshape(local_slices, 2 * row_count, columns)
    routes = [[(i, i ^ x) for i in range(bands)] for x in range(1, 4)]
    images = [own] + [lax.ppermute(own, "band", route) for route in routes]
    prepared = preparation(step_size, coil_maps, caipi_steps, band_order)

    odd = band % 2 == 1
    under = jnp.where(odd, images[1], images[3])[local_slices - 3 :]
    over = jnp.where(odd, images[3], images[1])[:3]
    under = jnp.where(band == 0, jnp.zeros_like(under), under)
    over = jnp.where(band == bands - 1, jnp.zeros_like(over), over)
    tall = jnp.concatenate([under, own, over], axis=0)
    tall = tall.reshape(-1, 2, row_count, columns)
    below, above = exchanged_rows(tall, 3)
    sums = partial_consistency(images, prepared, measured_kspace, sample_mask)
    sums, below, above = lax.optimization_barrier((sums, below, above))
    arrived = [lax.ppermute(part, "band", route) for part, route in zip(sums[1:], routes)]
    field = jnp.concatenate([below, tall, above, jnp.zeros_like(above[:, :, :2])], axis=2)
    windows = jnp.stack(
        [field[:, :, 4 * g : 4 * g + 8].reshape(-1, columns) for g in range(2)], axis=0
    )
    base = stepped_without_data(
        windows, prepared[1], current_image, langevin_noise, weight_in, weight_mid, weight_out
    )
    total = sums[0].astype(jnp.float32)
    for part in arrived:
        total = total + part.astype(jnp.float32)
    return base - total.reshape(base.shape)


def solution(mesh):
    band5 = P("band", None, None, "slab", None)
    in_specs = (
        band5,
        band5,
        P(),
        P(None, None, "band", None, "slab", None),
        P(None, "band", None, "slab", None),
        P(), P(), P(), P(), P(), P(),
    )
    return jax.shard_map(
        per_device, mesh=mesh, in_specs=in_specs, out_specs=band5, check_vma=False
    )
```
